128 devices in a mesh: fsdp: 16 (over z_hi, y, core), tp: 8 (over z_lo, x).
Axes of the slice: x: 4, y: 4, z: 4 (z_hi: 2, z_lo: 2; z = z_hi * 2 + z_lo), core: 2. Of those that a mesh axis runs over, the one named last changes fastest.
Arguments:
- layer_input: bfloat16 [24576, 1536], P(('fsdp', 'tp')), may hold values from -6 to 6
- input_gain: float32 [1536], replicated, may hold values from 0.5 to 1.5
- proj_inner: bfloat16 [1536, 2, 3072], P('fsdp', None, 'tp'), may hold values from -0.15625 to 0.15625
- proj_step: bfloat16 [1536, 48], P('fsdp', 'tp'), may hold values from -0.15625 to 0.15625
- proj_state: bfloat16 [1536, 256], P('fsdp'), may hold values from -0.15625 to 0.15625
- proj_output: bfloat16 [3072, 1536], P('tp', 'fsdp'), may hold values from -0.109375 to 0.109375
- conv_inner: float32 [4, 3072], P(None, 'tp'), may hold values from -3 to 3
- conv_inner_bias: float32 [3072], P('tp'), may hold values from -3 to 3
- conv_state: float32 [4, 256], replicated, may hold values from -3 to 3
- conv_state_bias: float32 [256], replicated, may hold values from -3 to 3
- inner_gain: float32 [3072], P('tp'), may hold values from 0.5 to 1.5
- decay_log: float32 [48], P('tp'), may hold values from 0 to 2.77
- step_bias: float32 [48], P('tp'), may hold values from -7 to -2.3
- skip_gain: float32 [48], P('tp'), may hold values from 0.5 to 1.5
- out_cotangent: bfloat16 [24576, 1536], P(('fsdp', 'tp')), may hold values from -6 to 6
Outputs:
- layer_output: bfloat16 [24576, 1536], P(('fsdp', 'tp'))
- input_grad: float32 [24576, 1536], P(('fsdp', 'tp'))
- grad_input_gain: float32 [1536], replicated
- grad_proj_inner: float32 [1536, 2, 3072], P('fsdp', None, 'tp')
- grad_proj_step: float32 [1536, 48], P('fsdp', 'tp')
- grad_proj_state: float32 [1536, 256], P('fsdp')
- grad_proj_output: float32 [3072, 1536], P('tp', 'fsdp')
- grad_conv_inner: float32 [4, 3072], P(None, 'tp')
- grad_conv_inner_bias: float32 [3072], P('tp')
- grad_conv_state: float32 [4, 256], replicated
- grad_conv_state_bias: float32 [256], replicated
- grad_inner_gain: float32 [3072], P('tp')
- grad_decay_log: float32 [48], P('tp')
- grad_step_bias: float32 [48], P('tp')
- grad_skip_gain: float32 [48], P('tp')
The draws below stay inside these ranges and needn't reach their ends.
All inputs are finite; a program needn't handle non-finite values.
Results may differ from the reference program's by a relative error of at most 0.013.
The reference program's roundings to bfloat16 on the way count: a program that leaves them out, or rounds other values in their place, can miss the bound.
Values may be sent and summed in bfloat16 or wider, within the bound.
No kernel may reach another device: no remote copies, remote signals or barrier semaphores. Data moves between devices by JAX's collectives and lax.ppermute only.
A program may use at most 128 MiB of HBM per device.

```python
import math
import jax
import jax.numpy as jnp
from jax import lax

D = 1536
H = 48
P_SIZE = 64
N = 128
CONV = 4
BLOCK = 256
LENGTH = 512
DI = 3072
TOKENS = 24576


def block_levels(stream_key, extent, shards, least, top_value):
    level = 1.0
    for position, blocks in shards:
        heights = jax.random.uniform(jax.random.fold_in(jax.random.fold_in(stream_key, 6), position), (blocks,), jnp.float32, least / len(shards), top_value / len(shards))
        level = level * jnp.repeat(jnp.exp(heights), extent[position] // blocks).reshape((-1,) + (1,) * (len(extent) - 1 - position))
    return level


def centred(rng, shape, scale, reach, split=(), dtype=jnp.bfloat16):
    array = scale * jax.random.normal(rng, shape, jnp.float32)
    if split:
        array = array * block_levels(rng, shape, split, -0.22, 0.18)
    return jnp.clip(array, -reach, reach).astype(dtype)


def setup_inputs(seed: int = 0) -> dict:
    key_list = jax.random.split(jax.random.key(seed), 16)
    layer_input = centred(key_list[0], (TOKENS, D), 1.0, 6.0, ((0, 128),))
    input_gain = jnp.clip(1.0 + 0.1 * jax.random.normal(key_list[1], (D,), jnp.float32), 0.5, 1.5)
    proj_inner = centred(key_list[2], (D, 2, DI), D ** -0.5, 0.15625, ((0, 16), (2, 8)))
    proj_step = centred(key_list[3], (D, H), D ** -0.5, 0.15625, ((0, 16), (1, 8)))
    proj_state = centred(key_list[4], (D, 2 * N), D ** -0.5, 0.15625, ((0, 16),))
    proj_output = centred(key_list[5], (DI, D), DI ** -0.5, 0.109375, ((0, 8), (1, 16)))
    conv_inner = centred(key_list[6], (CONV, DI), CONV ** -0.5, 3.0, ((1, 8),), jnp.float32)
    conv_inner_bias = centred(key_list[7], (DI,), 0.5, 3.0, ((0, 8),), jnp.float32)
    conv_state = centred(key_list[8], (CONV, 2 * N), CONV ** -0.5, 3.0, (), jnp.float32)
    conv_state_bias = centred(key_list[9], (2 * N,), 0.5, 3.0, (), jnp.float32)
    inner_gain = jnp.clip(1.0 + 0.1 * jax.random.normal(key_list[10], (DI,), jnp.float32), 0.5, 1.5)
    decay_log = jnp.clip(2.77 * jax.random.uniform(key_list[11], (H,), jnp.float32) ** block_levels(key_list[11], (H,), ((0, 8),), -0.2, 0.2), 0.0, 2.77)
    step_bias = jnp.clip(-7.0 + 4.7 * jax.random.uniform(key_list[12], (H,), jnp.float32) ** block_levels(key_list[12], (H,), ((0, 8),), -0.2, 0.2), -7.0, -2.3)
    skip_gain = jnp.clip(0.5 + 1.0 * jax.random.uniform(key_list[13], (H,), jnp.float32) ** block_levels(key_list[13], (H,), ((0, 8),), -0.2, 0.2), 0.5, 1.5)
    out_cotangent = centred(key_list[14], (TOKENS, D), 1.0, 6.0, ((0, 128),))
    return dict(layer_input=layer_input, input_gain=input_gain, proj_inner=proj_inner, proj_step=proj_step, proj_state=proj_state, proj_output=proj_output, conv_inner=conv_inner, conv_inner_bias=conv_inner_bias, conv_state=conv_state, conv_state_bias=conv_state_bias, inner_gain=inner_gain, decay_log=decay_log, step_bias=step_bias, skip_gain=skip_gain, out_cotangent=out_cotangent)


@jax.custom_vjp
def low(v):
    return lax.optimization_barrier(v.astype(jnp.bfloat16)).astype(jnp.float32)

@jax.custom_vjp
def low_back(v):
    return v

def low_keep(v):
    return (low(v), None)

def low_pass(kept, grad):
    return (grad,)

def back_keep(v):
    return (v, None)

def back_low(kept, grad):
    return (low(grad),)
low.defvjp(low_keep, low_pass)
low_back.defvjp(back_keep, back_low)
epsilon = 1e-05
HIGHEST = lax.Precision.HIGHEST

def causal_conv(signal, kernel, offset):
    tap_count = kernel.shape[0]
    channels = signal.shape[1]
    seq_count = signal.shape[0] // LENGTH
    framed = signal.reshape(seq_count, LENGTH, channels)
    padded = jnp.pad(framed, ((0, 0), (tap_count - 1, 0), (0, 0)))
    summed = jnp.broadcast_to(offset, framed.shape)
    for tap_index in range(tap_count):
        summed = summed + kernel[tap_index] * padded[:, tap_index:tap_index + LENGTH, :]
    return summed.reshape(seq_count * LENGTH, channels)

def ssd_scan(conv_values, decay_rate, step_size, state_in, state_out, skip_gain):
    head_count = step_size.shape[1]
    total_rows = step_size.shape[0]
    head_width = conv_values.shape[1] // head_count
    seq_count = total_rows // LENGTH
    block_count = LENGTH // BLOCK
    values_grid = conv_values.reshape(seq_count, block_count, BLOCK, head_count, head_width)
    in_grid = state_in.reshape(seq_count, block_count, BLOCK, N)
    out_grid = state_out.reshape(seq_count, block_count, BLOCK, N)
    step_grid = step_size.reshape(seq_count, block_count, BLOCK, head_count)
    cumulative = jnp.cumsum(-decay_rate * step_grid, axis=2)
    spread = cumulative[:, :, :, None, :] - cumulative[:, :, None, :, :]
    positions = jnp.arange(BLOCK)
    lower_mask = (positions[:, None] >= positions[None, :])[None, None, :, :, None]
    decay_weight = jnp.exp(jnp.where(lower_mask, spread, -1e+30))
    scores = jnp.einsum('scqn,scrn->scqr', out_grid, in_grid, precision=HIGHEST)
    weighted_x = values_grid * step_grid[..., None]
    inside = jnp.einsum('scqrh,scrhp->scqhp', scores[..., None] * decay_weight, weighted_x, precision=HIGHEST)
    fading = jnp.exp(cumulative[:, :, -1:, :] - cumulative)
    states = jnp.einsum('scqn,scqhp->schnp', in_grid, weighted_x * fading[..., None], precision=HIGHEST)
    carried = jnp.zeros((seq_count, head_count, N, head_width), jnp.float32)
    entering = []
    for block_index in range(block_count):
        entering.append(carried)
        carried = carried * jnp.exp(cumulative[:, block_index, -1, :])[:, :, None, None] + states[:, block_index]
    entering = jnp.stack(entering, axis=1)
    outside = jnp.einsum('scqn,schnp->scqhp', out_grid, entering, precision=HIGHEST) * jnp.exp(cumulative)[..., None]
    result = inside + outside + skip_gain[:, None] * values_grid
    return result.reshape(total_rows, head_count * head_width)

def mixer_layer(inner_pre, step_pre, state_pre, conv_inner, conv_inner_bias, conv_state, conv_state_bias, decay_log, step_bias, skip_gain):
    channels = inner_pre.shape[1] // 2
    gating = inner_pre[:, :channels]
    conv_values = low(jax.nn.silu(causal_conv(inner_pre[:, channels:], conv_inner, conv_inner_bias)))
    conv_states = low(jax.nn.silu(causal_conv(state_pre, conv_state, conv_state_bias)))
    step_size = jax.nn.softplus(step_pre + step_bias)
    ssd_out = low_back(ssd_scan(conv_values, jnp.exp(decay_log), step_size, conv_states[:, :N], conv_states[:, N:], skip_gain))
    return ssd_out * jax.nn.silu(gating)

def layer_block(row_values, input_gain, proj_inner, proj_step, proj_state, proj_output, conv_inner, conv_inner_bias, conv_state, conv_state_bias, inner_gain, decay_log, step_bias, skip_gain):
    inv_input = lax.rsqrt(lax.optimization_barrier(jnp.mean(row_values * row_values, axis=1, keepdims=True)) + epsilon)
    normed = low(row_values * inv_input * input_gain)
    inner_pre = low_back(jnp.dot(normed, proj_inner.reshape(D, 2 * H * P_SIZE), precision=HIGHEST))
    step_pre = low_back(jnp.dot(normed, proj_step, precision=HIGHEST))
    state_pre = low_back(jnp.dot(normed, proj_state, precision=HIGHEST))
    gated_rows = mixer_layer(inner_pre, step_pre, state_pre, conv_inner, conv_inner_bias, conv_state, conv_state_bias, decay_log, step_bias, skip_gain)
    inv_gated = lax.rsqrt(lax.optimization_barrier(jnp.mean(gated_rows * gated_rows, axis=1, keepdims=True)) + epsilon)
    mixed_rows = low(gated_rows * inv_gated * inner_gain)
    return row_values + jnp.dot(mixed_rows, proj_output, precision=HIGHEST)

def reference(layer_input, input_gain, proj_inner, proj_step, proj_state, proj_output, conv_inner, conv_inner_bias, conv_state, conv_state_bias, inner_gain, decay_log, step_bias, skip_gain, out_cotangent):
    weights = tuple((item.astype(jnp.float32) for item in (input_gain, proj_inner, proj_step, proj_state, proj_output, conv_inner, conv_inner_bias, conv_state, conv_state_bias, inner_gain, decay_log, step_bias, skip_gain)))
    row_values = layer_input.astype(jnp.float32)
    seq_total = row_values.shape[0] // LENGTH
    batch_seqs = math.gcd(seq_total, 4)

    def forward(rows_all, params):

        def one_batch(rows_block):
            return layer_block(rows_block, params[0], params[1], params[2], params[3], params[4], params[5], params[6], params[7], params[8], params[9], params[10], params[11], params[12])
        grouped = rows_all.reshape(seq_total // batch_seqs, batch_seqs * LENGTH, D)
        return lax.map(jax.checkpoint(one_batch), grouped).reshape(-1, D)
    result, pullback = jax.vjp(forward, row_values, weights)
    grad_rows, grad_params = pullback(out_cotangent.astype(jnp.float32))
    return (result.astype(jnp.bfloat16), grad_rows, grad_params[0], grad_params[1], grad_params[2], grad_params[3], grad_params[4], grad_params[5], grad_params[6], grad_params[7], grad_params[8], grad_params[9], grad_params[10], grad_params[11], grad_params[12])
```

```python
import functools
import itertools

import jax
import jax.numpy as jnp
import numpy as np
from jax import lax
from jax.experimental import pallas as pl
from jax.experimental.pallas import tpu as pltpu
from jax.sharding import Mesh
from jax.sharding import PartitionSpec as P

D = 1536
DI = 3072
N = 128
Q = 128
STEP = 256
ROWS = 768
CH = 768
HALF = 384
PAIRS = 6
LEFT = 1024
LATE = 640
FULL = LEFT + HALF
EPS = 1e-05
NEG = -1e30

AX = ("zh", "y", "c", "zl", "x")
SIZES = (2, 4, 2, 2, 4)
FSDP = ("zh", "y", "c")
TP = ("zl", "x")

bf16 = jnp.bfloat16
f32 = jnp.float32
VMEM_LIMIT = 56 * 1024 * 1024


def moved(d, axis, k):
    d = dict(d)
    if axis == "z":
        z = (2 * d["zh"] + d["zl"] + k) % 4
        d["zh"], d["zl"] = divmod(z, 2)
    elif axis == "first":
        return moved(d, "y" if d["c"] == 0 else "z", k)
    elif axis == "second":
        return moved(d, "z" if d["c"] == 0 else "y", k)
    else:
        d[axis] = (d[axis] + k) % SIZES[AX.index(axis)]
    return d


def send(a, axis, k):
    pairs = []
    for place in itertools.product(*map(range, SIZES)):
        to = moved(dict(zip(AX, place)), axis, k)
        pairs.append(
            (
                int(np.ravel_multi_index(place, SIZES)),
                int(np.ravel_multi_index([to[n] for n in AX], SIZES)),
            )
        )
    return lax.ppermute(a, AX, pairs)


def ring_gather(a, axis):
    h = a.shape[0] // 2
    m = send(a, axis, 1)
    p = send(a, axis, -1)
    o1 = send(m[:h], axis, 1)
    o2 = send(p[h:], axis, -1)
    return m, p, o1, o2


def add(a, b):
    return (a.astype(f32) + b.astype(f32)).astype(bf16)


def ring_scatter(a, axis):
    h = a.shape[1] // 2
    o1 = send(a[2, :h], axis, 1)
    o2 = send(a[2, h:], axis, -1)
    up = jnp.concatenate([add(a[1, :h], o1), a[1, h:]], axis=0)
    down = jnp.concatenate([a[3, :h], add(a[3, h:], o2)], axis=0)
    return a[0], send(up, axis, 1), send(down, axis, -1)


def add3(terms):
    a, b, c = terms
    return a.astype(f32) + b.astype(f32) + c.astype(f32)


def scatter_tiles(tiles):
    other = send(tiles[1], "c", 1)
    mine = add(tiles[0], other)
    once = add3(ring_scatter(mine, "second")).astype(bf16)
    return add3(ring_scatter(once, "first"))


def everyone(a, axis):
    return a + send(a, axis, 1) + send(a, axis, 2) + send(a, axis, 3)


def dot(a, b):
    return lax.dot_general(a, b, (((1,), (0,)), ((), ())), preferred_element_type=f32)


def dot_nt(a, b):
    return lax.dot_general(a, b, (((1,), (1,)), ((), ())), preferred_element_type=f32)


def dot_tn(a, b):
    return lax.dot_general(a, b, (((0,), (0,)), ((), ())), preferred_element_type=f32)


def halves(a):
    hi = a.astype(bf16)
    return hi, (a - hi.astype(f32)).astype(bf16)


def thirds(a):
    hi = a.astype(bf16)
    rest = a - hi.astype(f32)
    mid = rest.astype(bf16)
    return hi, mid, (rest - mid.astype(f32)).astype(bf16)


def tri_dot(tri, a):
    return dot(jnp.concatenate([tri] * 3, axis=1), jnp.concatenate(thirds(a), axis=0))


def lanes_of(a, i):
    return jnp.broadcast_to(a[:, i : i + 1], (Q, 128))


def iota(shape, dim):
    return lax.broadcasted_iota(jnp.int32, shape, dim)


def softplus(v):
    return jnp.maximum(v, 0.0) + jnp.log1p(jnp.exp(-jnp.abs(v)))


def here():
    return {n: lax.axis_index(n) for n in AX}


def row_copies(pieces, dst, sems):
    me = here()
    copies = []
    own, m, p, o1, o2 = pieces
    for ref, rel in ((own, 0), (m, 3), (p, 1)):
        x = lax.rem(me["x"] + rel, 4)
        for g in range(3):
            at = lax.rem(3 * x + g + 4 + 4 * me["zl"], 12)
            copies.append((ref.at[pl.ds(64 * g, 64)], dst.at[pl.ds(pl.multiple_of(64 * at, 64), 64)]))
    x = lax.rem(me["x"] + 2, 4)
    for ref, first in ((o1, 0), (o2, 3)):
        for g in range(3):
            at = lax.rem(6 * x + first + g + 8 + 8 * me["zl"], 24)
            copies.append((ref.at[pl.ds(32 * g, 32)], dst.at[pl.ds(pl.multiple_of(32 * at, 32), 32)]))
    return [pltpu.make_async_copy(s, d, sems.at[i]) for i, (s, d) in enumerate(copies)]


N_ROW_COPIES = 15


def weight_copies(pieces, column, width, dst, sems):
    me = here()
    copies = []
    for other in range(2):
        q, m, p, o1, o2 = pieces[5 * other : 5 * other + 5]
        core = lax.rem(me["c"] + other, 2)
        z0 = 2 * me["zh"] + me["zl"]
        for ref, rb, firsts in (
            (q, 0, ((0, 0), (3, 96), (1, 192), (2, 288))),
            (m, 3, ((0, 0), (3, 96), (1, 192), (2, 288))),
            (p, 1, ((0, 0), (3, 96), (1, 192), (2, 288))),
            (o1, 2, ((0, 0), (3, 96))),
            (o2, 2, ((1, 0), (2, 96))),
        ):
            for ra, row in firsts:
                y = lax.rem(me["y"] + jnp.where(core == 0, ra, rb), 4)
                z = lax.rem(z0 + jnp.where(core == 0, rb, ra), 4)
                f = (z // 2 * 4 + y) * 2 + core
                copies.append(
                    (
                        ref.at[pl.ds(row, 96), pl.ds(column, width)],
                        dst.at[
                            pl.ds(pl.multiple_of(96 * f, 96), 96),
                            pl.ds(pl.multiple_of(width * lax.rem(z, 2), 128), width),
                        ],
                    )
                )
    return [pltpu.make_async_copy(s, d, sems.at[i]) for i, (s, d) in enumerate(copies)]


def proj_kernel(*refs):
    rows, weights = refs[:5], refs[5:15]
    gain, feat_out, w_out, pre, raw, feat, w, rsem, wsem, osem = refs[15:]
    i = pl.program_id(0)
    outs = [
        pltpu.make_async_copy(feat, feat_out, osem.at[0]),
        pltpu.make_async_copy(w, w_out, osem.at[1]),
    ]

    @pl.when(i == 0)
    def _():
        row_c = row_copies(rows, raw, rsem)
        weight_c = weight_copies(weights, 0, LEFT, w, wsem)
        for c in row_c + weight_c:
            c.start()
        for c in row_c:
            c.wait()

        def norm(k, carry):
            at = pl.ds(pl.multiple_of(64 * k, 64), 64)
            v = raw[at, :].astype(f32)
            r = lax.rsqrt(jnp.mean(v * v, axis=1, keepdims=True) + EPS)
            feat[at, :] = (v * r * gain[...]).astype(bf16)
            return carry

        lax.fori_loop(0, ROWS // 64, norm, 0)
        for c in weight_c:
            c.wait()
        for c in outs:
            c.start()

    pre[...] = dot(feat[...], w[:, pl.ds(pl.multiple_of(256 * i, 256), 256)])

    @pl.when(i == pl.num_programs(0) - 1)
    def _():
        for c in outs:
            c.wait()


def pair_places(i):
    g, p = divmod(i, 3)
    return slice(128 * i, 128 * i + 128), g * LEFT + HALF + 128 * p


def step_sizes(pre, heads):
    raw = pre[:, 896:1024] + pre[:, LEFT + 896 : LEFT + 1024] + heads[1:2, :]
    return raw, softplus(raw)


def framed_inputs(s, zl, pre, prev, msg, vx, vs):
    for g in range(2):
        base = g * LEFT + HALF
        vx[8:264, g * HALF : (g + 1) * HALF] = pre[:, base : base + HALF]
        vs[8:264, g * N : (g + 1) * N] = pre[:, base + HALF : base + HALF + N]
        if s == 0:
            vx[0:8, g * HALF : (g + 1) * HALF] = jnp.zeros((8, HALF), f32)
            vs[0:8, g * N : (g + 1) * N] = jnp.zeros((8, N), f32)
            continue
        hx, hs = prev[:, base : base + HALF], prev[:, base + HALF : base + HALF + N]
        if s == 1:
            hx, hs = jnp.where(zl == 1, hx, 0.0), jnp.where(zl == 1, hs, 0.0)
        else:
            mx = msg[128:144, g * HALF : (g + 1) * HALF].astype(f32)[:8]
            ms = msg[144:160, g * N : (g + 1) * N].astype(f32)[:8]
            hx, hs = jnp.where(zl == 0, hx, mx), jnp.where(zl == 0, hs, ms)
        vx[0:8, g * HALF : (g + 1) * HALF] = hx
        vs[0:8, g * N : (g + 1) * N] = hs


def fwd_kernel(s, *refs):
    refs = list(refs)
    pre = refs.pop(0)
    prev = refs.pop(0) if s else None
    h_in = refs.pop(0) if s else None
    msg = refs.pop(0) if s == 2 else None
    prm, prs, heads = refs[:3]
    refs = refs[3:]
    if s:
        refs.pop(0)
    act, hs = refs[:2]
    refs = refs[2:]
    out_msg = refs.pop(0) if s == 0 else None
    vx, vs = refs
    zl = lax.axis_index("zl")
    framed_inputs(s, zl, pre, prev, msg, vx, vs)
    if s == 0:
        hs[0] = jnp.zeros((N, CH), f32)
    elif s == 1:
        hs[0] = jnp.where(zl == 1, h_in[...].reshape(N, CH), 0.0)
    else:
        hs[0] = jnp.where(zl == 0, h_in[...].reshape(N, CH), msg[0:128, :].astype(f32))
    _, dt_all = step_sizes(pre, heads)
    a_all = -heads[0:1, :] * dt_all
    sub, lane = iota((Q, 128), 0), iota((Q, 128), 1)
    low_mask = sub >= lane
    tri = jnp.where(low_mask, 1.0, 0.0).astype(bf16)
    left = lane < 64
    for j in range(2):
        r0 = Q * j
        bc = []
        for g in range(2):
            col = slice(g * N, (g + 1) * N)
            cs = prs[4:5, col] + sum(
                prs[k : k + 1, col] * vs[5 + k + r0 : 5 + k + r0 + Q, col] for k in range(4)
            )
            act[r0 : r0 + Q, 2 * CH + g * N : 2 * CH + (g + 1) * N] = cs
            bc.append((cs * jax.nn.sigmoid(cs)).astype(bf16))
        b, c = bc
        bt = b.astype(f32).T.astype(bf16)
        scores = dot_nt(c, b)
        dt = dt_all[r0 : r0 + Q]
        cum = tri_dot(tri, a_all[r0 : r0 + Q])
        cum_t = cum.T
        for i in range(PAIRS):
            col, _ = pair_places(i)
            cx = prm[4:5, col] + sum(
                prm[k : k + 1, col] * vx[5 + k + r0 : 5 + k + r0 + Q, col] for k in range(4)
            )
            act[r0 : r0 + Q, CH + 128 * i : CH + 128 * i + 128] = cx
            x = (cx * jax.nn.sigmoid(cx)).astype(bf16).astype(f32)
            c0, c1 = lanes_of(cum, 2 * i), lanes_of(cum, 2 * i + 1)
            m0 = scores * jnp.exp(jnp.where(low_mask, c0 - cum_t[2 * i : 2 * i + 1, :], NEG))
            m1 = scores * jnp.exp(jnp.where(low_mask, c1 - cum_t[2 * i + 1 : 2 * i + 2, :], NEG))
            cp = jnp.where(left, c0, c1)
            xdt = x * jnp.where(left, lanes_of(dt, 2 * i), lanes_of(dt, 2 * i + 1))
            xdtb = xdt.astype(bf16)
            zero = jnp.zeros_like(xdtb)
            last = cp[Q - 1 : Q, :]
            inside = dot(
                jnp.concatenate([m0.astype(bf16), m1.astype(bf16)], axis=1),
                jnp.concatenate([jnp.where(left, xdtb, zero), jnp.where(left, zero, xdtb)], axis=0),
            )
            h = hs[j, :, col]
            y = inside + jnp.exp(cp) * dot(c, h.astype(bf16)) + prm[6:7, col] * x
            act[r0 : r0 + Q, col] = y
            hs[j + 1, :, col] = h * jnp.exp(last) + dot(bt, (xdt * jnp.exp(last - cp)).astype(bf16))
    if s == 0:
        out_msg[0:128, :] = hs[2].astype(bf16)
        out_msg[128:144, :] = jnp.concatenate([vx[256:264, :]] * 2, axis=0).astype(bf16)
        out_msg[144:160, :] = jnp.concatenate(
            [jnp.concatenate([vs[256:264, :]] * 2, axis=0), jnp.zeros((16, CH - 2 * N), f32)], axis=1
        ).astype(bf16)


def cot_kernel(*refs):
    rows, weights = refs[:5], refs[5:15]
    z0, z1, ssd, prm, cot_out, w_out, gm, gb, sums, cot, w, rsem, wsem, osem = refs[15:]
    i = pl.program_id(0)
    outs = [
        pltpu.make_async_copy(cot, cot_out, osem.at[0]),
        pltpu.make_async_copy(w, w_out, osem.at[1]),
    ]

    @pl.when(i == 0)
    def _():
        cs = row_copies(rows, cot, rsem) + weight_copies(weights, LEFT, HALF, w, wsem)
        for c in cs:
            c.start()
        for c in cs:
            c.wait()
        for c in outs:
            c.start()

    at = pl.ds(pl.multiple_of(STEP * i, STEP), STEP)
    grad = dot(cot[at, :], w[...])
    gm[...] = grad
    squares = jnp.zeros((STEP, 1), f32)
    dots = jnp.zeros((STEP, 1), f32)
    for g, z in ((0, z0), (1, z1)):
        col = slice(g * HALF, (g + 1) * HALF)
        gate = z[:, 0:HALF]
        gated = ssd[:, col] * (gate * jax.nn.sigmoid(gate))
        scaled = gated * prm[5:6, col]
        gb[:, col] = scaled.astype(bf16)
        squares = squares + jnp.sum(gated * gated, axis=1, keepdims=True)
        dots = dots + jnp.sum(grad[:, col] * scaled, axis=1, keepdims=True)
    lane = iota((STEP, 128), 1)
    both = jnp.where(lane == 0, squares, jnp.where(lane == 1, dots, 0.0))
    sums[...] = both.T[0:8, :]

    @pl.when(i == pl.num_programs(0) - 1)
    def _():
        for c in outs:
            c.wait()


def store_rows(i, value, out):
    me = here()
    for g in range(4):
        natural = lax.rem(4 * i + g + 8 - 4 * me["zl"] + 12, 12)
        rel = lax.rem(natural // 3 - me["x"] + 4, 4)
        out[3 * rel + lax.rem(natural, 3)] = value[64 * g : 64 * g + 64, :]


def out_kernel(gb, w, out):
    store_rows(pl.program_id(0), dot_nt(gb[...], w[...]).astype(bf16), out)


def gate_kernel(s0, s1, s2, s3, gm, ssd, z0, z1, prm, dssd, lowz, mixed, ggain):
    i = pl.program_id(0)
    total = (s0[...] + s1[...] + s2[...] + s3[...]).T
    inv = lax.rsqrt(total[:, 0:1] / DI + EPS)
    pull = inv * inv * inv * (total[:, 1:2] / DI)

    @pl.when(i == 0)
    def _():
        ggain[...] = jnp.zeros_like(ggain)

    for g, z in ((0, z0), (1, z1)):
        col = slice(g * HALF, (g + 1) * HALF)
        gate = z[:, 0:HALF]
        sig = jax.nn.sigmoid(gate)
        silu = gate * sig
        y = ssd[:, col]
        gated = y * silu
        grad = gm[:, col]
        gain = prm[5:6, col]
        normal = gated * inv
        mixed[:, col] = (normal * gain).astype(bf16)
        dg = grad * gain * inv - gated * pull
        dssd[:, col] = (dg * silu).astype(bf16)
        lowz[:, col] = (dg * y * (sig * (1.0 + gate * (1.0 - sig)))).astype(bf16)
        part = jnp.sum(grad * normal, axis=0, keepdims=True)
        ggain[:, col] += jnp.where(iota((8, HALF), 0) == 0, part, 0.0)


def tile_index(f, g):
    me = here()
    core = f % 2
    y, zh = (f // 2) % 4, f // 8
    dy = lax.rem(y - me["y"] + 4, 4)
    dz = lax.rem(2 * zh + g - (2 * me["zh"] + me["zl"]) + 4, 4)
    other = lax.rem(me["c"] + core, 2)
    return 16 * other + (4 * dz + dy if core == 0 else 4 * dy + dz)


def grad_kernel(jobs, *refs):
    n_in = 1 + max(max(j[0], j[1]) for j in jobs)
    ins, out, buf, sem = refs[:n_in], refs[n_in], refs[n_in + 1], refs[n_in + 2]
    pending = {}
    for k, (a, b, col, width, g, to) in enumerate(jobs):
        slot = k % 2
        for c in pending.pop(slot, ()):
            c.wait()
        for m in range(4):
            rows = slice(384 * m, 384 * m + 384)
            part = dot_tn(ins[a][:, rows], ins[b][:, col : col + width])
            buf[slot, rows, 0:width] = part.astype(bf16)
        copies = []
        for f in range(16):
            copies.append(
                pltpu.make_async_copy(
                    buf.at[slot, pl.ds(96 * f, 96), pl.ds(0, width)],
                    out.at[tile_index(f, g), :, pl.ds(to, width)],
                    sem.at[slot, f],
                )
            )
        for c in copies:
            c.start()
        pending[slot] = copies
    for cs in pending.values():
        for c in cs:
            c.wait()


def bwd_kernel(s, *refs):
    refs = list(refs)
    pre = refs.pop(0)
    prev = refs.pop(0) if s else None
    msg = refs.pop(0) if s == 2 else None
    act, hs, dssd, prm, prs, heads = refs[:6]
    refs = refs[6:]
    if s < 2:
        dh_in, tail, acc_in, accs_in = refs[:4]
        refs = refs[4:]
        back = refs.pop(0) if s == 0 else None
        refs.pop(0)
    low, dh, head_rows, acc, accs = refs[:5]
    refs = refs[5:]
    out_msg = refs.pop(0) if s == 2 else None
    vx, vs, dp, ds = refs
    zl = lax.axis_index("zl")
    framed_inputs(s, zl, pre, prev, msg, vx, vs)
    if s == 2:
        dh[...] = jnp.zeros_like(dh)
        dp[256:264, :] = jnp.zeros((8, CH), f32)
        ds[256:264, :] = jnp.zeros((8, 2 * N), f32)
        acc[...] = jnp.zeros_like(acc)
        accs[...] = jnp.zeros_like(accs)
    else:
        hd, hp, hq = dh_in[...], tail[0:8, :], tail[8:16, 0 : 2 * N]
        if s == 1:
            hd, hp, hq = (jnp.where(zl == 0, v, 0.0) for v in (hd, hp, hq))
        else:
            hd = jnp.where(zl == 1, hd, back[0:128, :].astype(f32))
            hp = jnp.where(zl == 1, hp, back[128:144, :].astype(f32)[:8])
            hq = jnp.where(zl == 1, hq, back[144:160, 0 : 2 * N].astype(f32)[:8])
        dh[...], dp[256:264, :], ds[256:264, :] = hd, hp, hq
        acc[...] = acc_in[...]
        accs[...] = accs_in[...]
    raw_all, dt_all = step_sizes(pre, heads)
    rate = heads[0:1, :]
    a_all = -rate * dt_all
    sub, lane = iota((Q, 128), 0), iota((Q, 128), 1)
    tri = jnp.where(sub >= lane, 1.0, 0.0).astype(bf16)
    up_mask = lane >= sub
    tri_up = jnp.where(up_mask, 1.0, 0.0).astype(bf16)
    below = jnp.where(lane < sub, 1.0, 0.0).astype(bf16)
    left = lane < 64
    for j in (1, 0):
        r0 = Q * j
        rows = slice(r0, r0 + Q)
        pre_s = [act[rows, 2 * CH + g * N : 2 * CH + (g + 1) * N] for g in range(2)]
        sig_s = [jax.nn.sigmoid(v) for v in pre_s]
        bf, cf = [(v * w).astype(bf16).astype(f32) for v, w in zip(pre_s, sig_s)]
        b, c = bf.astype(bf16), cf.astype(bf16)
        ct = cf.T.astype(bf16)
        scores_t = dot_nt(c, b).T
        dt, a = dt_all[rows], a_all[rows]
        cum = tri_dot(tri, a)
        cum_t = cum.T
        d_scores_t = jnp.zeros((Q, Q), f32)
        d_b = jnp.zeros((Q, N), f32)
        d_c = jnp.zeros((Q, N), f32)
        per_head = jnp.zeros((3 * Q, 128), f32)
        for i in range(PAIRS):
            col, _ = pair_places(i)
            cx = act[rows, CH + 128 * i : CH + 128 * i + 128]
            sig = jax.nn.sigmoid(cx)
            x = (cx * sig).astype(bf16).astype(f32)
            dyb = dssd[rows, col]
            dy = dyb.astype(f32)
            skip = prm[6:7, col]
            c0, c1 = lanes_of(cum, 2 * i), lanes_of(cum, 2 * i + 1)
            l0 = jnp.exp(jnp.where(up_mask, cum_t[2 * i : 2 * i + 1, :] - c0, NEG))
            l1 = jnp.exp(jnp.where(up_mask, cum_t[2 * i + 1 : 2 * i + 2, :] - c1, NEG))
            cp = jnp.where(left, c0, c1)
            dtp = jnp.where(left, lanes_of(dt, 2 * i), lanes_of(dt, 2 * i + 1))
            last = cp[Q - 1 : Q, :]
            fade = jnp.exp(last - cp)
            xdt = x * dtp
            xdtb = xdt.astype(bf16)
            zero = jnp.zeros_like(xdtb)
            dy_split = jnp.concatenate([jnp.where(left, dyb, zero), jnp.where(left, zero, dyb)], axis=0)
            x_split = jnp.concatenate([jnp.where(left, xdtb, zero), jnp.where(left, zero, xdtb)], axis=0)
            dhp = dh[:, col]
            dhb = dhp.astype(bf16)
            m_t = jnp.concatenate([(scores_t * l0).astype(bf16), (scores_t * l1).astype(bf16)], axis=1)
            inside = dot(m_t, dy_split)
            beyond = fade * dot(b, dhb)
            dxdt = inside + beyond
            dx = dxdt * dtp + skip * dy
            acc[5:6, col] += jnp.sum(dy * x, axis=0, keepdims=True)
            d_m_t = dot_nt(x_split, dyb)
            d_scores_t = d_scores_t + d_m_t[:Q] * l0 + d_m_t[Q:] * l1
            h = hs[j, :, col]
            crossing = jnp.sum(dhp * h, axis=0, keepdims=True) * jnp.exp(last)
            t1 = dxdt * x
            t2 = dy * (act[rows, col] - skip * x) - xdtb.astype(f32) * inside
            t2 = t2 + jnp.where(sub == Q - 1, crossing, 0.0)
            t3 = xdt * beyond
            pick = (lane == jnp.where(sub < 64, 2 * i, 2 * i + 1)).astype(f32).astype(bf16)
            hi, lo = halves(jnp.concatenate([t1, t2, t3], axis=0))
            per_head = per_head + dot(
                jnp.concatenate([hi, lo], axis=1), jnp.concatenate([pick, pick], axis=0)
            )
            dye = (dy * jnp.exp(cp)).astype(bf16)
            d_c = d_c + dot_nt(dye, h.astype(bf16))
            d_b = d_b + dot_nt((xdt * fade).astype(bf16), dhb)
            dh[:, col] = dhp * jnp.exp(last) + dot(ct, dye)
            dp[rows, col] = dx * (sig * (1.0 + cx * (1.0 - sig)))
        d_b = d_b + dot(d_scores_t.astype(bf16), c)
        d_c = d_c + dot(d_scores_t.T.astype(bf16), b)
        for g, grad in ((0, d_b), (1, d_c)):
            ds[rows, g * N : (g + 1) * N] = grad * (sig_s[g] * (1.0 + pre_s[g] * (1.0 - sig_s[g])))
        da = tri_dot(tri_up, per_head[Q : 2 * Q]) + tri_dot(below, per_head[2 * Q :])
        ddt = per_head[:Q] - rate * da
        dstep = ddt * jax.nn.sigmoid(raw_all[rows])
        accs[5:6, 0:128] += jnp.sum(a * da, axis=0, keepdims=True)
        accs[6:7, 0:128] += jnp.sum(dstep, axis=0, keepdims=True)
        for g in range(2):
            low[rows, g * LATE + 512 : g * LATE + 640] = dstep.astype(bf16)
    for frame, grads, taps, out, width in ((vx, dp, prm, acc, CH), (vs, ds, prs, accs, 2 * N)):
        for i in range(width // 128):
            col = slice(128 * i, 128 * i + 128)
            g, p = divmod(i, width // 256)
            to = g * LATE + 128 * p + (HALF if width == 2 * N else 0)
            back_v = sum(taps[k : k + 1, col] * grads[3 - k : 3 - k + STEP, col] for k in range(4))
            low[:, to : to + 128] = back_v.astype(bf16)
            own = grads[0:STEP, col]
            for k in range(4):
                out[k : k + 1, col] += jnp.sum(own * frame[5 + k : 5 + k + STEP, col], axis=0, keepdims=True)
            out[4:5, col] += jnp.sum(own, axis=0, keepdims=True)
    head_rows[0:8, :] = dp[0:8, :]
    head_rows[8:16, :] = jnp.concatenate([ds[0:8, :], jnp.zeros((8, CH - 2 * N), f32)], axis=1)
    if s == 2:
        out_msg[0:128, :] = dh[...].astype(bf16)
        out_msg[128:144, :] = jnp.concatenate([head_rows[0:8, :]] * 2, axis=0).astype(bf16)
        out_msg[144:160, :] = jnp.concatenate([head_rows[8:16, :]] * 2, axis=0).astype(bf16)


def feat_kernel(lowz, lowl, w, feat, out, gain):
    i = pl.program_id(0)
    total = jnp.zeros((STEP, D), f32)
    for g in range(2):
        total = total + dot_nt(lowz[:, g * HALF : (g + 1) * HALF], w[:, g * LEFT : g * LEFT + HALF])
        total = total + dot_nt(lowl[:, g * LATE : (g + 1) * LATE], w[:, g * LEFT + HALF : (g + 1) * LEFT])

    @pl.when(i == 0)
    def _():
        gain[...] = jnp.zeros_like(gain)

    part = jnp.sum(total * feat[...].astype(f32), axis=0, keepdims=True)
    gain[...] += jnp.where(iota((8, D), 0) == 0, part, 0.0)
    store_rows(i, total.astype(bf16), out)


ANY = pl.BlockSpec(memory_space=pl.ANY)
PARAMS = pltpu.CompilerParams(vmem_limit_bytes=VMEM_LIMIT)


def shape(*s, dtype=f32):
    return jax.ShapeDtypeStruct(s, dtype)


def cost(flops, moved_bytes):
    return pl.CostEstimate(flops=int(flops), bytes_accessed=int(moved_bytes), transcendentals=0)


def whole(*s):
    return pl.BlockSpec(s, lambda i: (0,) * len(s))


def steps(width, column=0):
    return pl.BlockSpec((STEP, width), lambda i: (i, column))


def fixed(s, width, column=0):
    return pl.BlockSpec((STEP, width), lambda i: (s, column))


def project(rows, weights, gain):
    return pl.pallas_call(
        proj_kernel,
        grid=(8,),
        in_specs=[ANY] * 15 + [whole(1, D)],
        out_specs=[ANY, ANY, pl.BlockSpec((ROWS, 256), lambda i: (0, i))],
        out_shape=[shape(ROWS, D, dtype=bf16), shape(D, 2 * LEFT, dtype=bf16), shape(ROWS, 2 * LEFT)],
        scratch_shapes=[
            pltpu.VMEM((ROWS, D), bf16),
            pltpu.VMEM((ROWS, D), bf16),
            pltpu.VMEM((D, 2 * LEFT), bf16),
            pltpu.SemaphoreType.DMA((N_ROW_COPIES,)),
            pltpu.SemaphoreType.DMA((32,)),
            pltpu.SemaphoreType.DMA((2,)),
        ],
        compiler_params=PARAMS,
        cost_estimate=cost(2 * ROWS * D * 2 * LEFT, 24e6),
        name="project",
    )(*rows, *weights, gain)


def prev_spec(s):
    return pl.BlockSpec((8, 2 * LEFT), lambda i: (32 * s - 1, 0))


def forward(s, pre, act, h, msg, prm, prs, heads):
    ins, specs = [pre], [fixed(s, 2 * LEFT)]
    if s:
        ins += [pre, h]
        specs += [prev_spec(s), pl.BlockSpec((1, N, CH), lambda i: (2, 0, 0))]
    if s == 2:
        ins += [msg]
        specs += [whole(160, CH)]
    ins += [prm, prs, heads]
    specs += [whole(8, CH), whole(8, 2 * N), whole(8, 128)]
    aliases = {}
    if s:
        aliases = {len(ins): 0}
        ins += [act]
        specs += [ANY]
    outs = [shape(ROWS, 2 * CH + 2 * N), shape(3, N, CH)]
    out_specs = [fixed(s, 2 * CH + 2 * N), whole(3, N, CH)]
    if s == 0:
        outs += [shape(160, CH, dtype=bf16)]
        out_specs += [whole(160, CH)]
    return pl.pallas_call(
        functools.partial(fwd_kernel, s),
        grid=(1,),
        in_specs=specs,
        out_specs=out_specs,
        out_shape=outs,
        input_output_aliases=aliases,
        scratch_shapes=[pltpu.VMEM((264, CH), f32), pltpu.VMEM((264, 2 * N), f32)],
        compiler_params=PARAMS,
        cost_estimate=cost(1.5e9, 6e6),
        name=f"scan_rows_{s}",
    )(*ins)


def cotangent(rows, weights, pre, act, prm):
    return pl.pallas_call(
        cot_kernel,
        grid=(3,),
        in_specs=[ANY] * 15 + [steps(512, 0), steps(512, 2), steps(CH), whole(8, CH)],
        out_specs=[ANY, ANY, steps(CH), steps(CH), pl.BlockSpec((8, STEP), lambda i: (0, i))],
        out_shape=[
            shape(ROWS, D, dtype=bf16),
            shape(D, CH, dtype=bf16),
            shape(ROWS, CH),
            shape(ROWS, CH, dtype=bf16),
            shape(8, ROWS),
        ],
        scratch_shapes=[
            pltpu.VMEM((ROWS, D), bf16),
            pltpu.VMEM((D, CH), bf16),
            pltpu.SemaphoreType.DMA((N_ROW_COPIES,)),
            pltpu.SemaphoreType.DMA((32,)),
            pltpu.SemaphoreType.DMA((2,)),
        ],
        compiler_params=PARAMS,
        cost_estimate=cost(2 * ROWS * D * CH, 20e6),
        name="cotangent",
    )(*rows, *weights, pre, pre, act, prm)


def out_partial(gb, w):
    return pl.pallas_call(
        out_kernel,
        grid=(3,),
        in_specs=[steps(CH), whole(D, CH)],
        out_specs=whole(12, 64, D),
        out_shape=shape(12, 64, D, dtype=bf16),
        compiler_params=PARAMS,
        cost_estimate=cost(2 * ROWS * D * CH, 6e6),
        name="out_partial",
    )(gb, w)


def gate_back(sums, gm, act, pre, prm):
    row = pl.BlockSpec((8, STEP), lambda i: (0, i))
    return pl.pallas_call(
        gate_kernel,
        grid=(3,),
        in_specs=[row] * 4 + [steps(CH), steps(CH), steps(512, 0), steps(512, 2), whole(8, CH)],
        out_specs=[steps(CH), steps(CH), steps(CH), whole(8, CH)],
        out_shape=[shape(ROWS, CH, dtype=bf16)] * 3 + [shape(8, CH)],
        compiler_params=PARAMS,
        cost_estimate=cost(1e7, 12e6),
        name="gate_back",
    )(*sums, gm, act, pre, pre, prm)


def grad_tiles(ins, jobs, width):
    return pl.pallas_call(
        functools.partial(grad_kernel, jobs),
        in_specs=[pl.BlockSpec(memory_space=pltpu.VMEM)] * len(ins),
        out_specs=ANY,
        out_shape=shape(32, 96, width, dtype=bf16),
        scratch_shapes=[pltpu.VMEM((2, D, HALF), bf16), pltpu.SemaphoreType.DMA((2, 16))],
        compiler_params=PARAMS,
        cost_estimate=cost(sum(2 * ROWS * D * j[3] for j in jobs), 12e6),
        name="weight_grads",
    )(*ins)


def backward(s, pre, msg, act, hs, dssd, prm, prs, heads, carried, back, low):
    ins, specs = [pre], [fixed(s, 2 * LEFT)]
    if s:
        ins += [pre]
        specs += [prev_spec(s)]
    if s == 2:
        ins += [msg]
        specs += [whole(160, CH)]
    ins += [act, hs, dssd, prm, prs, heads]
    specs += [fixed(s, 2 * CH + 2 * N), whole(3, N, CH), fixed(s, CH)]
    specs += [whole(8, CH), whole(8, 2 * N), whole(8, 128)]
    aliases = {}
    if s < 2:
        ins += list(carried)
        specs += [whole(N, CH), whole(16, CH), whole(8, CH), whole(8, 2 * N)]
        if s == 0:
            ins += [back]
            specs += [whole(160, CH)]
        aliases = {len(ins): 0}
        ins += [low]
        specs += [ANY]
    outs = [shape(ROWS, 2 * LATE, dtype=bf16), shape(N, CH), shape(16, CH), shape(8, CH), shape(8, 2 * N)]
    out_specs = [fixed(s, 2 * LATE), whole(N, CH), whole(16, CH), whole(8, CH), whole(8, 2 * N)]
    if s == 2:
        outs += [shape(160, CH, dtype=bf16)]
        out_specs += [whole(160, CH)]
    return pl.pallas_call(
        functools.partial(bwd_kernel, s),
        grid=(1,),
        in_specs=specs,
        out_specs=out_specs,
        out_shape=outs,
        input_output_aliases=aliases,
        scratch_shapes=[
            pltpu.VMEM((264, CH), f32),
            pltpu.VMEM((264, 2 * N), f32),
            pltpu.VMEM((264, CH), f32),
            pltpu.VMEM((264, 2 * N), f32),
        ],
        compiler_params=PARAMS,
        cost_estimate=cost(4e9, 8e6),
        name=f"scan_back_{s}",
    )(*ins)


def feat_partial(lowz, lowl, w, feat):
    return pl.pallas_call(
        feat_kernel,
        grid=(3,),
        in_specs=[steps(CH), steps(2 * LATE), whole(D, 2 * LEFT), steps(D)],
        out_specs=[whole(12, 64, D), whole(8, D)],
        out_shape=[shape(12, 64, D, dtype=bf16), shape(8, D)],
        compiler_params=PARAMS,
        cost_estimate=cost(2 * ROWS * D * 2 * LEFT, 16e6),
        name="feat_partial",
    )(lowz, lowl, w, feat)


def local(
    layer_input,
    input_gain,
    proj_inner,
    proj_step,
    proj_state,
    proj_output,
    conv_inner,
    conv_inner_bias,
    conv_state,
    conv_state_bias,
    inner_gain,
    decay_log,
    step_bias,
    skip_gain,
    out_cotangent,
):
    zl = lax.axis_index("zl")
    small = jnp.concatenate(
        [
            conv_inner,
            conv_inner_bias[None],
            inner_gain[None],
            jnp.pad(jnp.stack([decay_log, step_bias, skip_gain]).reshape(1, -1), ((0, 0), (0, HALF - 18))),
            jnp.zeros((1, HALF), f32),
        ],
        axis=0,
    )
    far = send(small, "zl", 1)
    lo, hi = jnp.where(zl == 0, small, far), jnp.where(zl == 0, far, small)
    coef = jnp.concatenate([lo[6, :18].reshape(3, 6), hi[6, :18].reshape(3, 6)], axis=1)
    prm = jnp.concatenate(
        [
            jnp.concatenate([lo[:6], hi[:6]], axis=1),
            jnp.repeat(coef[2:3], 64, axis=1),
            jnp.zeros((1, CH), f32),
        ],
        axis=0,
    )
    heads = jnp.pad(jnp.stack([jnp.exp(coef[0]), coef[1]]), ((0, 6), (0, 116)))
    prs = jnp.concatenate([conv_state, conv_state_bias[None], jnp.zeros((3, 2 * N), f32)], axis=0)

    step_cols = jnp.where(
        zl == 0, jnp.pad(proj_step, ((0, 0), (0, 122))), jnp.pad(proj_step, ((0, 0), (6, 116)))
    )
    state_cols = jnp.where(zl == 0, proj_state[:, :N], proj_state[:, N:])
    shard = jnp.concatenate(
        [proj_inner[:, 0], proj_inner[:, 1], state_cols, step_cols, proj_output.T], axis=1
    )
    line = jnp.concatenate((shard,) + ring_gather(shard, "first"), axis=0)
    mine = (line,) + ring_gather(line, "second")
    weights = mine + tuple(send(a, "c", 1) for a in mine)

    rows = (layer_input,) + ring_gather(layer_input, "x")
    feat, w_in, pre = project(rows, weights, input_gain[None])
    cot_rows = (out_cotangent,) + ring_gather(out_cotangent, "x")

    act, hs0, msg = forward(0, pre, None, None, None, prm, prs, heads)
    msg = send(msg, "zl", 1)
    act, hs1 = forward(1, pre, act, hs0, None, prm, prs, heads)
    act, hs2 = forward(2, pre, act, hs1, msg, prm, prs, heads)
    cot, w_o, gm, gb, sums = cotangent(cot_rows, weights, pre, act, prm)
    others = tuple(send(sums, "x", k) for k in (1, 2, 3))
    part = out_partial(gb, w_o)
    out_terms = ring_scatter(part.reshape(4, 192, D), "x")
    dssd, lowz, mixed, ggain = gate_back((sums,) + others, gm, act, pre, prm)
    early = grad_tiles(
        (feat, lowz, cot, mixed),
        ((0, 1, 0, HALF, 0, 0), (0, 1, HALF, HALF, 1, 0), (2, 3, 0, HALF, 0, HALF), (2, 3, HALF, HALF, 1, HALF)),
        2 * HALF,
    )
    early = scatter_tiles(early.reshape(2, 4, 4, 96, 2 * HALF))

    low, *carried, back = backward(2, pre, msg, act, hs2, dssd, prm, prs, heads, None, None, None)
    back = send(back, "zl", 1)
    low, *carried = backward(1, pre, None, act, hs1, dssd, prm, prs, heads, carried, None, low)
    low, _, _, acc, accs = backward(0, pre, None, act, hs0, dssd, prm, prs, heads, carried, back, low)
    partial_feat, gain_part = feat_partial(lowz, low, w_in, feat)
    feat_terms = ring_scatter(partial_feat.reshape(4, 192, D), "x")
    late = grad_tiles(
        (feat, low),
        (
            (0, 1, 0, HALF, 0, 0),
            (0, 1, LATE, HALF, 1, 0),
            (0, 1, HALF, 256, 0, HALF),
            (0, 1, LATE + HALF, 256, 1, HALF),
        ),
        LATE,
    )
    late = scatter_tiles(late.reshape(2, 4, 4, 96, LATE))

    by_x = jnp.concatenate([accs[:5].reshape(-1), gain_part[0]]).reshape(22, 128)
    by_x = everyone(by_x, "x")
    both = jnp.concatenate(
        [acc[:6].reshape(36, 128), ggain[0].reshape(6, 128), accs[5:7, :128], by_x], axis=0
    )
    both = jnp.pad(both, ((0, 6), (0, 0)))
    both = both + send(both, "c", 1)
    both = everyone(both, "y")
    both = everyone(both, "z")

    own = lambda a: jnp.where(zl == 0, a[..., :HALF], a[..., HALF:])
    six = lambda a: jnp.where(zl == 0, a[:6], a[6:12])
    conv = own(both[:36].reshape(6, CH))
    g_inner_gain = own(both[36:42].reshape(CH))
    g_skip = six(both[30:36].reshape(12, 64).sum(axis=1))
    g_decay, g_bias = six(both[42]), six(both[43])
    states = both[44:54].reshape(5, 2 * N)
    g_input_gain = both[54:66].reshape(D) / input_gain

    values = layer_input.astype(f32)
    squares = sums[0] + others[0][0] + others[1][0] + others[2][0]
    at = lax.rem(192 * lax.axis_index("x") + 256 + 256 * zl, ROWS)
    squares = lax.dynamic_slice_in_dim(jnp.concatenate([squares, squares]), at, 192)
    scale = lax.rsqrt(squares / DI + EPS)[:, None]
    layer_output = (values + add3(out_terms) * scale).astype(bf16)
    inv = lax.rsqrt(jnp.mean(values * values, axis=1, keepdims=True) + EPS)
    weighted = add3(feat_terms) * input_gain
    input_grad = (
        out_cotangent.astype(f32)
        + weighted * inv
        - values * (inv * inv * inv) * jnp.mean(weighted * values, axis=1, keepdims=True)
    )
    state_part = late[:, HALF : HALF + N]
    state_part = everyone(state_part, "x")
    state_far = send(state_part, "zl", 1)
    g_state = jnp.where(
        zl == 0,
        jnp.concatenate([state_part, state_far], axis=1),
        jnp.concatenate([state_far, state_part], axis=1),
    )
    g_step = jnp.where(zl == 0, late[:, 512:518], late[:, 518:524])
    return (
        layer_output,
        input_grad,
        g_input_gain,
        jnp.stack([early[:, :HALF], late[:, :HALF]], axis=1),
        g_step,
        g_state,
        early[:, HALF:].T,
        conv[:4],
        conv[4],
        states[:4],
        states[4],
        g_inner_gain,
        g_decay,
        g_bias,
        g_skip,
    )


def solution(mesh):
    split = Mesh(mesh.devices.reshape(SIZES), AX)
    everything = FSDP + TP
    return jax.shard_map(
        local,
        mesh=split,
        in_specs=(
            P(everything, None),
            P(),
            P(FSDP, None, TP),
            P(FSDP, TP),
            P(FSDP, None),
            P(TP, FSDP),
            P(None, TP),
            P(TP),
            P(),
            P(),
            P(TP),
            P(TP),
            P(TP),
            P(TP),
            P(everything, None),
        ),
        out_specs=(
            P(everything, None),
            P(everything, None),
            P(),
            P(FSDP, None, TP),
            P(FSDP, TP),
            P(FSDP, None),
            P(TP, FSDP),
            P(None, TP),
            P(TP),
            P(),
            P(),
            P(TP),
            P(TP),
            P(TP),
            P(TP),
        ),
        check_vma=False,
    )
```

```python
import functools
import itertools

import jax
import jax.numpy as jnp
import numpy as np
from jax import lax
from jax.experimental import pallas as pl
from jax.experimental.pallas import tpu as pltpu
from jax.sharding import Mesh
from jax.sharding import PartitionSpec as P

D = 1536
DI = 3072
N = 128
Q = 128
STEP = 256
ROWS = 768
CH = 768
HALF = 384
PAIRS = 6
LEFT = 1024
FULL = LEFT + HALF
EPS = 1e-05
NEG = -1e30

AX = ("zh", "y", "c", "zl", "x")
SIZES = (2, 4, 2, 2, 4)
FSDP = ("zh", "y", "c")
TP = ("zl", "x")

bf16 = jnp.bfloat16
f32 = jnp.float32


def moved(d, axis, k):
    d = dict(d)
    if axis == "z":
        z = (2 * d["zh"] + d["zl"] + k) % 4
        d["zh"], d["zl"] = divmod(z, 2)
    elif axis == "first":
        return moved(d, "y" if d["c"] == 0 else "z", k)
    elif axis == "second":
        return moved(d, "z" if d["c"] == 0 else "y", k)
    else:
        d[axis] = (d[axis] + k) % SIZES[AX.index(axis)]
    return d


def send(a, axis, k):
    pairs = []
    for place in itertools.product(*map(range, SIZES)):
        to = moved(dict(zip(AX, place)), axis, k)
        pairs.append(
            (
                int(np.ravel_multi_index(place, SIZES)),
                int(np.ravel_multi_index([to[n] for n in AX], SIZES)),
            )
        )
    return lax.ppermute(a, AX, pairs)


def spread(a, axis):
    return tuple(send(a, axis, k) for k in (1, 2, 3))


def deal(parts, axis):
    return (parts[0],) + tuple(send(parts[k], axis, k) for k in (1, 2, 3))


def add4(terms):
    a, b, c, d = (t.astype(f32) for t in terms)
    return (a + b) + (c + d)


def dot(a, b):
    return lax.dot_general(a, b, (((1,), (0,)), ((), ())), preferred_element_type=f32)


def dot_nt(a, b):
    return lax.dot_general(a, b, (((1,), (1,)), ((), ())), preferred_element_type=f32)


def dot_tn(a, b):
    return lax.dot_general(a, b, (((0,), (0,)), ((), ())), preferred_element_type=f32)


def halves(a):
    hi = a.astype(bf16)
    return hi, (a - hi.astype(f32)).astype(bf16)


def thirds(a):
    hi = a.astype(bf16)
    rest = a - hi.astype(f32)
    mid = rest.astype(bf16)
    return hi, mid, (rest - mid.astype(f32)).astype(bf16)


def tri_dot(tri, a):
    return dot(jnp.concatenate([tri] * 3, axis=1), jnp.concatenate(thirds(a), axis=0))


def lanes_of(a, i):
    return jnp.broadcast_to(a[:, i : i + 1], (Q, 128))


def iota(shape, dim):
    return lax.broadcasted_iota(jnp.int32, shape, dim)


def softplus(v):
    return jnp.maximum(v, 0.0) + jnp.log1p(jnp.exp(-jnp.abs(v)))


def here():
    return {n: lax.axis_index(n) for n in AX}


def row_copies(pieces, dst, sems):
    me = here()
    copies = []
    for k, ref in enumerate(pieces):
        x = lax.rem(me["x"] + 4 - k, 4)
        for g in range(3):
            at = lax.rem(3 * x + g + 4 + 4 * me["zl"], 12)
            copies.append((ref.at[pl.ds(64 * g, 64)], dst.at[pl.ds(pl.multiple_of(64 * at, 64), 64)]))
    return [pltpu.make_async_copy(s, d, sems.at[i]) for i, (s, d) in enumerate(copies)]


N_ROW_COPIES = 12


def weight_copies(pieces, column, width, dst, sems):
    me = here()
    copies = []
    for k, ref in enumerate(pieces):
        core = lax.rem(me["c"] + k // 4, 2)
        rb = -k % 4
        for kk in range(4):
            ra = -kk % 4
            y = lax.rem(me["y"] + jnp.where(core == 0, ra, rb), 4)
            z = lax.rem(2 * me["zh"] + me["zl"] + jnp.where(core == 0, rb, ra), 4)
            f = (z // 2 * 4 + y) * 2 + core
            copies.append(
                (
                    ref.at[pl.ds(96 * kk, 96), pl.ds(column, width)],
                    dst.at[
                        pl.ds(pl.multiple_of(96 * f, 96), 96),
                        pl.ds(pl.multiple_of(width * lax.rem(z, 2), 128), width),
                    ],
                )
            )
    return [pltpu.make_async_copy(s, d, sems.at[i]) for i, (s, d) in enumerate(copies)]


def line_kernel(a, b, c, d, *rest):
    for k, ref in enumerate((a, b, c, d)):
        rest[-1][96 * k : 96 * k + 96, :] = ref[...]


def norm_kernel(*refs):
    rows, gain, feat, raw, sem = refs[:4], *refs[4:]
    copies = row_copies(rows, raw, sem)
    for c in copies:
        c.start()
    for c in copies:
        c.wait()

    def norm(k, carry):
        at = pl.ds(pl.multiple_of(32 * k, 32), 32)
        v = raw[at, :].astype(f32)
        r = lax.rsqrt(jnp.mean(v * v, axis=1, keepdims=True) + EPS)
        feat[at, :] = (v * r * gain[...]).astype(bf16)
        return carry

    lax.fori_loop(0, ROWS // 32, norm, 0)


def proj_kernel(*refs):
    weights, (feat, w_out, pre, w, wsem, osem) = refs[:8], refs[8:]
    i = pl.program_id(0)
    out = pltpu.make_async_copy(w, w_out, osem.at[0])

    @pl.when(i == 0)
    def _():
        copies = weight_copies(weights, 0, LEFT, w, wsem)
        for c in copies:
            c.start()
        for c in copies:
            c.wait()
        out.start()

    pre[...] = dot(feat[...], w[:, pl.ds(pl.multiple_of(256 * i, 256), 256)])

    @pl.when(i == pl.num_programs(0) - 1)
    def _():
        out.wait()


def pair_places(i):
    g, p = divmod(i, 3)
    return slice(128 * i, 128 * i + 128), g * LEFT + HALF + 128 * p


def step_sizes(pre, heads):
    raw = pre[:, 896:1024] + pre[:, LEFT + 896 : LEFT + 1024] + heads[1:2, :]
    return raw, softplus(raw)


def framed_inputs(s, zl, pre, prev, msg, vx, vs):
    for g in range(2):
        base = g * LEFT + HALF
        vx[8:264, g * HALF : (g + 1) * HALF] = pre[:, base : base + HALF]
        vs[8:264, g * N : (g + 1) * N] = pre[:, base + HALF : base + HALF + N]
        if s == 0:
            vx[0:8, g * HALF : (g + 1) * HALF] = jnp.zeros((8, HALF), f32)
            vs[0:8, g * N : (g + 1) * N] = jnp.zeros((8, N), f32)
            continue
        hx, hs = prev[:, base : base + HALF], prev[:, base + HALF : base + HALF + N]
        if s == 1:
            hx, hs = jnp.where(zl == 1, hx, 0.0), jnp.where(zl == 1, hs, 0.0)
        else:
            mx = msg[128:144, g * HALF : (g + 1) * HALF].astype(f32)[:8]
            ms = msg[144:160, g * N : (g + 1) * N].astype(f32)[:8]
            hx, hs = jnp.where(zl == 0, hx, mx), jnp.where(zl == 0, hs, ms)
        vx[0:8, g * HALF : (g + 1) * HALF] = hx
        vs[0:8, g * N : (g + 1) * N] = hs


def fwd_kernel(s, *refs):
    refs = list(refs)
    pre = refs.pop(0)
    prev = refs.pop(0) if s else None
    h_in = refs.pop(0) if s else None
    msg = refs.pop(0) if s == 2 else None
    prm, prs, heads = refs[:3]
    refs = refs[3:]
    if s:
        refs.pop(0)
    act, hs = refs[:2]
    refs = refs[2:]
    out_msg = refs.pop(0) if s == 0 else None
    vx, vs = refs
    zl = lax.axis_index("zl")
    framed_inputs(s, zl, pre, prev, msg, vx, vs)
    if s == 0:
        hs[0] = jnp.zeros((N, CH), f32)
    elif s == 1:
        hs[0] = jnp.where(zl == 1, h_in[...].reshape(N, CH), 0.0)
    else:
        hs[0] = jnp.where(zl == 0, h_in[...].reshape(N, CH), msg[0:128, :].astype(f32))
    _, dt_all = step_sizes(pre, heads)
    a_all = -heads[0:1, :] * dt_all
    sub, lane = iota((Q, 128), 0), iota((Q, 128), 1)
    low_mask = sub >= lane
    tri = jnp.where(low_mask, 1.0, 0.0).astype(bf16)
    left = lane < 64
    for j in range(2):
        r0 = Q * j
        bc = []
        for g in range(2):
            col = slice(g * N, (g + 1) * N)
            cs = prs[4:5, col] + sum(
                prs[k : k + 1, col] * vs[5 + k + r0 : 5 + k + r0 + Q, col] for k in range(4)
            )
            act[r0 : r0 + Q, 2 * CH + g * N : 2 * CH + (g + 1) * N] = cs
            bc.append((cs * jax.nn.sigmoid(cs)).astype(bf16))
        b, c = bc
        bt = b.astype(f32).T.astype(bf16)
        scores = dot_nt(c, b)
        dt = dt_all[r0 : r0 + Q]
        cum = tri_dot(tri, a_all[r0 : r0 + Q])
        cum_t = cum.T
        for i in range(PAIRS):
            col, _ = pair_places(i)
            cx = prm[4:5, col] + sum(
                prm[k : k + 1, col] * vx[5 + k + r0 : 5 + k + r0 + Q, col] for k in range(4)
            )
            act[r0 : r0 + Q, CH + 128 * i : CH + 128 * i + 128] = cx
            x = (cx * jax.nn.sigmoid(cx)).astype(bf16).astype(f32)
            c0, c1 = lanes_of(cum, 2 * i), lanes_of(cum, 2 * i + 1)
            m0 = scores * jnp.exp(jnp.where(low_mask, c0 - cum_t[2 * i : 2 * i + 1, :], NEG))
            m1 = scores * jnp.exp(jnp.where(low_mask, c1 - cum_t[2 * i + 1 : 2 * i + 2, :], NEG))
            cp = jnp.where(left, c0, c1)
            xdt = x * jnp.where(left, lanes_of(dt, 2 * i), lanes_of(dt, 2 * i + 1))
            xdtb = xdt.astype(bf16)
            zero = jnp.zeros_like(xdtb)
            last = cp[Q - 1 : Q, :]
            inside = dot(
                jnp.concatenate([m0.astype(bf16), m1.astype(bf16)], axis=1),
                jnp.concatenate([jnp.where(left, xdtb, zero), jnp.where(left, zero, xdtb)], axis=0),
            )
            h = hs[j, :, col]
            y = inside + jnp.exp(cp) * dot(c, h.astype(bf16)) + prm[6:7, col] * x
            act[r0 : r0 + Q, col] = y
            hs[j + 1, :, col] = h * jnp.exp(last) + dot(bt, (xdt * jnp.exp(last - cp)).astype(bf16))
    if s == 0:
        out_msg[0:128, :] = hs[2].astype(bf16)
        out_msg[128:144, :] = jnp.concatenate([vx[256:264, :]] * 2, axis=0).astype(bf16)
        out_msg[144:160, :] = jnp.concatenate(
            [jnp.concatenate([vs[256:264, :]] * 2, axis=0), jnp.zeros((16, CH - 2 * N), f32)], axis=1
        ).astype(bf16)


def cot_kernel(*refs):
    rows, weights = refs[:4], refs[4:12]
    z0, z1, ssd, prm, cot_out, w_out, gm, gb, sums, cot, w, rsem, wsem, osem = refs[12:]
    i = pl.program_id(0)
    outs = [
        pltpu.make_async_copy(cot, cot_out, osem.at[0]),
        pltpu.make_async_copy(w, w_out, osem.at[1]),
    ]

    @pl.when(i == 0)
    def _():
        cs = row_copies(rows, cot, rsem) + weight_copies(weights, LEFT, HALF, w, wsem)
        for c in cs:
            c.start()
        for c in cs:
            c.wait()
        for c in outs:
            c.start()

    at = pl.ds(pl.multiple_of(STEP * i, STEP), STEP)
    grad = dot(cot[at, :], w[...])
    gm[...] = grad
    squares = jnp.zeros((STEP, 1), f32)
    dots = jnp.zeros((STEP, 1), f32)
    for g, z in ((0, z0), (1, z1)):
        col = slice(g * HALF, (g + 1) * HALF)
        gate = z[:, 0:HALF]
        gated = ssd[:, col] * (gate * jax.nn.sigmoid(gate))
        scaled = gated * prm[5:6, col]
        gb[:, col] = scaled.astype(bf16)
        squares = squares + jnp.sum(gated * gated, axis=1, keepdims=True)
        dots = dots + jnp.sum(grad[:, col] * scaled, axis=1, keepdims=True)
    lane = iota((STEP, 128), 1)
    both = jnp.where(lane == 0, squares, jnp.where(lane == 1, dots, 0.0))
    sums[...] = both.T[0:8, :]

    @pl.when(i == pl.num_programs(0) - 1)
    def _():
        for c in outs:
            c.wait()


def store_rows(i, value, outs):
    me = here()
    for g in range(4):
        natural = lax.rem(4 * i + g + 8 - 4 * me["zl"] + 12, 12)
        rel = lax.rem(natural // 3 - me["x"] + 4, 4)
        at = pl.ds(pl.multiple_of(64 * lax.rem(natural, 3), 64), 64)
        for k in range(4):

            @pl.when(rel == k)
            def _(k=k, g=g, at=at):
                outs[k][at, :] = value[64 * g : 64 * g + 64, :]


def out_kernel(gb, w, *outs):
    store_rows(pl.program_id(0), dot_nt(gb[...], w[...]).astype(bf16), outs)


def gate_kernel(s0, s1, s2, s3, gm, ssd, z0, z1, prm, *refs):
    dssd, lowz, mixed, ggain = refs[-4:]
    i = pl.program_id(0)
    total = (s0[...] + s1[...] + s2[...] + s3[...]).T
    inv = lax.rsqrt(total[:, 0:1] / DI + EPS)
    pull = inv * inv * inv * (total[:, 1:2] / DI)

    @pl.when(i == 0)
    def _():
        ggain[...] = jnp.zeros_like(ggain)

    for g, z in ((0, z0), (1, z1)):
        col = slice(g * HALF, (g + 1) * HALF)
        gate = z[:, 0:HALF]
        sig = jax.nn.sigmoid(gate)
        silu = gate * sig
        y = ssd[:, col]
        gated = y * silu
        grad = gm[:, col]
        gain = prm[5:6, col]
        normal = gated * inv
        mixed[:, col] = (normal * gain).astype(bf16)
        dg = grad * gain * inv - gated * pull
        dssd[:, col] = (dg * silu).astype(bf16)
        lowz[:, col] = (dg * y * (sig * (1.0 + gate * (1.0 - sig)))).astype(bf16)
        part = jnp.sum(grad * normal, axis=0, keepdims=True)
        ggain[:, col] += jnp.where(iota((8, HALF), 0) == 0, part, 0.0)


def tile_place(f, g):
    me = here()
    core = f % 2
    y, zh = (f // 2) % 4, f // 8
    dy = lax.rem(y - me["y"] + 4, 4)
    dz = lax.rem(2 * zh + g - (2 * me["zh"] + me["zl"]) + 4, 4)
    return me["c"] == core, (4 * dz + dy if core == 0 else 4 * dy + dz)


def grad_kernel(jobs, n_in, *refs):
    ins, own, far, buf, sem = refs[:n_in], *refs[-4:]
    count = 0
    pending = []
    base = 0
    for a, pieces, places in jobs:
        rhs = jnp.concatenate([ins[b][:, col : col + width] for b, col, width in pieces], axis=1)
        total = rhs.shape[1]
        for m in range(4):
            rows = slice(384 * m, 384 * m + 384)
            part = dot_tn(ins[a][:, rows], rhs)
            buf[rows, base : base + total] = part.astype(bf16)
            for f in range(4 * m, 4 * m + 4):
                for col, g, to in places:
                    here_too, at = tile_place(f, g)
                    src = buf.at[pl.ds(96 * f, 96), pl.ds(base + col, HALF)]
                    for flag, out in ((here_too, own), (jnp.logical_not(here_too), far)):
                        copy = pltpu.make_async_copy(
                            src, out.at[pl.ds(pl.multiple_of(96 * at, 96), 96), pl.ds(to, HALF)], sem.at[count]
                        )

                        @pl.when(flag)
                        def _(copy=copy):
                            copy.start()

                    pending.append(copy)
                    count += 1
        base += total
    for copy in pending:
        copy.wait()


def split_small(total):
    return jnp.concatenate(halves(total), axis=0)


def sum_small(block):
    return block[:16].astype(f32) + block[16:].astype(f32)


def core_sum_kernel(with_small, *refs):
    own, far = refs[:2]
    outs = refs[-4:]
    if with_small:
        small = split_small(refs[2][...] + refs[3][...])
    for k, out in enumerate(outs):
        rows = slice(384 * k, 384 * k + 384)
        out[0:384, :] = (own[rows, :].astype(f32) + far[rows, :].astype(f32)).astype(bf16)
        if with_small:
            out[384:416, :] = small


def axis_sum_kernel(with_small, *refs):
    terms, outs = refs[:4], refs[-4:]
    if with_small:
        small = split_small(sum(sum_small(t[384:416, :]) for t in terms))
    for k, out in enumerate(outs):
        rows = slice(96 * k, 96 * k + 96)
        out[0:96, :] = add4([t[rows, :] for t in terms]).astype(bf16)
        if with_small:
            out[96:128, :] = small


def last_sum_kernel(*refs):
    terms, (tile, small, to_x) = refs[:4], refs[-3:]
    total = add4([t[0:96, :] for t in terms])
    tile[...] = total
    every = sum(sum_small(t[96:128, :]) for t in terms)
    small[...] = every
    for k in range(3):
        rows = slice(32 * k, 32 * k + 32)
        to_x[0:32, 256 * k : 256 * k + 128] = total[rows, HALF : HALF + N].astype(bf16)
        to_x[0:32, 256 * k + 128 : 256 * k + 256] = total[rows, HALF + 2 * N : HALF + 3 * N].astype(bf16)
    hi, lo = halves(every[8:16, :])
    to_x[32:48, :] = jnp.concatenate([hi.astype(f32), lo.astype(f32)], axis=0).astype(bf16)


def x_sum_kernel(a, b, c, d, state, small):
    total = add4([a[...], b[...], c[...], d[...]])
    for k in range(3):
        state[32 * k : 32 * k + 32, :] = total[0:32, 256 * k : 256 * k + 256]
    small[...] = total[32:40, :] + total[40:48, :]


def bwd_kernel(s, *refs):
    refs = list(refs)
    pre = refs.pop(0)
    prev = refs.pop(0) if s else None
    msg = refs.pop(0) if s == 2 else None
    act, hs, dssd, lowz, prm, prs, heads = refs[:7]
    refs = refs[7:]
    if s < 2:
        dh_in, tail, acc_in, accs_in = refs[:4]
        refs = refs[4:]
        back = refs.pop(0) if s == 0 else None
    refs = refs[len(refs) - (10 if s == 2 else 9) :]
    low, dh, head_rows, acc, accs = refs[:5]
    refs = refs[5:]
    for g in range(2):
        low[:, g * LEFT : g * LEFT + HALF] = lowz[:, g * HALF : (g + 1) * HALF]
    out_msg = refs.pop(0) if s == 2 else None
    vx, vs, dp, ds = refs
    zl = lax.axis_index("zl")
    framed_inputs(s, zl, pre, prev, msg, vx, vs)
    if s == 2:
        dh[...] = jnp.zeros_like(dh)
        dp[256:264, :] = jnp.zeros((8, CH), f32)
        ds[256:264, :] = jnp.zeros((8, 2 * N), f32)
        acc[...] = jnp.zeros_like(acc)
        accs[...] = jnp.zeros_like(accs)
    else:
        hd, hp, hq = dh_in[...], tail[0:8, :], tail[8:16, 0 : 2 * N]
        if s == 1:
            hd, hp, hq = (jnp.where(zl == 0, v, 0.0) for v in (hd, hp, hq))
        else:
            hd = jnp.where(zl == 1, hd, back[0:128, :].astype(f32))
            hp = jnp.where(zl == 1, hp, back[128:144, :].astype(f32)[:8])
            hq = jnp.where(zl == 1, hq, back[144:160, 0 : 2 * N].astype(f32)[:8])
        dh[...], dp[256:264, :], ds[256:264, :] = hd, hp, hq
        acc[...] = acc_in[...]
        accs[...] = accs_in[...]
    raw_all, dt_all = step_sizes(pre, heads)
    rate = heads[0:1, :]
    a_all = -rate * dt_all
    sub, lane = iota((Q, 128), 0), iota((Q, 128), 1)
    tri = jnp.where(sub >= lane, 1.0, 0.0).astype(bf16)
    up_mask = lane >= sub
    tri_up = jnp.where(up_mask, 1.0, 0.0).astype(bf16)
    below = jnp.where(lane < sub, 1.0, 0.0).astype(bf16)
    left = lane < 64
    for j in (1, 0):
        r0 = Q * j
        rows = slice(r0, r0 + Q)
        pre_s = [act[rows, 2 * CH + g * N : 2 * CH + (g + 1) * N] for g in range(2)]
        sig_s = [jax.nn.sigmoid(v) for v in pre_s]
        bf, cf = [(v * w).astype(bf16).astype(f32) for v, w in zip(pre_s, sig_s)]
        b, c = bf.astype(bf16), cf.astype(bf16)
        ct = cf.T.astype(bf16)
        scores_t = dot_nt(c, b).T
        dt, a = dt_all[rows], a_all[rows]
        cum = tri_dot(tri, a)
        cum_t = cum.T
        d_scores_t = jnp.zeros((Q, Q), f32)
        d_b = jnp.zeros((Q, N), f32)
        d_c = jnp.zeros((Q, N), f32)
        per_head = jnp.zeros((3 * Q, 128), f32)
        for i in range(PAIRS):
            col, _ = pair_places(i)
            cx = act[rows, CH + 128 * i : CH + 128 * i + 128]
            sig = jax.nn.sigmoid(cx)
            x = (cx * sig).astype(bf16).astype(f32)
            dyb = dssd[rows, col]
            dy = dyb.astype(f32)
            skip = prm[6:7, col]
            c0, c1 = lanes_of(cum, 2 * i), lanes_of(cum, 2 * i + 1)
            l0 = jnp.exp(jnp.where(up_mask, cum_t[2 * i : 2 * i + 1, :] - c0, NEG))
            l1 = jnp.exp(jnp.where(up_mask, cum_t[2 * i + 1 : 2 * i + 2, :] - c1, NEG))
            cp = jnp.where(left, c0, c1)
            dtp = jnp.where(left, lanes_of(dt, 2 * i), lanes_of(dt, 2 * i + 1))
            last = cp[Q - 1 : Q, :]
            fade = jnp.exp(last - cp)
            xdt = x * dtp
            xdtb = xdt.astype(bf16)
            zero = jnp.zeros_like(xdtb)
            dy_split = jnp.concatenate([jnp.where(left, dyb, zero), jnp.where(left, zero, dyb)], axis=0)
            x_split = jnp.concatenate([jnp.where(left, xdtb, zero), jnp.where(left, zero, xdtb)], axis=0)
            dhp = dh[:, col]
            dhb = dhp.astype(bf16)
            m_t = jnp.concatenate([(scores_t * l0).astype(bf16), (scores_t * l1).astype(bf16)], axis=1)
            inside = dot(m_t, dy_split)
            beyond = fade * dot(b, dhb)
            dxdt = inside + beyond
            dx = dxdt * dtp + skip * dy
            acc[5:6, col] += jnp.sum(dy * x, axis=0, keepdims=True)
            d_m_t = dot_nt(x_split, dyb)
            d_scores_t = d_scores_t + d_m_t[:Q] * l0 + d_m_t[Q:] * l1
            h = hs[j, :, col]
            crossing = jnp.sum(dhp * h, axis=0, keepdims=True) * jnp.exp(last)
            t1 = dxdt * x
            t2 = dy * (act[rows, col] - skip * x) - xdtb.astype(f32) * inside
            t2 = t2 + jnp.where(sub == Q - 1, crossing, 0.0)
            t3 = xdt * beyond
            pick = (lane == jnp.where(sub < 64, 2 * i, 2 * i + 1)).astype(f32).astype(bf16)
            hi, lo = halves(jnp.concatenate([t1, t2, t3], axis=0))
            per_head = per_head + dot(
                jnp.concatenate([hi, lo], axis=1), jnp.concatenate([pick, pick], axis=0)
            )
            dye = (dy * jnp.exp(cp)).astype(bf16)
            d_c = d_c + dot_nt(dye, h.astype(bf16))
            d_b = d_b + dot_nt((xdt * fade).astype(bf16), dhb)
            dh[:, col] = dhp * jnp.exp(last) + dot(ct, dye)
            dp[rows, col] = dx * (sig * (1.0 + cx * (1.0 - sig)))
        d_b = d_b + dot(d_scores_t.astype(bf16), c)
        d_c = d_c + dot(d_scores_t.T.astype(bf16), b)
        for g, grad in ((0, d_b), (1, d_c)):
            ds[rows, g * N : (g + 1) * N] = grad * (sig_s[g] * (1.0 + pre_s[g] * (1.0 - sig_s[g])))
        da = tri_dot(tri_up, per_head[Q : 2 * Q]) + tri_dot(below, per_head[2 * Q :])
        ddt = per_head[:Q] - rate * da
        dstep = ddt * jax.nn.sigmoid(raw_all[rows])
        accs[5:6, 0:128] += jnp.sum(a * da, axis=0, keepdims=True)
        accs[6:7, 0:128] += jnp.sum(dstep, axis=0, keepdims=True)
        for g in range(2):
            low[rows, (g + 1) * LEFT - N : (g + 1) * LEFT] = dstep.astype(bf16)
    for frame, grads, taps, out, width in ((vx, dp, prm, acc, CH), (vs, ds, prs, accs, 2 * N)):
        for i in range(width // 128):
            col = slice(128 * i, 128 * i + 128)
            g, p = divmod(i, width // 256)
            to = g * LEFT + HALF + 128 * p + (HALF if width == 2 * N else 0)
            back_v = sum(taps[k : k + 1, col] * grads[3 - k : 3 - k + STEP, col] for k in range(4))
            low[:, to : to + 128] = back_v.astype(bf16)
            own = grads[0:STEP, col]
            for k in range(4):
                out[k : k + 1, col] += jnp.sum(own * frame[5 + k : 5 + k + STEP, col], axis=0, keepdims=True)
            out[4:5, col] += jnp.sum(own, axis=0, keepdims=True)
    head_rows[0:8, :] = dp[0:8, :]
    head_rows[8:16, :] = jnp.concatenate([ds[0:8, :], jnp.zeros((8, CH - 2 * N), f32)], axis=1)
    if s == 2:
        out_msg[0:128, :] = dh[...].astype(bf16)
        out_msg[128:144, :] = jnp.concatenate([head_rows[0:8, :]] * 2, axis=0).astype(bf16)
        out_msg[144:160, :] = jnp.concatenate([head_rows[8:16, :]] * 2, axis=0).astype(bf16)


def feat_kernel(low, w, feat, acc, accs, ggain, *refs):
    outs, small = refs[-5:-1], refs[-1]
    i = pl.program_id(0)
    total = dot_nt(low[...], w[...])

    @pl.when(i == 0)
    def _():
        small[...] = jnp.zeros_like(small)
        small[0:6, :] = acc[0:6, :]
        small[6:7, :] = ggain[0:1, :]
        for row, firsts in ((7, (5, 6)), (10, (0, 1, 2)), (11, (3, 4))):
            for k, r in enumerate(firsts):
                small[row : row + 1, 256 * k : 256 * k + 256] = accs[r : r + 1, :]

    part = jnp.sum(total * feat[...].astype(f32), axis=0, keepdims=True)
    small[8:9, :] += part[:, :CH]
    small[9:10, :] += part[:, CH:]
    store_rows(i, total.astype(bf16), outs)


ANY = pl.BlockSpec(memory_space=pl.ANY)
VM = pl.BlockSpec(memory_space=pltpu.VMEM)


def params(mib):
    return pltpu.CompilerParams(vmem_limit_bytes=mib * 1024 * 1024)


def shape(*s, dtype=f32):
    return jax.ShapeDtypeStruct(s, dtype)


def cost(flops, moved_bytes):
    return pl.CostEstimate(flops=int(flops), bytes_accessed=int(moved_bytes), transcendentals=0)


def whole(*s):
    return pl.BlockSpec(s, lambda i: (0,) * len(s))


def steps(width, column=0):
    return pl.BlockSpec((STEP, width), lambda i: (i, column))


def fixed(s, width, column=0):
    return pl.BlockSpec((STEP, width), lambda i: (s, column))


def line_up(parts, deps):
    return pl.pallas_call(
        line_kernel,
        in_specs=[VM] * 4 + [ANY] * len(deps),
        out_specs=VM,
        out_shape=shape(384, FULL, dtype=bf16),
        compiler_params=params(4),
        cost_estimate=cost(1e6, 2e6),
        name="line_up",
    )(*parts, *deps)


def normalize(rows, gain):
    return pl.pallas_call(
        norm_kernel,
        in_specs=[ANY] * 4 + [VM],
        out_specs=VM,
        out_shape=shape(ROWS, D, dtype=bf16),
        scratch_shapes=[pltpu.VMEM((ROWS, D), bf16), pltpu.SemaphoreType.DMA((N_ROW_COPIES,))],
        compiler_params=params(12),
        cost_estimate=cost(1e7, 5e6),
        name="normalize",
    )(*rows, gain)


def project(feat, weights):
    return pl.pallas_call(
        proj_kernel,
        grid=(8,),
        in_specs=[ANY] * 8 + [whole(ROWS, D)],
        out_specs=[ANY, pl.BlockSpec((ROWS, 256), lambda i: (0, i))],
        out_shape=[shape(D, 2 * LEFT, dtype=bf16), shape(ROWS, 2 * LEFT)],
        scratch_shapes=[
            pltpu.VMEM((D, 2 * LEFT), bf16),
            pltpu.SemaphoreType.DMA((32,)),
            pltpu.SemaphoreType.DMA((1,)),
        ],
        compiler_params=params(20),
        cost_estimate=cost(2 * ROWS * D * 2 * LEFT, 24e6),
        name="project",
    )(*weights, feat)


def prev_spec(s):
    return pl.BlockSpec((8, 2 * LEFT), lambda i: (32 * s - 1, 0))


def forward(s, pre, act, h, msg, prm, prs, heads):
    ins, specs = [pre], [fixed(s, 2 * LEFT)]
    if s:
        ins += [pre, h]
        specs += [prev_spec(s), pl.BlockSpec((1, N, CH), lambda i: (2, 0, 0))]
    if s == 2:
        ins += [msg]
        specs += [whole(160, CH)]
    ins += [prm, prs, heads]
    specs += [whole(8, CH), whole(8, 2 * N), whole(8, 128)]
    aliases = {}
    if s:
        aliases = {len(ins): 0}
        ins += [act]
        specs += [ANY]
    outs = [shape(ROWS, 2 * CH + 2 * N), shape(3, N, CH)]
    out_specs = [fixed(s, 2 * CH + 2 * N), whole(3, N, CH)]
    if s == 0:
        outs += [shape(160, CH, dtype=bf16)]
        out_specs += [whole(160, CH)]
    return pl.pallas_call(
        functools.partial(fwd_kernel, s),
        grid=(1,),
        in_specs=specs,
        out_specs=out_specs,
        out_shape=outs,
        input_output_aliases=aliases,
        scratch_shapes=[pltpu.VMEM((264, CH), f32), pltpu.VMEM((264, 2 * N), f32)],
        compiler_params=params(24),
        cost_estimate=cost(1.5e9, 6e6),
        name=f"scan_rows_{s}",
    )(*ins)


def cotangent(rows, weights, pre, act, prm):
    return pl.pallas_call(
        cot_kernel,
        grid=(3,),
        in_specs=[ANY] * 12 + [steps(512, 0), steps(512, 2), steps(CH), whole(8, CH)],
        out_specs=[ANY, ANY, steps(CH), steps(CH), pl.BlockSpec((8, STEP), lambda i: (0, i))],
        out_shape=[
            shape(ROWS, D, dtype=bf16),
            shape(D, CH, dtype=bf16),
            shape(ROWS, CH),
            shape(ROWS, CH, dtype=bf16),
            shape(8, ROWS),
        ],
        scratch_shapes=[
            pltpu.VMEM((ROWS, D), bf16),
            pltpu.VMEM((D, CH), bf16),
            pltpu.SemaphoreType.DMA((N_ROW_COPIES,)),
            pltpu.SemaphoreType.DMA((32,)),
            pltpu.SemaphoreType.DMA((2,)),
        ],
        compiler_params=params(24),
        cost_estimate=cost(2 * ROWS * D * CH, 20e6),
        name="cotangent",
    )(*rows, *weights, pre, pre, act, prm)


def out_partial(gb, w):
    return pl.pallas_call(
        out_kernel,
        grid=(3,),
        in_specs=[steps(CH), whole(D, CH)],
        out_specs=[whole(192, D)] * 4,
        out_shape=[shape(192, D, dtype=bf16)] * 4,
        compiler_params=params(16),
        cost_estimate=cost(2 * ROWS * D * CH, 6e6),
        name="out_partial",
    )(gb, w)


def gate_back(sums, gm, act, pre, prm, deps):
    row = pl.BlockSpec((8, STEP), lambda i: (0, i))
    return pl.pallas_call(
        gate_kernel,
        grid=(3,),
        in_specs=[row] * 4
        + [steps(CH), steps(CH), steps(512, 0), steps(512, 2), whole(8, CH)]
        + [ANY] * len(deps),
        out_specs=[steps(CH), steps(CH), steps(CH), whole(8, CH)],
        out_shape=[shape(ROWS, CH, dtype=bf16)] * 3 + [shape(8, CH)],
        compiler_params=params(20),
        cost_estimate=cost(1e7, 12e6),
        name="gate_back",
    )(*sums, gm, act, pre, pre, prm, *deps)


def grad_tiles(ins, jobs, name):
    columns = sum(p[2] for j in jobs for p in j[1])
    copies = sum(16 * len(j[2]) for j in jobs)
    return pl.pallas_call(
        functools.partial(grad_kernel, jobs, len(ins)),
        in_specs=[VM] * len(ins),
        out_specs=[ANY, ANY],
        out_shape=[shape(ROWS * 2, CH, dtype=bf16)] * 2,
        scratch_shapes=[pltpu.VMEM((D, columns), bf16), pltpu.SemaphoreType.DMA((copies,))],
        compiler_params=params(32),
        cost_estimate=cost(2 * ROWS * D * columns, 12e6),
        name=name,
    )(*ins)


def tile_sums(kernel, ins, outs, deps, name):
    return pl.pallas_call(
        kernel,
        in_specs=[VM] * len(ins) + [ANY] * len(deps),
        out_specs=[VM] * len(outs),
        out_shape=outs,
        compiler_params=params(16),
        cost_estimate=cost(1e6, 4e6),
        name=name,
    )(*ins, *deps)


def core_sum(own, far, small, deps, name):
    ins = [own, far] + list(small)
    rows = 416 if small else 384
    kernel = functools.partial(core_sum_kernel, bool(small))
    return tile_sums(kernel, ins, [shape(rows, CH, dtype=bf16)] * 4, deps, name)


def axis_sum(terms, with_small, deps, name):
    rows = 128 if with_small else 96
    kernel = functools.partial(axis_sum_kernel, with_small)
    return tile_sums(kernel, list(terms), [shape(rows, CH, dtype=bf16)] * 4, deps, name)


def backward(s, pre, msg, act, hs, dssd, lowz, prm, prs, heads, carried, back, low, deps):
    ins, specs = [pre], [fixed(s, 2 * LEFT)]
    if s:
        ins += [pre]
        specs += [prev_spec(s)]
    if s == 2:
        ins += [msg]
        specs += [whole(160, CH)]
    ins += [act, hs, dssd, lowz, prm, prs, heads]
    specs += [fixed(s, 2 * CH + 2 * N), whole(3, N, CH), fixed(s, CH), fixed(s, CH)]
    specs += [whole(8, CH), whole(8, 2 * N), whole(8, 128)]
    aliases = {}
    if s < 2:
        ins += list(carried)
        specs += [whole(N, CH), whole(16, CH), whole(8, CH), whole(8, 2 * N)]
        if s == 0:
            ins += [back]
            specs += [whole(160, CH)]
        aliases = {len(ins): 0}
        ins += [low]
        specs += [ANY]
    ins += list(deps)
    specs += [ANY] * len(deps)
    outs = [shape(ROWS, 2 * LEFT, dtype=bf16), shape(N, CH), shape(16, CH), shape(8, CH), shape(8, 2 * N)]
    out_specs = [fixed(s, 2 * LEFT), whole(N, CH), whole(16, CH), whole(8, CH), whole(8, 2 * N)]
    if s == 2:
        outs += [shape(160, CH, dtype=bf16)]
        out_specs += [whole(160, CH)]
    return pl.pallas_call(
        functools.partial(bwd_kernel, s),
        grid=(1,),
        in_specs=specs,
        out_specs=out_specs,
        out_shape=outs,
        input_output_aliases=aliases,
        scratch_shapes=[
            pltpu.VMEM((264, CH), f32),
            pltpu.VMEM((264, 2 * N), f32),
            pltpu.VMEM((264, CH), f32),
            pltpu.VMEM((264, 2 * N), f32),
        ],
        compiler_params=params(28),
        cost_estimate=cost(4e9, 8e6),
        name=f"scan_back_{s}",
    )(*ins)


def feat_partial(low, w, feat, acc, accs, ggain, deps):
    return pl.pallas_call(
        feat_kernel,
        grid=(3,),
        in_specs=[steps(2 * LEFT), whole(D, 2 * LEFT), steps(D), whole(8, CH), whole(8, 2 * N), whole(8, CH)]
        + [ANY] * len(deps),
        out_specs=[whole(192, D)] * 4 + [whole(16, CH)],
        out_shape=[shape(192, D, dtype=bf16)] * 4 + [shape(16, CH)],
        compiler_params=params(32),
        cost_estimate=cost(2 * ROWS * D * 2 * LEFT, 16e6),
        name="feat_partial",
    )(low, w, feat, acc, accs, ggain, *deps)


def local(
    layer_input,
    input_gain,
    proj_inner,
    proj_step,
    proj_state,
    proj_output,
    conv_inner,
    conv_inner_bias,
    conv_state,
    conv_state_bias,
    inner_gain,
    decay_log,
    step_bias,
    skip_gain,
    out_cotangent,
):
    zl = lax.axis_index("zl")
    small = jnp.concatenate(
        [
            conv_inner,
            conv_inner_bias[None],
            inner_gain[None],
            jnp.pad(jnp.stack([decay_log, step_bias, skip_gain]).reshape(1, -1), ((0, 0), (0, HALF - 18))),
            jnp.zeros((1, HALF), f32),
        ],
        axis=0,
    )
    far = send(small, "zl", 1)
    lo, hi = jnp.where(zl == 0, small, far), jnp.where(zl == 0, far, small)
    coef = jnp.concatenate([lo[6, :18].reshape(3, 6), hi[6, :18].reshape(3, 6)], axis=1)
    prm = jnp.concatenate(
        [
            jnp.concatenate([lo[:6], hi[:6]], axis=1),
            jnp.repeat(coef[2:3], 64, axis=1),
            jnp.zeros((1, CH), f32),
        ],
        axis=0,
    )
    heads = jnp.pad(jnp.stack([jnp.exp(coef[0]), coef[1]]), ((0, 6), (0, 116)))
    prs = jnp.concatenate([conv_state, conv_state_bias[None], jnp.zeros((3, 2 * N), f32)], axis=0)

    step_cols = jnp.where(
        zl == 0, jnp.pad(proj_step, ((0, 0), (0, 122))), jnp.pad(proj_step, ((0, 0), (6, 116)))
    )
    state_cols = jnp.where(zl == 0, proj_state[:, :N], proj_state[:, N:])
    shard = jnp.concatenate(
        [proj_inner[:, 0], proj_inner[:, 1], state_cols, step_cols, proj_output.T], axis=1
    )
    rows = (layer_input,) + spread(layer_input, "x")
    line = line_up((shard,) + spread(shard, "first"), (rows[1], rows[3]))
    mine = (line,) + spread(line, "second")
    weights = mine + tuple(send(a, "c", 1) for a in mine)
    feat = normalize(rows, input_gain[None])
    w_in, pre = project(feat, weights)
    cot_rows = (out_cotangent,) + spread(out_cotangent, "x")

    act, hs0, msg = forward(0, pre, None, None, None, prm, prs, heads)
    msg = send(msg, "zl", 1)
    act, hs1 = forward(1, pre, act, hs0, None, prm, prs, heads)
    act, hs2 = forward(2, pre, act, hs1, msg, prm, prs, heads)
    cot, w_o, gm, gb, sums = cotangent(cot_rows, weights, pre, act, prm)
    all_sums = (sums,) + spread(sums, "x")
    parts = out_partial(gb, w_o)
    out_terms = deal(parts, "x")
    dssd, lowz, mixed, ggain = gate_back(all_sums, gm, act, pre, prm, (parts[0],))

    own, far = grad_tiles(
        (feat, lowz, cot, mixed),
        (
            (0, ((1, 0, CH),), ((0, 0, 0), (HALF, 1, 0))),
            (2, ((3, 0, CH),), ((0, 0, HALF), (HALF, 1, HALF))),
        ),
        "early_grads",
    )
    far = send(far, "c", 1)
    scan = (prm, prs, heads)
    low, *carried, back = backward(2, pre, msg, act, hs2, dssd, lowz, *scan, None, None, None, (own,))
    back = send(back, "zl", 1)
    parts = core_sum(own, far, (), (low,), "early_core_sum")
    terms = deal(parts, "second")
    low, *carried = backward(1, pre, None, act, hs1, dssd, lowz, *scan, carried, None, low, (parts[0],))
    low, _, _, acc, accs = backward(0, pre, None, act, hs0, dssd, lowz, *scan, carried, back, low, ())
    parts = axis_sum(terms, False, (low,) + out_terms, "early_axis_sum")
    early_terms = deal(parts, "first")

    own, far = grad_tiles(
        (feat, low, parts[0]),
        (
            (
                0,
                ((1, HALF, HALF), (1, LEFT + HALF, HALF), (1, 2 * HALF, 2 * N), (1, LEFT + 2 * HALF, N)),
                ((0, 0, 0), (HALF, 1, 0), (2 * HALF, 0, HALF), (2 * HALF, 1, HALF)),
            ),
        ),
        "late_grads",
    )
    far = send(far, "c", 1)
    *parts, small = feat_partial(low, w_in, feat, acc, accs, ggain, (own,))
    feat_terms = deal(parts, "x")
    early = add4(early_terms)
    parts = core_sum(own, far, (small, send(small, "c", 1)), (), "late_core_sum")
    parts = axis_sum(deal(parts, "second"), True, (), "late_axis_sum")
    late, small, to_x = tile_sums(
        last_sum_kernel,
        deal(parts, "first"),
        [shape(96, CH), shape(16, CH), shape(48, CH, dtype=bf16)],
        feat_terms,
        "late_last_sum",
    )
    g_state, by_x = tile_sums(
        x_sum_kernel, (to_x,) + spread(to_x, "x"), [shape(96, 2 * N), shape(8, CH)], (), "x_sum"
    )

    own = lambda a: jnp.where(zl == 0, a[..., :HALF], a[..., HALF:])
    six = lambda a: jnp.where(zl == 0, a[:6], a[6:12])
    conv = own(small[:7])
    g_skip = six(small[5].reshape(12, 64).sum(axis=1))
    g_decay, g_bias = six(small[7, :128]), six(small[7, 256:384])
    states = by_x[2:4].reshape(6, 2 * N)
    g_input_gain = by_x[0:2].reshape(D) / input_gain
    g_step = jnp.where(zl == 0, late[:, 512:518], late[:, 518:524])

    values = layer_input.astype(f32)
    squares = all_sums[0][0] + all_sums[1][0] + all_sums[2][0] + all_sums[3][0]
    at = lax.rem(192 * lax.axis_index("x") + 256 + 256 * zl, ROWS)
    squares = lax.dynamic_slice_in_dim(jnp.concatenate([squares, squares]), at, 192)
    scale = lax.rsqrt(squares / DI + EPS)[:, None]
    layer_output = (values + add4(out_terms) * scale).astype(bf16)
    inv = lax.rsqrt(jnp.mean(values * values, axis=1, keepdims=True) + EPS)
    weighted = add4(feat_terms) * input_gain
    input_grad = (
        out_cotangent.astype(f32)
        + weighted * inv
        - values * (inv * inv * inv) * jnp.mean(weighted * values, axis=1, keepdims=True)
    )
    return (
        layer_output,
        input_grad,
        g_input_gain,
        jnp.stack([early[:, :HALF], late[:, :HALF]], axis=1),
        g_step,
        g_state,
        early[:, HALF:].T,
        conv[:4],
        conv[4],
        states[:4],
        states[4],
        conv[6],
        g_decay,
        g_bias,
        g_skip,
    )


def solution(mesh):
    split = Mesh(mesh.devices.reshape(SIZES), AX)
    everything = FSDP + TP
    return jax.shard_map(
        local,
        mesh=split,
        in_specs=(
            P(everything, None),
            P(),
            P(FSDP, None, TP),
            P(FSDP, TP),
            P(FSDP, None),
            P(TP, FSDP),
            P(None, TP),
            P(TP),
            P(),
            P(),
            P(TP),
            P(TP),
            P(TP),
            P(TP),
            P(everything, None),
        ),
        out_specs=(
            P(everything, None),
            P(everything, None),
            P(),
            P(FSDP, None, TP),
            P(FSDP, TP),
            P(FSDP, None),
            P(TP, FSDP),
            P(None, TP),
            P(TP),
            P(),
            P(),
            P(TP),
            P(TP),
            P(TP),
            P(TP),
        ),
        check_vma=False,
    )
```

```python
import functools
import itertools

import jax
import jax.numpy as jnp
import numpy as np
from jax import lax
from jax.experimental import pallas as pl
from jax.experimental.pallas import tpu as pltpu
from jax.sharding import Mesh
from jax.sharding import PartitionSpec as P

D = 1536
DI = 3072
N = 128
Q = 128
STEP = 256
ROWS = 768
CH = 768
HALF = 384
PAIRS = 6
LEFT = 1024
FULL = LEFT + HALF
EPS = 1e-05
NEG = -1e30

AX = ("zh", "y", "c", "zl", "x")
SIZES = (2, 4, 2, 2, 4)
FSDP = ("zh", "y", "c")
TP = ("zl", "x")

bf16 = jnp.bfloat16
f32 = jnp.float32


def moved(d, axis, k):
    d = dict(d)
    if axis == "z":
        z = (2 * d["zh"] + d["zl"] + k) % 4
        d["zh"], d["zl"] = divmod(z, 2)
    elif axis == "first":
        return moved(d, "y" if d["c"] == 0 else "z", k)
    elif axis == "second":
        return moved(d, "z" if d["c"] == 0 else "y", k)
    else:
        d[axis] = (d[axis] + k) % SIZES[AX.index(axis)]
    return d


def send(a, axis, k):
    pairs = []
    for place in itertools.product(*map(range, SIZES)):
        to = moved(dict(zip(AX, place)), axis, k)
        pairs.append(
            (
                int(np.ravel_multi_index(place, SIZES)),
                int(np.ravel_multi_index([to[n] for n in AX], SIZES)),
            )
        )
    return lax.ppermute(a, AX, pairs)


def spread(a, axis):
    return tuple(send(a, axis, k) for k in (1, 2, 3))


def deal(parts, axis):
    return (parts[0],) + tuple(send(parts[k], axis, k) for k in (1, 2, 3))


def add4(terms):
    a, b, c, d = (t.astype(f32) for t in terms)
    return (a + b) + (c + d)


def dot(a, b):
    return lax.dot_general(a, b, (((1,), (0,)), ((), ())), preferred_element_type=f32)


def dot_nt(a, b):
    return lax.dot_general(a, b, (((1,), (1,)), ((), ())), preferred_element_type=f32)


def dot_tn(a, b):
    return lax.dot_general(a, b, (((0,), (0,)), ((), ())), preferred_element_type=f32)


def halves(a):
    hi = a.astype(bf16)
    return hi, (a - hi.astype(f32)).astype(bf16)


def thirds(a):
    hi = a.astype(bf16)
    rest = a - hi.astype(f32)
    mid = rest.astype(bf16)
    return hi, mid, (rest - mid.astype(f32)).astype(bf16)


def tri_dot(tri, a):
    return dot(jnp.concatenate([tri] * 3, axis=1), jnp.concatenate(thirds(a), axis=0))


def lanes_of(a, i):
    return jnp.broadcast_to(a[:, i : i + 1], (Q, 128))


def iota(shape, dim):
    return lax.broadcasted_iota(jnp.int32, shape, dim)


def softplus(v):
    return jnp.maximum(v, 0.0) + jnp.log1p(jnp.exp(-jnp.abs(v)))


def here():
    return {n: lax.axis_index(n) for n in AX}


def row_copies(pieces, dst, sems):
    me = here()
    copies = []
    for k, ref in enumerate(pieces):
        x = lax.rem(me["x"] + 4 - k, 4)
        for g in range(3):
            at = lax.rem(3 * x + g + 4 + 4 * me["zl"], 12)
            copies.append((ref.at[pl.ds(64 * g, 64)], dst.at[pl.ds(pl.multiple_of(64 * at, 64), 64)]))
    return [pltpu.make_async_copy(s, d, sems.at[i]) for i, (s, d) in enumerate(copies)]


N_ROW_COPIES = 12


def weight_copies(pieces, column, width, dst, sems):
    me = here()
    copies = []
    for k, ref in enumerate(pieces):
        core = lax.rem(me["c"] + k // 4, 2)
        rb = -k % 4
        for kk in range(4):
            ra = -kk % 4
            y = lax.rem(me["y"] + jnp.where(core == 0, ra, rb), 4)
            z = lax.rem(2 * me["zh"] + me["zl"] + jnp.where(core == 0, rb, ra), 4)
            f = (z // 2 * 4 + y) * 2 + core
            copies.append(
                (
                    ref.at[pl.ds(96 * kk, 96), pl.ds(column, width)],
                    dst.at[
                        pl.ds(pl.multiple_of(96 * f, 96), 96),
                        pl.ds(pl.multiple_of(width * lax.rem(z, 2), 128), width),
                    ],
                    lax.rem(z, 2),
                )
            )
    return [pltpu.make_async_copy(s, d, sems.at[g]) for s, d, g in copies]


def wait_half(g, width, dst, sems):
    half = dst.at[:, pl.ds(g * width, width)]
    pltpu.make_async_copy(half, half, sems.at[g]).wait()


def line_kernel(a, b, c, d, *rest):
    for k, ref in enumerate((a, b, c, d)):
        rest[-1][96 * k : 96 * k + 96, :] = ref[...]


def norm_kernel(*refs):
    rows, (gain, feat, feat_t, raw, sem) = refs[:4], refs[4:]
    copies = row_copies(rows, raw, sem)
    for c in copies:
        c.start()
    for c in copies:
        c.wait()
    for k in range(ROWS // 128):
        at = slice(128 * k, 128 * k + 128)
        v = raw[at, :].astype(f32)
        r = lax.rsqrt(jnp.mean(v * v, axis=1, keepdims=True) + EPS)
        normed = v * r * gain[...]
        feat[at, :] = normed.astype(bf16)
        for m in range(D // 128):
            col = slice(128 * m, 128 * m + 128)
            feat_t[col, at] = normed[:, col].T.astype(bf16)


def param_kernel(small, far, prm, heads):
    at_0 = lax.axis_index("zl") == 0
    lo = jnp.where(at_0, small[...], far[...])
    hi = jnp.where(at_0, far[...], small[...])
    prm[:, :HALF] = lo
    prm[:, HALF:] = hi
    lane = iota((1, 128), 1)

    def twelve(k):
        col = slice(128 * k, 128 * k + 128)
        return jnp.where(lane < 6, lo[6:7, col], pltpu.roll(hi[6:7, col], 6, 1))

    heads[...] = jnp.zeros_like(heads)
    heads[0:1, :] = jnp.where(lane < 12, jnp.exp(twelve(0)), 0.0)
    heads[1:2, :] = jnp.where(lane < 12, twelve(1), 0.0)
    skip = twelve(2)
    for i in range(PAIRS):
        pair = [jnp.broadcast_to(skip[:, 2 * i + k : 2 * i + k + 1], (1, 128)) for k in range(2)]
        prm[6:7, 128 * i : 128 * i + 128] = jnp.where(lane < 64, pair[0], pair[1])


def touch_kernel(*refs):
    pass


def proj_kernel(*refs):
    weights, (feat, w_out, wo_out, pre, w, wo, wsem, wosem, osem) = refs[:8], refs[8:]
    i = pl.program_id(0)
    outs = [
        pltpu.make_async_copy(w, w_out, osem.at[0]),
        pltpu.make_async_copy(wo, wo_out, osem.at[1]),
    ]

    @pl.when(i == 0)
    def _():
        for c in weight_copies(weights, 0, LEFT, w, wsem):
            c.start()
        for c in weight_copies(weights, LEFT, HALF, wo, wosem):
            c.start()
        wait_half(0, LEFT, w, wsem)

    @pl.when(i == 2)
    def _():
        wait_half(1, LEFT, w, wsem)
        outs[0].start()

    @pl.when(i == 3)
    def _():
        for g in range(2):
            wait_half(g, HALF, wo, wosem)
        outs[1].start()

    pre[...] = dot(feat[...], w[:, pl.ds(pl.multiple_of(512 * i, 512), 512)])

    @pl.when(i == pl.num_programs(0) - 1)
    def _():
        for c in outs:
            c.wait()


def pair_places(i):
    g, p = divmod(i, 3)
    return slice(128 * i, 128 * i + 128), g * LEFT + HALF + 128 * p


def step_sizes(pre, heads):
    raw = pre[:, 896:1024] + pre[:, LEFT + 896 : LEFT + 1024] + heads[1:2, :]
    return raw, softplus(raw)


def framed_inputs(s, zl, pre, prev, msg, vx, vs):
    for g in range(2):
        base = g * LEFT + HALF
        vx[8:264, g * HALF : (g + 1) * HALF] = pre[:, base : base + HALF]
        vs[8:264, g * N : (g + 1) * N] = pre[:, base + HALF : base + HALF + N]
        if s == 0:
            vx[0:8, g * HALF : (g + 1) * HALF] = jnp.zeros((8, HALF), f32)
            vs[0:8, g * N : (g + 1) * N] = jnp.zeros((8, N), f32)
            continue
        hx, hs = prev[:, base : base + HALF], prev[:, base + HALF : base + HALF + N]
        if s == 1:
            hx, hs = jnp.where(zl == 1, hx, 0.0), jnp.where(zl == 1, hs, 0.0)
        else:
            mx = msg[128:144, g * HALF : (g + 1) * HALF].astype(f32)[:8]
            ms = msg[144:160, g * N : (g + 1) * N].astype(f32)[:8]
            hx, hs = jnp.where(zl == 0, hx, mx), jnp.where(zl == 0, hs, ms)
        vx[0:8, g * HALF : (g + 1) * HALF] = hx
        vs[0:8, g * N : (g + 1) * N] = hs


def fwd_kernel(s, *refs):
    refs = list(refs)
    pre = refs.pop(0)
    prev = refs.pop(0) if s else None
    h_in = refs.pop(0) if s else None
    msg = refs.pop(0) if s == 2 else None
    prm, prs, heads = refs[:3]
    refs = refs[3:]
    if s:
        refs.pop(0)
    act, hs = refs[:2]
    refs = refs[2:]
    out_msg = refs.pop(0) if s == 0 else None
    vx, vs = refs
    zl = lax.axis_index("zl")
    framed_inputs(s, zl, pre, prev, msg, vx, vs)
    if s == 0:
        hs[0] = jnp.zeros((N, CH), f32)
    elif s == 1:
        hs[0] = jnp.where(zl == 1, h_in[...].reshape(N, CH), 0.0)
    else:
        hs[0] = jnp.where(zl == 0, h_in[...].reshape(N, CH), msg[0:128, :].astype(f32))
    _, dt_all = step_sizes(pre, heads)
    a_all = -heads[0:1, :] * dt_all
    sub, lane = iota((Q, 128), 0), iota((Q, 128), 1)
    low_mask = sub >= lane
    tri = jnp.where(low_mask, 1.0, 0.0).astype(bf16)
    left = lane < 64
    for j in range(2):
        r0 = Q * j
        bc = []
        for g in range(2):
            col = slice(g * N, (g + 1) * N)
            cs = prs[4:5, col] + sum(
                prs[k : k + 1, col] * vs[5 + k + r0 : 5 + k + r0 + Q, col] for k in range(4)
            )
            act[r0 : r0 + Q, 2 * CH + g * N : 2 * CH + (g + 1) * N] = cs
            bc.append((cs * jax.nn.sigmoid(cs)).astype(bf16))
        b, c = bc
        bt = b.astype(f32).T.astype(bf16)
        scores = dot_nt(c, b)
        dt = dt_all[r0 : r0 + Q]
        cum = tri_dot(tri, a_all[r0 : r0 + Q])
        cum_t = cum.T
        for i in range(PAIRS):
            col, _ = pair_places(i)
            cx = prm[4:5, col] + sum(
                prm[k : k + 1, col] * vx[5 + k + r0 : 5 + k + r0 + Q, col] for k in range(4)
            )
            act[r0 : r0 + Q, CH + 128 * i : CH + 128 * i + 128] = cx
            x = (cx * jax.nn.sigmoid(cx)).astype(bf16).astype(f32)
            c0, c1 = lanes_of(cum, 2 * i), lanes_of(cum, 2 * i + 1)
            m0 = scores * jnp.exp(jnp.where(low_mask, c0 - cum_t[2 * i : 2 * i + 1, :], NEG))
            m1 = scores * jnp.exp(jnp.where(low_mask, c1 - cum_t[2 * i + 1 : 2 * i + 2, :], NEG))
            cp = jnp.where(left, c0, c1)
            xdt = x * jnp.where(left, lanes_of(dt, 2 * i), lanes_of(dt, 2 * i + 1))
            xdtb = xdt.astype(bf16)
            zero = jnp.zeros_like(xdtb)
            last = cp[Q - 1 : Q, :]
            inside = dot(
                jnp.concatenate([m0.astype(bf16), m1.astype(bf16)], axis=1),
                jnp.concatenate([jnp.where(left, xdtb, zero), jnp.where(left, zero, xdtb)], axis=0),
            )
            h = hs[j, :, col]
            y = inside + jnp.exp(cp) * dot(c, h.astype(bf16)) + prm[6:7, col] * x
            act[r0 : r0 + Q, col] = y
            hs[j + 1, :, col] = h * jnp.exp(last) + dot(bt, (xdt * jnp.exp(last - cp)).astype(bf16))
    if s == 0:
        out_msg[0:128, :] = hs[2].astype(bf16)
        out_msg[128:144, :] = jnp.concatenate([vx[256:264, :]] * 2, axis=0).astype(bf16)
        out_msg[144:160, :] = jnp.concatenate(
            [jnp.concatenate([vs[256:264, :]] * 2, axis=0), jnp.zeros((16, CH - 2 * N), f32)], axis=1
        ).astype(bf16)


def cot_kernel(*refs):
    rows, (w, z0, z1, ssd, prm, cot_out, gm, gb, sums, cot, rsem, osem) = refs[:4], refs[4:]
    i = pl.program_id(0)
    out = pltpu.make_async_copy(cot, cot_out, osem.at[0])

    @pl.when(i == 0)
    def _():
        cs = row_copies(rows, cot, rsem)
        for c in cs:
            c.start()
        for c in cs:
            c.wait()
        out.start()

    at = pl.ds(pl.multiple_of(STEP * i, STEP), STEP)
    grad = dot(cot[at, :], w[...])
    gm[...] = grad
    squares = jnp.zeros((STEP, 1), f32)
    dots = jnp.zeros((STEP, 1), f32)
    for g, z in ((0, z0), (1, z1)):
        col = slice(g * HALF, (g + 1) * HALF)
        gate = z[:, 0:HALF]
        gated = ssd[:, col] * (gate * jax.nn.sigmoid(gate))
        scaled = gated * prm[5:6, col]
        gb[:, col] = scaled.astype(bf16)
        squares = squares + jnp.sum(gated * gated, axis=1, keepdims=True)
        dots = dots + jnp.sum(grad[:, col] * scaled, axis=1, keepdims=True)
    lane = iota((STEP, 128), 1)
    both = jnp.where(lane == 0, squares, jnp.where(lane == 1, dots, 0.0))
    sums[...] = both.T[0:8, :]

    @pl.when(i == pl.num_programs(0) - 1)
    def _():
        out.wait()


def store_rows(i, value, outs):
    me = here()
    for g in range(4):
        natural = lax.rem(4 * i + g + 8 - 4 * me["zl"] + 12, 12)
        rel = lax.rem(natural // 3 - me["x"] + 4, 4)
        at = pl.ds(pl.multiple_of(64 * lax.rem(natural, 3), 64), 64)
        for k in range(4):

            @pl.when(rel == k)
            def _(k=k, g=g, at=at):
                outs[k][at, :] = value[64 * g : 64 * g + 64, :]


def out_kernel(gb, w, *outs):
    store_rows(pl.program_id(0), dot_nt(gb[...], w[...]).astype(bf16), outs)


def gate_kernel(s0, s1, s2, s3, gm, ssd, z0, z1, prm, *refs):
    dssd, lowz, mixed, ggain = refs[-4:]
    i = pl.program_id(0)
    total = (s0[...] + s1[...] + s2[...] + s3[...]).T
    inv = lax.rsqrt(total[:, 0:1] / DI + EPS)
    pull = inv * inv * inv * (total[:, 1:2] / DI)

    @pl.when(i == 0)
    def _():
        ggain[...] = jnp.zeros_like(ggain)

    for g, z in ((0, z0), (1, z1)):
        col = slice(g * HALF, (g + 1) * HALF)
        gate = z[:, 0:HALF]
        sig = jax.nn.sigmoid(gate)
        silu = gate * sig
        y = ssd[:, col]
        gated = y * silu
        grad = gm[:, col]
        gain = prm[5:6, col]
        normal = gated * inv
        mixed[:, col] = (normal * gain).astype(bf16)
        dg = grad * gain * inv - gated * pull
        dssd[:, col] = (dg * silu).astype(bf16)
        lowz[:, col] = (dg * y * (sig * (1.0 + gate * (1.0 - sig)))).astype(bf16)
        part = jnp.sum(grad * normal, axis=0, keepdims=True)
        ggain[:, col] += jnp.where(iota((8, HALF), 0) == 0, part, 0.0)


def tile_place(m, k, g):
    me = here()
    core = k % 2
    dy = lax.rem(lax.rem(2 * m + k // 2, 4) - me["y"] + 4, 4)
    dz = lax.rem(2 * (m // 2) + g - (2 * me["zh"] + me["zl"]) + 4, 4)
    return me["c"] == core, (4 * dz + dy if core == 0 else 4 * dy + dz)


def grad_block(part, base, places, buf, own, far, sem):
    m = pl.program_id(0)
    rows = pl.ds(pl.multiple_of(384 * m, 384), 384)
    buf[rows, base : base + part.shape[1]] = part.astype(bf16)
    for k in range(4):
        for col, g, to in places:
            here_too, at = tile_place(m, k, g)
            src = buf.at[pl.ds(pl.multiple_of(384 * m + 96 * k, 96), 96), pl.ds(base + col, HALF)]
            for flag, out in ((here_too, own), (jnp.logical_not(here_too), far)):
                dst = out.at[pl.ds(pl.multiple_of(96 * at, 96), 96), pl.ds(to, HALF)]

                @pl.when(flag)
                def _(dst=dst, src=src):
                    pltpu.make_async_copy(src, dst, sem.at[m]).start()


def row_gain(part, w):
    ones = jnp.ones((8, part.shape[1]), bf16)
    hi, lo = halves(part * w.astype(f32))
    return dot_nt(ones, hi) + dot_nt(ones, lo)


def wait_tiles(own, sem):
    for m in range(4):
        block = own.at[pl.ds(0, ROWS)]
        pltpu.make_async_copy(block, block, sem.at[m]).wait()


def early_kernel(feat_t, cot, lowz, mixed, w, own, far, gains, buf, sem):
    part = dot(feat_t[...], lowz[...])
    grad_block(part, 0, ((0, 0, 0), (HALF, 1, 0)), buf, own, far, sem)
    gains[...] = row_gain(part, jnp.concatenate([w[:, :HALF], w[:, LEFT : LEFT + HALF]], axis=1))
    part = dot_tn(cot[...], mixed[...])
    grad_block(part, CH, ((0, 0, HALF), (HALF, 1, HALF)), buf, own, far, sem)

    @pl.when(pl.program_id(0) == 3)
    def _():
        wait_tiles(own, sem)


def late_kernel(feat_t, low, w, gains_in, acc, accs, ggain, *refs):
    own, far, small, buf, gains, tail, sem, tail_sem = refs[-8:]
    m = pl.program_id(0)
    gain = gains_in[...]
    firsts = (((0, 0, 0),), ((0, 1, 0),), ((0, 0, HALF), (0, 1, HALF)))
    for k, places in enumerate(firsts):
        if k < 2:
            at = k * LEFT + HALF
            rhs, taps = low[:, at : at + HALF], w[:, at : at + HALF]
        else:
            rhs = jnp.concatenate([low[:, CH:LEFT], low[:, LEFT + CH : LEFT + CH + N]], axis=1)
            both = w[:, LEFT - N : LEFT].astype(f32) + w[:, 2 * LEFT - N :].astype(f32)
            taps = jnp.concatenate([w[:, CH : CH + N], both.astype(bf16), w[:, LEFT + CH : LEFT + CH + N]], axis=1)
        part = dot(feat_t[...], rhs)
        grad_block(part, k * HALF, places, buf, own, far, sem)
        gain = gain + row_gain(part, taps)
    gains[m] = gain

    @pl.when(m == 3)
    def _():
        small[...] = jnp.zeros_like(small)
        small[0:6, :] = acc[0:6, :]
        small[6:7, :] = ggain[0:1, :]
        small[8:9, :] = jnp.concatenate([gains[0, 0:1, :], gains[1, 0:1, :]], axis=1)
        small[9:10, :] = jnp.concatenate([gains[2, 0:1, :], gains[3, 0:1, :]], axis=1)
        for row, rs in ((7, (5, 6)), (10, (0, 1, 2)), (11, (3, 4))):
            for k, r in enumerate(rs):
                small[row : row + 1, 256 * k : 256 * k + 256] = accs[r : r + 1, :]
        tail[...] = split_small(small[...])
        copy = pltpu.make_async_copy(tail, far.at[pl.ds(2 * ROWS, 32)], tail_sem.at[0])
        copy.start()
        wait_tiles(own, sem)
        copy.wait()


def split_small(total):
    return jnp.concatenate(halves(total), axis=0)


def sum_small(block):
    return block[:16].astype(f32) + block[16:].astype(f32)


def core_sum_kernel(with_small, *refs):
    own, far = refs[:2]
    outs = refs[-4:]
    if with_small:
        small = split_small(refs[2][...] + sum_small(far[2 * ROWS : 2 * ROWS + 32, :]))
    for k, out in enumerate(outs):
        rows = slice(384 * k, 384 * k + 384)
        out[0:384, :] = (own[rows, :].astype(f32) + far[rows, :].astype(f32)).astype(bf16)
        if with_small:
            out[384:416, :] = small


def axis_sum_kernel(*refs):
    early, late, outs = refs[:4], refs[4:8], refs[-4:]
    small = split_small(sum(sum_small(t[384:416, :]) for t in late))
    for k, out in enumerate(outs):
        rows = slice(96 * k, 96 * k + 96)
        out[0:96, :] = add4([t[rows, :] for t in early]).astype(bf16)
        out[96:192, :] = add4([t[rows, :] for t in late]).astype(bf16)
        out[192:224, :] = small


def last_sum_kernel(*refs):
    terms, (early, tile, small, to_x) = refs[:4], refs[-4:]
    early[...] = add4([t[0:96, :] for t in terms])
    total = add4([t[96:192, :] for t in terms])
    tile[...] = total
    every = sum(sum_small(t[192:224, :]) for t in terms)
    small[...] = every
    for k in range(3):
        rows = slice(32 * k, 32 * k + 32)
        to_x[0:32, 256 * k : 256 * k + 128] = total[rows, HALF : HALF + N].astype(bf16)
        to_x[0:32, 256 * k + 128 : 256 * k + 256] = total[rows, HALF + 2 * N : HALF + 3 * N].astype(bf16)
    hi, lo = halves(every[8:16, :])
    to_x[32:48, :] = jnp.concatenate([hi.astype(f32), lo.astype(f32)], axis=0).astype(bf16)


def x_sum_kernel(a, b, c, d, state, small):
    total = add4([a[...], b[...], c[...], d[...]])
    for k in range(3):
        state[32 * k : 32 * k + 32, :] = total[0:32, 256 * k : 256 * k + 256]
    small[...] = total[32:40, :] + total[40:48, :]


def bwd_kernel(s, *refs):
    refs = list(refs)
    pre = refs.pop(0)
    prev = refs.pop(0) if s else None
    msg = refs.pop(0) if s == 2 else None
    act, hs, dssd, lowz, prm, prs, heads = refs[:7]
    refs = refs[7:]
    if s < 2:
        dh_in, tail, acc_in, accs_in = refs[:4]
        refs = refs[4:]
        back = refs.pop(0) if s == 0 else None
    refs = refs[len(refs) - (10 if s == 2 else 9) :]
    low, dh, head_rows, acc, accs = refs[:5]
    refs = refs[5:]
    for g in range(2):
        low[:, g * LEFT : g * LEFT + HALF] = lowz[:, g * HALF : (g + 1) * HALF]
    out_msg = refs.pop(0) if s == 2 else None
    vx, vs, dp, ds = refs
    zl = lax.axis_index("zl")
    framed_inputs(s, zl, pre, prev, msg, vx, vs)
    if s == 2:
        dh[...] = jnp.zeros_like(dh)
        dp[256:264, :] = jnp.zeros((8, CH), f32)
        ds[256:264, :] = jnp.zeros((8, 2 * N), f32)
        acc[...] = jnp.zeros_like(acc)
        accs[...] = jnp.zeros_like(accs)
    else:
        hd, hp, hq = dh_in[...], tail[0:8, :], tail[8:16, 0 : 2 * N]
        if s == 1:
            hd, hp, hq = (jnp.where(zl == 0, v, 0.0) for v in (hd, hp, hq))
        else:
            hd = jnp.where(zl == 1, hd, back[0:128, :].astype(f32))
            hp = jnp.where(zl == 1, hp, back[128:144, :].astype(f32)[:8])
            hq = jnp.where(zl == 1, hq, back[144:160, 0 : 2 * N].astype(f32)[:8])
        dh[...], dp[256:264, :], ds[256:264, :] = hd, hp, hq
        acc[...] = acc_in[...]
        accs[...] = accs_in[...]
    raw_all, dt_all = step_sizes(pre, heads)
    rate = heads[0:1, :]
    a_all = -rate * dt_all
    sub, lane = iota((Q, 128), 0), iota((Q, 128), 1)
    tri = jnp.where(sub >= lane, 1.0, 0.0).astype(bf16)
    up_mask = lane >= sub
    tri_up = jnp.where(up_mask, 1.0, 0.0).astype(bf16)
    below = jnp.where(lane < sub, 1.0, 0.0).astype(bf16)
    left = lane < 64
    for j in (1, 0):
        r0 = Q * j
        rows = slice(r0, r0 + Q)
        pre_s = [act[rows, 2 * CH + g * N : 2 * CH + (g + 1) * N] for g in range(2)]
        sig_s = [jax.nn.sigmoid(v) for v in pre_s]
        bf, cf = [(v * w).astype(bf16).astype(f32) for v, w in zip(pre_s, sig_s)]
        b, c = bf.astype(bf16), cf.astype(bf16)
        ct = cf.T.astype(bf16)
        scores_t = dot_nt(c, b).T
        dt, a = dt_all[rows], a_all[rows]
        cum = tri_dot(tri, a)
        cum_t = cum.T
        d_scores_t = jnp.zeros((Q, Q), f32)
        d_b = jnp.zeros((Q, N), f32)
        d_c = jnp.zeros((Q, N), f32)
        per_head = jnp.zeros((3 * Q, 128), f32)
        for i in range(PAIRS):
            col, _ = pair_places(i)
            cx = act[rows, CH + 128 * i : CH + 128 * i + 128]
            sig = jax.nn.sigmoid(cx)
            x = (cx * sig).astype(bf16).astype(f32)
            dyb = dssd[rows, col]
            dy = dyb.astype(f32)
            skip = prm[6:7, col]
            c0, c1 = lanes_of(cum, 2 * i), lanes_of(cum, 2 * i + 1)
            l0 = jnp.exp(jnp.where(up_mask, cum_t[2 * i : 2 * i + 1, :] - c0, NEG))
            l1 = jnp.exp(jnp.where(up_mask, cum_t[2 * i + 1 : 2 * i + 2, :] - c1, NEG))
            cp = jnp.where(left, c0, c1)
            dtp = jnp.where(left, lanes_of(dt, 2 * i), lanes_of(dt, 2 * i + 1))
            last = cp[Q - 1 : Q, :]
            fade = jnp.exp(last - cp)
            xdt = x * dtp
            xdtb = xdt.astype(bf16)
            zero = jnp.zeros_like(xdtb)
            dy_split = jnp.concatenate([jnp.where(left, dyb, zero), jnp.where(left, zero, dyb)], axis=0)
            x_split = jnp.concatenate([jnp.where(left, xdtb, zero), jnp.where(left, zero, xdtb)], axis=0)
            dhp = dh[:, col]
            dhb = dhp.astype(bf16)
            m_t = jnp.concatenate([(scores_t * l0).astype(bf16), (scores_t * l1).astype(bf16)], axis=1)
            inside = dot(m_t, dy_split)
            beyond = fade * dot(b, dhb)
            dxdt = inside + beyond
            dx = dxdt * dtp + skip * dy
            acc[5:6, col] += jnp.sum(dy * x, axis=0, keepdims=True)
            d_m_t = dot_nt(x_split, dyb)
            d_scores_t = d_scores_t + d_m_t[:Q] * l0 + d_m_t[Q:] * l1
            h = hs[j, :, col]
            crossing = jnp.sum(dhp * h, axis=0, keepdims=True) * jnp.exp(last)
            t1 = dxdt * x
            t2 = dy * (act[rows, col] - skip * x) - xdtb.astype(f32) * inside
            t2 = t2 + jnp.where(sub == Q - 1, crossing, 0.0)
            t3 = xdt * beyond
            pick = (lane == jnp.where(sub < 64, 2 * i, 2 * i + 1)).astype(f32).astype(bf16)
            hi, lo = halves(jnp.concatenate([t1, t2, t3], axis=0))
            per_head = per_head + dot(
                jnp.concatenate([hi, lo], axis=1), jnp.concatenate([pick, pick], axis=0)
            )
            dye = (dy * jnp.exp(cp)).astype(bf16)
            d_c = d_c + dot_nt(dye, h.astype(bf16))
            d_b = d_b + dot_nt((xdt * fade).astype(bf16), dhb)
            dh[:, col] = dhp * jnp.exp(last) + dot(ct, dye)
            dp[rows, col] = dx * (sig * (1.0 + cx * (1.0 - sig)))
        d_b = d_b + dot(d_scores_t.astype(bf16), c)
        d_c = d_c + dot(d_scores_t.T.astype(bf16), b)
        for g, grad in ((0, d_b), (1, d_c)):
            ds[rows, g * N : (g + 1) * N] = grad * (sig_s[g] * (1.0 + pre_s[g] * (1.0 - sig_s[g])))
        da = tri_dot(tri_up, per_head[Q : 2 * Q]) + tri_dot(below, per_head[2 * Q :])
        ddt = per_head[:Q] - rate * da
        dstep = ddt * jax.nn.sigmoid(raw_all[rows])
        accs[5:6, 0:128] += jnp.sum(a * da, axis=0, keepdims=True)
        accs[6:7, 0:128] += jnp.sum(dstep, axis=0, keepdims=True)
        for g in range(2):
            low[rows, (g + 1) * LEFT - N : (g + 1) * LEFT] = dstep.astype(bf16)
    for frame, grads, taps, out, width in ((vx, dp, prm, acc, CH), (vs, ds, prs, accs, 2 * N)):
        for i in range(width // 128):
            col = slice(128 * i, 128 * i + 128)
            g, p = divmod(i, width // 256)
            to = g * LEFT + HALF + 128 * p + (HALF if width == 2 * N else 0)
            back_v = sum(taps[k : k + 1, col] * grads[3 - k : 3 - k + STEP, col] for k in range(4))
            low[:, to : to + 128] = back_v.astype(bf16)
            own = grads[0:STEP, col]
            for k in range(4):
                out[k : k + 1, col] += jnp.sum(own * frame[5 + k : 5 + k + STEP, col], axis=0, keepdims=True)
            out[4:5, col] += jnp.sum(own, axis=0, keepdims=True)
    head_rows[0:8, :] = dp[0:8, :]
    head_rows[8:16, :] = jnp.concatenate([ds[0:8, :], jnp.zeros((8, CH - 2 * N), f32)], axis=1)
    if s == 2:
        out_msg[0:128, :] = dh[...].astype(bf16)
        out_msg[128:144, :] = jnp.concatenate([head_rows[0:8, :]] * 2, axis=0).astype(bf16)
        out_msg[144:160, :] = jnp.concatenate([head_rows[8:16, :]] * 2, axis=0).astype(bf16)


def feat_kernel(low, w, *refs):
    store_rows(pl.program_id(0), dot_nt(low[...], w[...]).astype(bf16), refs[-4:])


ANY = pl.BlockSpec(memory_space=pl.ANY)
VM = pl.BlockSpec(memory_space=pltpu.VMEM)


def params(mib):
    return pltpu.CompilerParams(vmem_limit_bytes=mib * 1024 * 1024)


def shape(*s, dtype=f32):
    return jax.ShapeDtypeStruct(s, dtype)


def cost(flops, moved_bytes):
    return pl.CostEstimate(flops=int(flops / 10), bytes_accessed=int(moved_bytes / 10), transcendentals=0)


ONCE = pl.Buffered(buffer_count=1)


def whole(*s):
    return pl.BlockSpec(s, lambda i: (0,) * len(s), pipeline_mode=ONCE)


def steps(width, column=0):
    return pl.BlockSpec((STEP, width), lambda i: (i, column))


def fixed(s, width, column=0):
    return pl.BlockSpec((STEP, width), lambda i: (s, column), pipeline_mode=ONCE)


def line_up(parts, deps):
    return pl.pallas_call(
        line_kernel,
        in_specs=[VM] * 4 + [ANY] * len(deps),
        out_specs=VM,
        out_shape=shape(384, FULL, dtype=bf16),
        compiler_params=params(4),
        cost_estimate=cost(1e6, 2e6),
        name="line_up",
    )(*parts, *deps)


def touch(a, deps):
    return pl.pallas_call(
        touch_kernel,
        in_specs=[ANY] * (1 + len(deps)),
        out_specs=ANY,
        out_shape=jax.ShapeDtypeStruct(a.shape, a.dtype),
        input_output_aliases={0: 0},
        compiler_params=params(1),
        cost_estimate=cost(1, 1),
        name="touch",
    )(a, *deps)


def normalize(rows, gain):
    return pl.pallas_call(
        norm_kernel,
        in_specs=[ANY] * 4 + [VM],
        out_specs=[VM, VM],
        out_shape=[shape(ROWS, D, dtype=bf16), shape(D, ROWS, dtype=bf16)],
        scratch_shapes=[pltpu.VMEM((ROWS, D), bf16), pltpu.SemaphoreType.DMA((N_ROW_COPIES,))],
        compiler_params=params(12),
        cost_estimate=cost(1e7, 5e6),
        name="normalize",
    )(*rows, gain)


def project(feat, weights):
    return pl.pallas_call(
        proj_kernel,
        grid=(4,),
        in_specs=[ANY] * 8 + [whole(ROWS, D)],
        out_specs=[ANY, ANY, pl.BlockSpec((ROWS, 512), lambda i: (0, i))],
        out_shape=[shape(D, 2 * LEFT, dtype=bf16), shape(D, CH, dtype=bf16), shape(ROWS, 2 * LEFT)],
        scratch_shapes=[
            pltpu.VMEM((D, 2 * LEFT), bf16),
            pltpu.VMEM((D, CH), bf16),
            pltpu.SemaphoreType.DMA((2,)),
            pltpu.SemaphoreType.DMA((2,)),
            pltpu.SemaphoreType.DMA((2,)),
        ],
        compiler_params=params(20),
        cost_estimate=cost(2 * ROWS * D * 2 * LEFT, 24e6),
        name="project",
    )(*weights, feat)


def prev_spec(s):
    return pl.BlockSpec((8, 2 * LEFT), lambda i: (32 * s - 1, 0))


def forward(s, pre, act, h, msg, prm, prs, heads):
    ins, specs = [pre], [fixed(s, 2 * LEFT)]
    if s:
        ins += [pre, h]
        specs += [prev_spec(s), pl.BlockSpec((1, N, CH), lambda i: (2, 0, 0))]
    if s == 2:
        ins += [msg]
        specs += [whole(160, CH)]
    ins += [prm, prs, heads]
    specs += [whole(8, CH), whole(8, 2 * N), whole(8, 128)]
    aliases = {}
    if s:
        aliases = {len(ins): 0}
        ins += [act]
        specs += [ANY]
    outs = [shape(ROWS, 2 * CH + 2 * N), shape(3, N, CH)]
    out_specs = [fixed(s, 2 * CH + 2 * N), whole(3, N, CH)]
    if s == 0:
        outs += [shape(160, CH, dtype=bf16)]
        out_specs += [whole(160, CH)]
    return pl.pallas_call(
        functools.partial(fwd_kernel, s),
        grid=(1,),
        in_specs=specs,
        out_specs=out_specs,
        out_shape=outs,
        input_output_aliases=aliases,
        scratch_shapes=[pltpu.VMEM((264, CH), f32), pltpu.VMEM((264, 2 * N), f32)],
        compiler_params=params(12),
        cost_estimate=cost(1.5e9, 6e6),
        name=f"scan_rows_{s}",
    )(*ins)


def cotangent(rows, w, pre, act, prm):
    return pl.pallas_call(
        cot_kernel,
        grid=(3,),
        in_specs=[ANY] * 4 + [whole(D, CH), steps(512, 0), steps(512, 2), steps(CH), whole(8, CH)],
        out_specs=[ANY, steps(CH), steps(CH), pl.BlockSpec((8, STEP), lambda i: (0, i))],
        out_shape=[
            shape(ROWS, D, dtype=bf16),
            shape(ROWS, CH),
            shape(ROWS, CH, dtype=bf16),
            shape(8, ROWS),
        ],
        scratch_shapes=[
            pltpu.VMEM((ROWS, D), bf16),
            pltpu.SemaphoreType.DMA((N_ROW_COPIES,)),
            pltpu.SemaphoreType.DMA((1,)),
        ],
        compiler_params=params(16),
        cost_estimate=cost(2 * ROWS * D * CH, 20e6),
        name="cotangent",
    )(*rows, w, pre, pre, act, prm)


def out_partial(gb, w):
    return pl.pallas_call(
        out_kernel,
        grid=(3,),
        in_specs=[steps(CH), whole(D, CH)],
        out_specs=[whole(192, D)] * 4,
        out_shape=[shape(192, D, dtype=bf16)] * 4,
        compiler_params=params(12),
        cost_estimate=cost(2 * ROWS * D * CH, 6e6),
        name="out_partial",
    )(gb, w)


def gate_back(sums, gm, act, pre, prm, deps):
    row = pl.BlockSpec((8, STEP), lambda i: (0, i))
    return pl.pallas_call(
        gate_kernel,
        grid=(3,),
        in_specs=[row] * 4
        + [steps(CH), steps(CH), steps(512, 0), steps(512, 2), whole(8, CH)]
        + [ANY] * len(deps),
        out_specs=[steps(CH), steps(CH), steps(CH), whole(8, CH)],
        out_shape=[shape(ROWS, CH, dtype=bf16)] * 3 + [shape(8, CH)],
        compiler_params=params(11),
        cost_estimate=cost(1e7, 12e6),
        name="gate_back",
    )(*sums, gm, act, pre, pre, prm, *deps)


def early_grads(feat_t, cot, lowz, mixed, w):
    return pl.pallas_call(
        early_kernel,
        grid=(4,),
        in_specs=[
            pl.BlockSpec((HALF, ROWS), lambda m: (m, 0)),
            pl.BlockSpec((ROWS, HALF), lambda m: (0, m)),
            whole(ROWS, CH),
            whole(ROWS, CH),
            pl.BlockSpec((HALF, 2 * LEFT), lambda m: (m, 0)),
        ],
        out_specs=[ANY, ANY, pl.BlockSpec((8, HALF), lambda m: (0, m))],
        out_shape=[shape(2 * ROWS, CH, dtype=bf16)] * 2 + [shape(8, D)],
        scratch_shapes=[pltpu.VMEM((D, 2 * CH), bf16), pltpu.SemaphoreType.DMA((4,))],
        compiler_params=params(18),
        cost_estimate=cost(2 * ROWS * D * 2 * CH, 12e6),
        name="early_grads",
    )(feat_t, cot, lowz, mixed, w)


def late_grads(feat_t, low, w, gains, acc, accs, ggain, deps):
    return pl.pallas_call(
        late_kernel,
        grid=(4,),
        in_specs=[
            pl.BlockSpec((HALF, ROWS), lambda m: (m, 0)),
            whole(ROWS, 2 * LEFT),
            pl.BlockSpec((HALF, 2 * LEFT), lambda m: (m, 0)),
            pl.BlockSpec((8, HALF), lambda m: (0, m)),
            whole(8, CH),
            whole(8, 2 * N),
            whole(8, CH),
        ]
        + [ANY] * len(deps),
        out_specs=[ANY, ANY, whole(16, CH)],
        out_shape=[shape(2 * ROWS, CH, dtype=bf16), shape(2 * ROWS + 32, CH, dtype=bf16), shape(16, CH)],
        scratch_shapes=[
            pltpu.VMEM((D, 3 * HALF), bf16),
            pltpu.VMEM((4, 8, HALF), f32),
            pltpu.VMEM((32, CH), bf16),
            pltpu.SemaphoreType.DMA((4,)),
            pltpu.SemaphoreType.DMA((1,)),
        ],
        compiler_params=params(18),
        cost_estimate=cost(2 * ROWS * D * 3 * HALF, 12e6),
        name="late_grads",
    )(feat_t, low, w, gains, acc, accs, ggain, *deps)


def tile_sums(kernel, ins, outs, deps, name):
    return pl.pallas_call(
        kernel,
        in_specs=[VM] * len(ins) + [ANY] * len(deps),
        out_specs=[VM] * len(outs),
        out_shape=outs,
        compiler_params=params(14),
        cost_estimate=cost(1e6, 4e6),
        name=name,
    )(*ins, *deps)


def core_sum(own, far, small, deps, name):
    ins = [own, far] + list(small)
    rows = 416 if small else 384
    kernel = functools.partial(core_sum_kernel, bool(small))
    return tile_sums(kernel, ins, [shape(rows, CH, dtype=bf16)] * 4, deps, name)


def backward(s, pre, msg, act, hs, dssd, lowz, prm, prs, heads, carried, back, low, deps):
    ins, specs = [pre], [fixed(s, 2 * LEFT)]
    if s:
        ins += [pre]
        specs += [prev_spec(s)]
    if s == 2:
        ins += [msg]
        specs += [whole(160, CH)]
    ins += [act, hs, dssd, lowz, prm, prs, heads]
    specs += [fixed(s, 2 * CH + 2 * N), whole(3, N, CH), fixed(s, CH), fixed(s, CH)]
    specs += [whole(8, CH), whole(8, 2 * N), whole(8, 128)]
    aliases = {}
    if s < 2:
        ins += list(carried)
        specs += [whole(N, CH), whole(16, CH), whole(8, CH), whole(8, 2 * N)]
        if s == 0:
            ins += [back]
            specs += [whole(160, CH)]
        aliases = {len(ins): 0}
        ins += [low]
        specs += [ANY]
    ins += list(deps)
    specs += [ANY] * len(deps)
    outs = [shape(ROWS, 2 * LEFT, dtype=bf16), shape(N, CH), shape(16, CH), shape(8, CH), shape(8, 2 * N)]
    out_specs = [fixed(s, 2 * LEFT), whole(N, CH), whole(16, CH), whole(8, CH), whole(8, 2 * N)]
    if s == 2:
        outs += [shape(160, CH, dtype=bf16)]
        out_specs += [whole(160, CH)]
    return pl.pallas_call(
        functools.partial(bwd_kernel, s),
        grid=(1,),
        in_specs=specs,
        out_specs=out_specs,
        out_shape=outs,
        input_output_aliases=aliases,
        scratch_shapes=[
            pltpu.VMEM((264, CH), f32),
            pltpu.VMEM((264, 2 * N), f32),
            pltpu.VMEM((264, CH), f32),
            pltpu.VMEM((264, 2 * N), f32),
        ],
        compiler_params=params(16),
        cost_estimate=cost(4e9, 8e6),
        name=f"scan_back_{s}",
    )(*ins)


def feat_partial(low, w, deps):
    return pl.pallas_call(
        feat_kernel,
        grid=(3,),
        in_specs=[steps(2 * LEFT), whole(D, 2 * LEFT)] + [ANY] * len(deps),
        out_specs=[whole(192, D)] * 4,
        out_shape=[shape(192, D, dtype=bf16)] * 4,
        compiler_params=params(18),
        cost_estimate=cost(2 * ROWS * D * 2 * LEFT, 16e6),
        name="feat_partial",
    )(low, w, *deps)


def local(
    layer_input,
    input_gain,
    proj_inner,
    proj_step,
    proj_state,
    proj_output,
    conv_inner,
    conv_inner_bias,
    conv_state,
    conv_state_bias,
    inner_gain,
    decay_log,
    step_bias,
    skip_gain,
    out_cotangent,
):
    zl = lax.axis_index("zl")
    coef = jnp.pad(jnp.stack([decay_log, step_bias, skip_gain]), ((0, 0), (0, 122))).reshape(1, HALF)
    small = jnp.concatenate(
        [conv_inner, conv_inner_bias[None], inner_gain[None], coef, jnp.zeros((1, HALF), f32)], axis=0
    )
    prm, heads = pl.pallas_call(
        param_kernel,
        in_specs=[VM, VM],
        out_specs=[VM, VM],
        out_shape=[shape(8, CH), shape(8, 128)],
        compiler_params=params(1),
        cost_estimate=cost(1, 1),
        name="parameters",
    )(small, send(small, "zl", 1))
    prs = jnp.concatenate([conv_state, conv_state_bias[None], jnp.zeros((3, 2 * N), f32)], axis=0)

    step_cols = jnp.where(
        zl == 0, jnp.pad(proj_step, ((0, 0), (0, 122))), jnp.pad(proj_step, ((0, 0), (6, 116)))
    )
    state_cols = jnp.where(zl == 0, proj_state[:, :N], proj_state[:, N:])
    shard = jnp.concatenate(
        [proj_inner[:, 0], proj_inner[:, 1], state_cols, step_cols, proj_output.T], axis=1
    )
    rows = (layer_input,) + spread(layer_input, "x")
    line = line_up((shard,) + spread(shard, "first"), (rows[1], rows[3]))
    far = spread(line, "second")
    first = touch(far[0], (rows[2], prm, heads, prs))
    feat, feat_t = normalize(rows, input_gain[None])
    third = touch(far[2], (feat,))
    mine = (line, first, far[1], third)
    weights = mine + tuple(send(a, "c", 1) for a in mine)
    w_in, w_o, pre = project(feat, weights)
    cot_rows = (out_cotangent,) + spread(out_cotangent, "x")

    act, hs0, msg = forward(0, pre, None, None, None, prm, prs, heads)
    msg = send(msg, "zl", 1)
    act, hs1 = forward(1, pre, act, hs0, None, prm, prs, heads)
    act, hs2 = forward(2, pre, act, hs1, msg, prm, prs, heads)
    cot, gm, gb, sums = cotangent(cot_rows, w_o, pre, act, prm)
    all_sums = (sums,) + spread(sums, "x")
    parts = out_partial(gb, w_o)
    out_terms = deal(parts, "x")
    dssd, lowz, mixed, ggain = gate_back(all_sums, gm, act, pre, prm, (parts[0],))

    own, far, gains = early_grads(feat_t, cot, lowz, mixed, w_in)
    far = send(far, "c", 1)
    scan = (prm, prs, heads)
    low, *carried, back = backward(2, pre, msg, act, hs2, dssd, lowz, *scan, None, None, None, (own,))
    back = send(back, "zl", 1)
    parts = core_sum(own, far, (), (low,), "early_core_sum")
    terms = deal(parts, "second")
    low, *carried = backward(1, pre, None, act, hs1, dssd, lowz, *scan, carried, None, low, (parts[0],))
    low, _, _, acc, accs = backward(0, pre, None, act, hs0, dssd, lowz, *scan, carried, back, low, ())

    own, far, small = late_grads(feat_t, low, w_in, gains, acc, accs, ggain, terms[1:] + out_terms[1:])
    far = send(far, "c", 1)
    feat_parts = feat_partial(low, w_in, (own,))
    feat_terms = deal(feat_parts, "x")
    parts = core_sum(own, far, (small,), (feat_parts[0],), "late_core_sum")
    late_terms = deal(parts, "second")
    parts = tile_sums(
        axis_sum_kernel, terms + late_terms, [shape(224, CH, dtype=bf16)] * 4, (), "axis_sum"
    )
    early, late, small, to_x = tile_sums(
        last_sum_kernel,
        deal(parts, "first"),
        [shape(96, CH), shape(96, CH), shape(16, CH), shape(48, CH, dtype=bf16)],
        (),
        "last_sum",
    )
    g_state, by_x = tile_sums(
        x_sum_kernel, (to_x,) + spread(to_x, "x"), [shape(96, 2 * N), shape(8, CH)], (), "x_sum"
    )

    own = lambda a: jnp.where(zl == 0, a[..., :HALF], a[..., HALF:])
    six = lambda a: jnp.where(zl == 0, a[:6], a[6:12])
    conv = own(small[:7])
    g_skip = six(small[5].reshape(12, 64).sum(axis=1))
    g_decay, g_bias = six(small[7, :128]), six(small[7, 256:384])
    states = by_x[2:4].reshape(6, 2 * N)
    g_input_gain = by_x[0:2].reshape(D) / input_gain
    g_step = jnp.where(zl == 0, late[:, 512:518], late[:, 518:524])

    values = layer_input.astype(f32)
    squares = all_sums[0][0] + all_sums[1][0] + all_sums[2][0] + all_sums[3][0]
    at = lax.rem(192 * lax.axis_index("x") + 256 + 256 * zl, ROWS)
    squares = lax.dynamic_slice_in_dim(jnp.concatenate([squares, squares]), at, 192)
    scale = lax.rsqrt(squares / DI + EPS)[:, None]
    layer_output = (values + add4(out_terms) * scale).astype(bf16)
    inv = lax.rsqrt(jnp.mean(values * values, axis=1, keepdims=True) + EPS)
    weighted = add4(feat_terms) * input_gain
    input_grad = (
        out_cotangent.astype(f32)
        + weighted * inv
        - values * (inv * inv * inv) * jnp.mean(weighted * values, axis=1, keepdims=True)
    )
    return (
        layer_output,
        input_grad,
        g_input_gain,
        jnp.stack([early[:, :HALF], late[:, :HALF]], axis=1),
        g_step,
        g_state,
        early[:, HALF:].T,
        conv[:4],
        conv[4],
        states[:4],
        states[4],
        conv[6],
        g_decay,
        g_bias,
        g_skip,
    )


def solution(mesh):
    split = Mesh(mesh.devices.reshape(SIZES), AX)
    everything = FSDP + TP
    return jax.shard_map(
        local,
        mesh=split,
        in_specs=(
            P(everything, None),
            P(),
            P(FSDP, None, TP),
            P(FSDP, TP),
            P(FSDP, None),
            P(TP, FSDP),
            P(None, TP),
            P(TP),
            P(),
            P(),
            P(TP),
            P(TP),
            P(TP),
            P(TP),
            P(everything, None),
        ),
        out_specs=(
            P(everything, None),
            P(everything, None),
            P(),
            P(FSDP, None, TP),
            P(FSDP, TP),
            P(FSDP, None),
            P(TP, FSDP),
            P(None, TP),
            P(TP),
            P(),
            P(),
            P(TP),
            P(TP),
            P(TP),
            P(TP),
        ),
        check_vma=False,
    )
```

```python
import functools
import itertools

import jax
import jax.numpy as jnp
import numpy as np
from jax import lax
from jax.experimental import pallas as pl
from jax.experimental.pallas import tpu as pltpu
from jax.sharding import Mesh
from jax.sharding import PartitionSpec as P

D = 1536
DI = 3072
N = 128
Q = 128
STEP = 256
ROWS = 768
CH = 768
HALF = 384
PAIRS = 6
LEFT = 1024
FULL = LEFT + HALF
EPS = 1e-05
NEG = -1e30

AX = ("zh", "y", "c", "zl", "x")
SIZES = (2, 4, 2, 2, 4)
FSDP = ("zh", "y", "c")
TP = ("zl", "x")

bf16 = jnp.bfloat16
f32 = jnp.float32


def moved(d, axis, k):
    d = dict(d)
    if axis == "z":
        z = (2 * d["zh"] + d["zl"] + k) % 4
        d["zh"], d["zl"] = divmod(z, 2)
    elif axis == "first":
        return moved(d, "y" if d["c"] == 0 else "z", k)
    elif axis == "second":
        return moved(d, "z" if d["c"] == 0 else "y", k)
    else:
        d[axis] = (d[axis] + k) % SIZES[AX.index(axis)]
    return d


def send(a, axis, k):
    pairs = []
    for place in itertools.product(*map(range, SIZES)):
        to = moved(dict(zip(AX, place)), axis, k)
        pairs.append(
            (
                int(np.ravel_multi_index(place, SIZES)),
                int(np.ravel_multi_index([to[n] for n in AX], SIZES)),
            )
        )
    return lax.ppermute(a, AX, pairs)


def spread(a, axis):
    return tuple(send(a, axis, k) for k in (1, 2, 3))


def deal(parts, axis):
    return (parts[0],) + tuple(send(parts[k], axis, k) for k in (1, 2, 3))


def ring(parts, axis, middle, deps=()):
    own, up, down, one, two = parts
    one, two = send(one, axis, 1), send(two, axis, 3)
    up, down, *more = middle((up, down, one, two), deps)
    return (own, send(up, axis, 1), send(down, axis, 3)), (up, *more)


def add3(terms):
    a, b, c = (t.astype(f32) for t in terms)
    return a + (b + c)


def add4(terms):
    a, b, c, d = (t.astype(f32) for t in terms)
    return (a + b) + (c + d)


def dot(a, b):
    return lax.dot_general(a, b, (((1,), (0,)), ((), ())), preferred_element_type=f32)


def dot_nt(a, b):
    return lax.dot_general(a, b, (((1,), (1,)), ((), ())), preferred_element_type=f32)


def dot_tn(a, b):
    return lax.dot_general(a, b, (((0,), (0,)), ((), ())), preferred_element_type=f32)


def halves(a):
    hi = a.astype(bf16)
    return hi, (a - hi.astype(f32)).astype(bf16)


def thirds(a):
    hi = a.astype(bf16)
    rest = a - hi.astype(f32)
    mid = rest.astype(bf16)
    return hi, mid, (rest - mid.astype(f32)).astype(bf16)


def tri_dot(tri, a):
    return dot(jnp.concatenate([tri] * 3, axis=1), jnp.concatenate(thirds(a), axis=0))


def lanes_of(a, i):
    return jnp.broadcast_to(a[:, i : i + 1], (Q, 128))


def iota(shape, dim):
    return lax.broadcasted_iota(jnp.int32, shape, dim)


def softplus(v):
    return jnp.maximum(v, 0.0) + jnp.log1p(jnp.exp(-jnp.abs(v)))


def here():
    return {n: lax.axis_index(n) for n in AX}


def row_copies(pieces, dst, sems):
    me = here()
    places = ((0, 0, D), (1, 0, D), (2, 0, D), (3, 0, D))
    if len(pieces) == 5:
        places = ((0, 0, D), (1, 0, D), (3, 0, D), (2, 0, CH), (2, CH, CH))
    copies = []
    for ref, (k, col, width) in zip(pieces, places):
        x = lax.rem(me["x"] + 4 - k, 4)
        for g in range(3):
            at = lax.rem(3 * x + g + 4 + 4 * me["zl"], 12)
            to = dst.at[pl.ds(pl.multiple_of(64 * at, 64), 64), pl.ds(col, width)]
            copies.append((ref.at[pl.ds(64 * g, 64)], to))
    return [pltpu.make_async_copy(s, d, sems.at[i]) for i, (s, d) in enumerate(copies)]


N_ROW_COPIES = 15


def weight_copies(pieces, column, width, dst, sems):
    me = here()
    copies = []
    for k, ref in enumerate(pieces):
        core = lax.rem(me["c"] + k // 4, 2)
        rb = -k % 4
        for kk in range(4):
            ra = -kk % 4
            y = lax.rem(me["y"] + jnp.where(core == 0, ra, rb), 4)
            z = lax.rem(2 * me["zh"] + me["zl"] + jnp.where(core == 0, rb, ra), 4)
            f = (z // 2 * 4 + y) * 2 + core
            copies.append(
                (
                    ref.at[pl.ds(96 * kk, 96), pl.ds(column, width)],
                    dst.at[
                        pl.ds(pl.multiple_of(96 * f, 96), 96),
                        pl.ds(pl.multiple_of(width * lax.rem(z, 2), 128), width),
                    ],
                    lax.rem(z, 2),
                )
            )
    return [pltpu.make_async_copy(s, d, sems.at[g]) for s, d, g in copies]


def wait_half(g, width, dst, sems):
    half = dst.at[:, pl.ds(g * width, width)]
    pltpu.make_async_copy(half, half, sems.at[g]).wait()


def line_kernel(a, b, c, d, *rest):
    for k, ref in enumerate((a, b, c, d)):
        rest[-1][96 * k : 96 * k + 96, :] = ref[...]


def norm_kernel(*refs):
    rows, (gain, feat, feat_t, raw, sem) = refs[:4], refs[4:]
    copies = row_copies(rows, raw, sem)
    for c in copies:
        c.start()
    for c in copies:
        c.wait()
    for k in range(ROWS // 128):
        at = slice(128 * k, 128 * k + 128)
        v = raw[at, :].astype(f32)
        r = lax.rsqrt(jnp.mean(v * v, axis=1, keepdims=True) + EPS)
        normed = v * r * gain[...]
        feat[at, :] = normed.astype(bf16)
        for m in range(D // 128):
            col = slice(128 * m, 128 * m + 128)
            feat_t[col, at] = normed[:, col].T.astype(bf16)


def param_kernel(small, far, prm, heads):
    at_0 = lax.axis_index("zl") == 0
    lo = jnp.where(at_0, small[...], far[...])
    hi = jnp.where(at_0, far[...], small[...])
    prm[:, :HALF] = lo
    prm[:, HALF:] = hi
    lane = iota((1, 128), 1)

    def twelve(k):
        col = slice(128 * k, 128 * k + 128)
        return jnp.where(lane < 6, lo[6:7, col], pltpu.roll(hi[6:7, col], 6, 1))

    heads[...] = jnp.zeros_like(heads)
    heads[0:1, :] = jnp.where(lane < 12, jnp.exp(twelve(0)), 0.0)
    heads[1:2, :] = jnp.where(lane < 12, twelve(1), 0.0)
    skip = twelve(2)
    for i in range(PAIRS):
        pair = [jnp.broadcast_to(skip[:, 2 * i + k : 2 * i + k + 1], (1, 128)) for k in range(2)]
        prm[6:7, 128 * i : 128 * i + 128] = jnp.where(lane < 64, pair[0], pair[1])


def touch_kernel(*refs):
    pass


def proj_kernel(*refs):
    weights, (feat, w_out, wo_out, pre, w, wo, wsem, wosem, osem) = refs[:8], refs[8:]
    i = pl.program_id(0)
    outs = [
        pltpu.make_async_copy(w, w_out, osem.at[0]),
        pltpu.make_async_copy(wo, wo_out, osem.at[1]),
    ]

    @pl.when(i == 0)
    def _():
        for c in weight_copies(weights, 0, LEFT, w, wsem):
            c.start()
        for c in weight_copies(weights, LEFT, HALF, wo, wosem):
            c.start()
        wait_half(0, LEFT, w, wsem)

    @pl.when(i == 2)
    def _():
        wait_half(1, LEFT, w, wsem)
        outs[0].start()

    @pl.when(i == 3)
    def _():
        for g in range(2):
            wait_half(g, HALF, wo, wosem)
        outs[1].start()

    pre[...] = dot(feat[...], w[:, pl.ds(pl.multiple_of(512 * i, 512), 512)])

    @pl.when(i == pl.num_programs(0) - 1)
    def _():
        for c in outs:
            c.wait()


def pair_places(i):
    g, p = divmod(i, 3)
    return slice(128 * i, 128 * i + 128), g * LEFT + HALF + 128 * p


def step_sizes(pre, heads):
    raw = pre[:, 896:1024] + pre[:, LEFT + 896 : LEFT + 1024] + heads[1:2, :]
    return raw, softplus(raw)


def framed_inputs(s, zl, pre, prev, msg, vx, vs):
    for g in range(2):
        base = g * LEFT + HALF
        vx[8:264, g * HALF : (g + 1) * HALF] = pre[:, base : base + HALF]
        vs[8:264, g * N : (g + 1) * N] = pre[:, base + HALF : base + HALF + N]
        if s == 0:
            vx[0:8, g * HALF : (g + 1) * HALF] = jnp.zeros((8, HALF), f32)
            vs[0:8, g * N : (g + 1) * N] = jnp.zeros((8, N), f32)
            continue
        hx, hs = prev[:, base : base + HALF], prev[:, base + HALF : base + HALF + N]
        if s == 1:
            hx, hs = jnp.where(zl == 1, hx, 0.0), jnp.where(zl == 1, hs, 0.0)
        else:
            mx = msg[128:144, g * HALF : (g + 1) * HALF].astype(f32)[:8]
            ms = msg[144:160, g * N : (g + 1) * N].astype(f32)[:8]
            hx, hs = jnp.where(zl == 0, hx, mx), jnp.where(zl == 0, hs, ms)
        vx[0:8, g * HALF : (g + 1) * HALF] = hx
        vs[0:8, g * N : (g + 1) * N] = hs


def fwd_kernel(s, *refs):
    refs = list(refs)
    pre = refs.pop(0)
    prev = refs.pop(0) if s else None
    h_in = refs.pop(0) if s else None
    msg = refs.pop(0) if s == 2 else None
    prm, prs, heads = refs[:3]
    refs = refs[3:]
    refs = refs[len(refs) - (5 if s == 0 else 4) :]
    act, hs = refs[:2]
    refs = refs[2:]
    out_msg = refs.pop(0) if s == 0 else None
    vx, vs = refs
    zl = lax.axis_index("zl")
    framed_inputs(s, zl, pre, prev, msg, vx, vs)
    if s == 0:
        hs[0] = jnp.zeros((N, CH), f32)
    elif s == 1:
        hs[0] = jnp.where(zl == 1, h_in[...].reshape(N, CH), 0.0)
    else:
        hs[0] = jnp.where(zl == 0, h_in[...].reshape(N, CH), msg[0:128, :].astype(f32))
    _, dt_all = step_sizes(pre, heads)
    a_all = -heads[0:1, :] * dt_all
    sub, lane = iota((Q, 128), 0), iota((Q, 128), 1)
    low_mask = sub >= lane
    tri = jnp.where(low_mask, 1.0, 0.0).astype(bf16)
    left = lane < 64
    for j in range(2):
        r0 = Q * j
        bc = []
        for g in range(2):
            col = slice(g * N, (g + 1) * N)
            cs = prs[4:5, col] + sum(
                prs[k : k + 1, col] * vs[5 + k + r0 : 5 + k + r0 + Q, col] for k in range(4)
            )
            act[r0 : r0 + Q, 2 * CH + g * N : 2 * CH + (g + 1) * N] = cs
            bc.append((cs * jax.nn.sigmoid(cs)).astype(bf16))
        b, c = bc
        bt = b.astype(f32).T.astype(bf16)
        scores = dot_nt(c, b)
        dt = dt_all[r0 : r0 + Q]
        cum = tri_dot(tri, a_all[r0 : r0 + Q])
        cum_t = cum.T
        for i in range(PAIRS):
            col, _ = pair_places(i)
            cx = prm[4:5, col] + sum(
                prm[k : k + 1, col] * vx[5 + k + r0 : 5 + k + r0 + Q, col] for k in range(4)
            )
            act[r0 : r0 + Q, CH + 128 * i : CH + 128 * i + 128] = cx
            x = (cx * jax.nn.sigmoid(cx)).astype(bf16).astype(f32)
            c0, c1 = lanes_of(cum, 2 * i), lanes_of(cum, 2 * i + 1)
            m0 = scores * jnp.exp(jnp.where(low_mask, c0 - cum_t[2 * i : 2 * i + 1, :], NEG))
            m1 = scores * jnp.exp(jnp.where(low_mask, c1 - cum_t[2 * i + 1 : 2 * i + 2, :], NEG))
            cp = jnp.where(left, c0, c1)
            xdt = x * jnp.where(left, lanes_of(dt, 2 * i), lanes_of(dt, 2 * i + 1))
            xdtb = xdt.astype(bf16)
            zero = jnp.zeros_like(xdtb)
            last = cp[Q - 1 : Q, :]
            inside = dot(
                jnp.concatenate([m0.astype(bf16), m1.astype(bf16)], axis=1),
                jnp.concatenate([jnp.where(left, xdtb, zero), jnp.where(left, zero, xdtb)], axis=0),
            )
            h = hs[j, :, col]
            y = inside + jnp.exp(cp) * dot(c, h.astype(bf16)) + prm[6:7, col] * x
            act[r0 : r0 + Q, col] = y
            hs[j + 1, :, col] = h * jnp.exp(last) + dot(bt, (xdt * jnp.exp(last - cp)).astype(bf16))
    if s == 0:
        out_msg[0:128, :] = hs[2].astype(bf16)
        out_msg[128:144, :] = jnp.concatenate([vx[256:264, :]] * 2, axis=0).astype(bf16)
        out_msg[144:160, :] = jnp.concatenate(
            [jnp.concatenate([vs[256:264, :]] * 2, axis=0), jnp.zeros((16, CH - 2 * N), f32)], axis=1
        ).astype(bf16)


def cot_kernel(*refs):
    rows, (w, z0, z1, ssd, prm, cot_out, gm, gb, sums, cot, rsem, osem) = refs[:5], refs[5:]
    i = pl.program_id(0)
    out = pltpu.make_async_copy(cot, cot_out, osem.at[0])

    @pl.when(i == 0)
    def _():
        cs = row_copies(rows, cot, rsem)
        for c in cs:
            c.start()
        for c in cs:
            c.wait()
        out.start()

    at = pl.ds(pl.multiple_of(STEP * i, STEP), STEP)
    grad = dot(cot[at, :], w[...])
    gm[...] = grad
    squares = jnp.zeros((STEP, 1), f32)
    dots = jnp.zeros((STEP, 1), f32)
    for g, z in ((0, z0), (1, z1)):
        col = slice(g * HALF, (g + 1) * HALF)
        gate = z[:, 0:HALF]
        gated = ssd[:, col] * (gate * jax.nn.sigmoid(gate))
        scaled = gated * prm[5:6, col]
        gb[:, col] = scaled.astype(bf16)
        squares = squares + jnp.sum(gated * gated, axis=1, keepdims=True)
        dots = dots + jnp.sum(grad[:, col] * scaled, axis=1, keepdims=True)
    lane = iota((STEP, 128), 1)
    both = jnp.where(lane == 0, squares, jnp.where(lane == 1, dots, 0.0))
    sums[...] = both.T[0:8, :]

    @pl.when(i == pl.num_programs(0) - 1)
    def _():
        out.wait()


def store_rows(i, value, outs):
    own, up, down, one, two = outs
    me = here()
    for g in range(4):
        natural = lax.rem(4 * i + g + 8 - 4 * me["zl"] + 12, 12)
        rel = lax.rem(natural // 3 - me["x"] + 4, 4)
        at = pl.ds(pl.multiple_of(64 * lax.rem(natural, 3), 64), 64)
        rows = slice(64 * g, 64 * g + 64)
        for k, out in ((0, own), (1, up), (3, down)):

            @pl.when(rel == k)
            def _(out=out, rows=rows, at=at):
                out[at, :] = value[rows, :]

        @pl.when(rel == 2)
        def _(rows=rows, at=at):
            one[at, :] = value[rows, :CH]
            two[at, :] = value[rows, CH:]


def add(a, b):
    return (a.astype(f32) + b.astype(f32)).astype(bf16)


def row_middle_kernel(up, down, one, two, *refs):
    up_out, down_out = refs[-2:]
    up_out[:, :CH] = add(up[:, :CH], one[...])
    up_out[:, CH:] = up[:, CH:]
    down_out[:, :CH] = down[:, :CH]
    down_out[:, CH:] = add(down[:, CH:], two[...])


def out_kernel(gb, w, *outs):
    store_rows(pl.program_id(0), dot_nt(gb[...], w[...]).astype(bf16), outs)


def gate_kernel(s0, s1, s2, s3, gm, ssd, z0, z1, prm, *refs):
    dssd, lowz, mixed, ggain = refs[-4:]
    i = pl.program_id(0)
    total = (s0[...] + s1[...] + s2[...] + s3[...]).T
    inv = lax.rsqrt(total[:, 0:1] / DI + EPS)
    pull = inv * inv * inv * (total[:, 1:2] / DI)

    @pl.when(i == 0)
    def _():
        ggain[...] = jnp.zeros_like(ggain)

    for g, z in ((0, z0), (1, z1)):
        col = slice(g * HALF, (g + 1) * HALF)
        gate = z[:, 0:HALF]
        sig = jax.nn.sigmoid(gate)
        silu = gate * sig
        y = ssd[:, col]
        gated = y * silu
        grad = gm[:, col]
        gain = prm[5:6, col]
        normal = gated * inv
        mixed[:, col] = (normal * gain).astype(bf16)
        dg = grad * gain * inv - gated * pull
        dssd[:, col] = (dg * silu).astype(bf16)
        lowz[:, col] = (dg * y * (sig * (1.0 + gate * (1.0 - sig)))).astype(bf16)
        part = jnp.sum(grad * normal, axis=0, keepdims=True)
        ggain[:, col] += jnp.where(iota((8, HALF), 0) == 0, part, 0.0)


def send_tiles(buf, own, far, sem):
    me = here()
    m = pl.program_id(0)
    z0 = 2 * me["zh"] + me["zl"]
    for core in range(2):

        @pl.when(me["c"] == core)
        def _(core=core):
            for k in range(4):
                dy = lax.rem(lax.rem(2 * m + k // 2, 4) - me["y"] + 4, 4)
                for g in range(2):
                    dz = lax.rem(2 * (m // 2) + g - z0 + 4, 4)
                    at = 4 * dz + dy if k % 2 == 0 else 4 * dy + dz
                    pltpu.make_async_copy(
                        buf.at[pl.ds(pl.multiple_of(384 * m + 96 * k, 96), 96), pl.ds(g * CH, CH)],
                        (own if k % 2 == core else far).at[pl.ds(pl.multiple_of(96 * at, 96), 96)],
                        sem.at[m],
                    ).start()


def row_gain(part, w):
    lanes = sum(part[:, k : k + 128] * w[:, k : k + 128].astype(f32) for k in range(0, part.shape[1], 128))
    ones = jnp.ones((8, 128), bf16)
    hi, lo = halves(lanes)
    return dot_nt(ones, hi) + dot_nt(ones, lo)


def wait_tiles(own, sem):
    for m in range(4):
        block = own.at[pl.ds(0, ROWS)]
        pltpu.make_async_copy(block, block, sem.at[m]).wait()


def early_kernel(feat_t, cot, lowz, mixed, w, own, far, gains, buf, sem):
    m = pl.program_id(0)
    rows = pl.ds(pl.multiple_of(384 * m, 384), 384)
    part = dot(feat_t[...], lowz[...])
    out = dot_tn(cot[...], mixed[...]).astype(bf16)
    low = part.astype(bf16)
    for g in range(2):
        col = slice(g * HALF, (g + 1) * HALF)
        buf[rows, g * CH : g * CH + HALF] = low[:, col]
        buf[rows, g * CH + HALF : (g + 1) * CH] = out[:, col]
    send_tiles(buf, own, far, sem)
    gains[...] = row_gain(part, jnp.concatenate([w[:, :HALF], w[:, LEFT : LEFT + HALF]], axis=1))

    @pl.when(m == 3)
    def _():
        wait_tiles(own, sem)


def late_kernel(feat_t, low, w, gains_in, acc, accs, ggain, *refs):
    own, far, small, buf, gains, tail, sem, tail_sem = refs[-8:]
    m = pl.program_id(0)
    rows = pl.ds(pl.multiple_of(384 * m, 384), 384)
    both = w[:, LEFT - N : LEFT].astype(f32) + w[:, 2 * LEFT - N :].astype(f32)
    rhs = jnp.concatenate(
        [low[:, HALF:LEFT], low[:, LEFT + HALF : LEFT + CH], low[:, LEFT + CH : LEFT + CH + N]], axis=1
    )
    taps = jnp.concatenate(
        [w[:, HALF : CH + N], both.astype(bf16), w[:, LEFT + HALF : LEFT + CH], w[:, LEFT + CH : LEFT + CH + N]],
        axis=1,
    )
    part = dot(feat_t[...], rhs)
    low_part = part.astype(bf16)
    shared = jnp.concatenate([low_part[:, HALF : HALF + 2 * N], low_part[:, 1024:1152]], axis=1)
    buf[rows, 0:HALF] = low_part[:, 0:HALF]
    buf[rows, CH : CH + HALF] = low_part[:, 640:1024]
    for g in range(2):
        buf[rows, g * CH + HALF : (g + 1) * CH] = shared
    send_tiles(buf, own, far, sem)
    gain = gains_in[...] + row_gain(part, taps)
    gains[m] = gain

    @pl.when(m == 3)
    def _():
        small[...] = jnp.zeros_like(small)
        small[0:6, :] = acc[0:6, :]
        small[6:7, :] = ggain[0:1, :]
        small[8:9, :] = jnp.concatenate([gains[0, 0:1, :], gains[1, 0:1, :]], axis=1)
        small[9:10, :] = jnp.concatenate([gains[2, 0:1, :], gains[3, 0:1, :]], axis=1)
        for row, rs in ((7, (5, 6)), (10, (0, 1, 2)), (11, (3, 4))):
            for k, r in enumerate(rs):
                small[row : row + 1, 256 * k : 256 * k + 256] = accs[r : r + 1, :]
        tail[...] = split_small(small[...])
        copy = pltpu.make_async_copy(tail, far.at[pl.ds(2 * ROWS, 32)], tail_sem.at[0])
        copy.start()
        wait_tiles(own, sem)
        copy.wait()


def split_small(total):
    return jnp.concatenate(halves(total), axis=0)


def sum_small(block):
    return block[:16].astype(f32) + block[16:].astype(f32)


def core_sum_kernel(with_small, *refs):
    own, far = refs[:2]
    outs = refs[-5:]
    if with_small:
        small = split_small(refs[2][...] + sum_small(far[2 * ROWS : 2 * ROWS + 32, :]))
    for out, first, count in zip(outs, (0, 384, 1152, 768, 960), (384, 384, 384, 192, 192)):
        rows = slice(first, first + count)
        out[0:count, :] = add(own[rows, :], far[rows, :])
        if with_small:
            out[count : count + 32, :] = small


def tile_middle_kernel(with_small, up, down, one, two, *refs):
    outs = refs[-3:] if with_small else refs[-2:]
    up_out, down_out = outs[:2]
    up_out[0:192, :] = add(up[0:192, :], one[0:192, :])
    up_out[192:384, :] = up[192:384, :]
    down_out[0:192, :] = down[0:192, :]
    down_out[192:384, :] = add(down[192:384, :], two[0:192, :])
    if with_small:
        up_out[384:416, :] = one[192:224, :]
        down_out[384:416, :] = down[384:416, :]
        outs[2][...] = split_small(sum_small(one[192:224, :]) + sum_small(two[192:224, :]))


def axis_sum_kernel(*refs):
    early, late, near, outs = refs[:3], refs[3:6], refs[6], refs[-4:]
    own, up = late[:2]
    small = split_small(sum_small(own[384:416, :]) + sum_small(up[384:416, :]) + sum_small(near[...]))
    for k, out in enumerate(outs):
        rows = slice(96 * k, 96 * k + 96)
        out[0:96, :] = add3([t[rows, :] for t in early]).astype(bf16)
        out[96:192, :] = add3([t[rows, :] for t in late]).astype(bf16)
        out[192:224, :] = small


def last_sum_kernel(*refs):
    terms, (early, tile, small, to_x) = refs[:4], refs[-4:]
    early[...] = add4([t[0:96, :] for t in terms])
    total = add4([t[96:192, :] for t in terms])
    tile[...] = total
    every = sum(sum_small(t[192:224, :]) for t in terms)
    small[...] = every
    for k in range(3):
        rows = slice(32 * k, 32 * k + 32)
        to_x[0:32, 256 * k : 256 * k + 128] = total[rows, HALF : HALF + N].astype(bf16)
        to_x[0:32, 256 * k + 128 : 256 * k + 256] = total[rows, HALF + 2 * N : HALF + 3 * N].astype(bf16)
    hi, lo = halves(every[8:16, :])
    to_x[32:48, :] = jnp.concatenate([hi.astype(f32), lo.astype(f32)], axis=0).astype(bf16)


def x_sum_kernel(a, b, c, d, gain, state, g_gain, g_conv, g_bias):
    total = add4([a[...], b[...], c[...], d[...]])
    for k in range(3):
        state[32 * k : 32 * k + 32, :] = total[0:32, 256 * k : 256 * k + 256]
    small = total[32:40, :] + total[40:48, :]
    g_gain[:, :CH] = small[0:1, :] / gain[:, :CH]
    g_gain[:, CH:] = small[1:2, :] / gain[:, CH:]
    for k in range(3):
        g_conv[k : k + 1, :] = small[2:3, 256 * k : 256 * k + 256]
    g_conv[3:4, :] = small[3:4, 0:256]
    g_bias[...] = small[3:4, 256:512]


def bwd_kernel(s, *refs):
    refs = list(refs)
    pre = refs.pop(0)
    prev = refs.pop(0) if s else None
    msg = refs.pop(0) if s == 2 else None
    act, hs, dssd, lowz, prm, prs, heads = refs[:7]
    refs = refs[7:]
    if s < 2:
        dh_in, tail, acc_in, accs_in = refs[:4]
        refs = refs[4:]
        back = refs.pop(0) if s == 0 else None
    refs = refs[len(refs) - (10 if s == 2 else 9) :]
    low, dh, head_rows, acc, accs = refs[:5]
    refs = refs[5:]
    for g in range(2):
        low[:, g * LEFT : g * LEFT + HALF] = lowz[:, g * HALF : (g + 1) * HALF]
    out_msg = refs.pop(0) if s == 2 else None
    vx, vs, dp, ds = refs
    zl = lax.axis_index("zl")
    framed_inputs(s, zl, pre, prev, msg, vx, vs)
    if s == 2:
        dh[...] = jnp.zeros_like(dh)
        dp[256:264, :] = jnp.zeros((8, CH), f32)
        ds[256:264, :] = jnp.zeros((8, 2 * N), f32)
        acc[...] = jnp.zeros_like(acc)
        accs[...] = jnp.zeros_like(accs)
    else:
        hd, hp, hq = dh_in[...], tail[0:8, :], tail[8:16, 0 : 2 * N]
        if s == 1:
            hd, hp, hq = (jnp.where(zl == 0, v, 0.0) for v in (hd, hp, hq))
        else:
            hd = jnp.where(zl == 1, hd, back[0:128, :].astype(f32))
            hp = jnp.where(zl == 1, hp, back[128:144, :].astype(f32)[:8])
            hq = jnp.where(zl == 1, hq, back[144:160, 0 : 2 * N].astype(f32)[:8])
        dh[...], dp[256:264, :], ds[256:264, :] = hd, hp, hq
        acc[...] = acc_in[...]
        accs[...] = accs_in[...]
    raw_all, dt_all = step_sizes(pre, heads)
    rate = heads[0:1, :]
    a_all = -rate * dt_all
    sub, lane = iota((Q, 128), 0), iota((Q, 128), 1)
    tri = jnp.where(sub >= lane, 1.0, 0.0).astype(bf16)
    up_mask = lane >= sub
    tri_up = jnp.where(up_mask, 1.0, 0.0).astype(bf16)
    below = jnp.where(lane < sub, 1.0, 0.0).astype(bf16)
    left = lane < 64
    for j in (1, 0):
        r0 = Q * j
        rows = slice(r0, r0 + Q)
        pre_s = [act[rows, 2 * CH + g * N : 2 * CH + (g + 1) * N] for g in range(2)]
        sig_s = [jax.nn.sigmoid(v) for v in pre_s]
        bf, cf = [(v * w).astype(bf16).astype(f32) for v, w in zip(pre_s, sig_s)]
        b, c = bf.astype(bf16), cf.astype(bf16)
        ct = cf.T.astype(bf16)
        scores_t = dot_nt(c, b).T
        dt, a = dt_all[rows], a_all[rows]
        cum = tri_dot(tri, a)
        cum_t = cum.T
        d_scores_t = jnp.zeros((Q, Q), f32)
        d_b = jnp.zeros((Q, N), f32)
        d_c = jnp.zeros((Q, N), f32)
        per_head = jnp.zeros((3 * Q, 128), f32)
        for i in range(PAIRS):
            col, _ = pair_places(i)
            cx = act[rows, CH + 128 * i : CH + 128 * i + 128]
            sig = jax.nn.sigmoid(cx)
            x = (cx * sig).astype(bf16).astype(f32)
            dyb = dssd[rows, col]
            dy = dyb.astype(f32)
            skip = prm[6:7, col]
            c0, c1 = lanes_of(cum, 2 * i), lanes_of(cum, 2 * i + 1)
            l0 = jnp.exp(jnp.where(up_mask, cum_t[2 * i : 2 * i + 1, :] - c0, NEG))
            l1 = jnp.exp(jnp.where(up_mask, cum_t[2 * i + 1 : 2 * i + 2, :] - c1, NEG))
            cp = jnp.where(left, c0, c1)
            dtp = jnp.where(left, lanes_of(dt, 2 * i), lanes_of(dt, 2 * i + 1))
            last = cp[Q - 1 : Q, :]
            fade = jnp.exp(last - cp)
            xdt = x * dtp
            xdtb = xdt.astype(bf16)
            zero = jnp.zeros_like(xdtb)
            dy_split = jnp.concatenate([jnp.where(left, dyb, zero), jnp.where(left, zero, dyb)], axis=0)
            x_split = jnp.concatenate([jnp.where(left, xdtb, zero), jnp.where(left, zero, xdtb)], axis=0)
            dhp = dh[:, col]
            dhb = dhp.astype(bf16)
            m_t = jnp.concatenate([(scores_t * l0).astype(bf16), (scores_t * l1).astype(bf16)], axis=1)
            inside = dot(m_t, dy_split)
            beyond = fade * dot(b, dhb)
            dxdt = inside + beyond
            dx = dxdt * dtp + skip * dy
            acc[5:6, col] += jnp.sum(dy * x, axis=0, keepdims=True)
            d_m_t = dot_nt(x_split, dyb)
            d_scores_t = d_scores_t + d_m_t[:Q] * l0 + d_m_t[Q:] * l1
            h = hs[j, :, col]
            crossing = jnp.sum(dhp * h, axis=0, keepdims=True) * jnp.exp(last)
            t1 = dxdt * x
            t2 = dy * (act[rows, col] - skip * x) - xdtb.astype(f32) * inside
            t2 = t2 + jnp.where(sub == Q - 1, crossing, 0.0)
            t3 = xdt * beyond
            pick = (lane == jnp.where(sub < 64, 2 * i, 2 * i + 1)).astype(f32).astype(bf16)
            hi, lo = halves(jnp.concatenate([t1, t2, t3], axis=0))
            per_head = per_head + dot(
                jnp.concatenate([hi, lo], axis=1), jnp.concatenate([pick, pick], axis=0)
            )
            dye = (dy * jnp.exp(cp)).astype(bf16)
            d_c = d_c + dot_nt(dye, h.astype(bf16))
            d_b = d_b + dot_nt((xdt * fade).astype(bf16), dhb)
            dh[:, col] = dhp * jnp.exp(last) + dot(ct, dye)
            dp[rows, col] = dx * (sig * (1.0 + cx * (1.0 - sig)))
        d_b = d_b + dot(d_scores_t.astype(bf16), c)
        d_c = d_c + dot(d_scores_t.T.astype(bf16), b)
        for g, grad in ((0, d_b), (1, d_c)):
            ds[rows, g * N : (g + 1) * N] = grad * (sig_s[g] * (1.0 + pre_s[g] * (1.0 - sig_s[g])))
        da = tri_dot(tri_up, per_head[Q : 2 * Q]) + tri_dot(below, per_head[2 * Q :])
        ddt = per_head[:Q] - rate * da
        dstep = ddt * jax.nn.sigmoid(raw_all[rows])
        accs[5:6, 0:128] += jnp.sum(a * da, axis=0, keepdims=True)
        accs[6:7, 0:128] += jnp.sum(dstep, axis=0, keepdims=True)
        for g in range(2):
            low[rows, (g + 1) * LEFT - N : (g + 1) * LEFT] = dstep.astype(bf16)
    for frame, grads, taps, out, width in ((vx, dp, prm, acc, CH), (vs, ds, prs, accs, 2 * N)):
        for i in range(width // 128):
            col = slice(128 * i, 128 * i + 128)
            g, p = divmod(i, width // 256)
            to = g * LEFT + HALF + 128 * p + (HALF if width == 2 * N else 0)
            back_v = sum(taps[k : k + 1, col] * grads[3 - k : 3 - k + STEP, col] for k in range(4))
            low[:, to : to + 128] = back_v.astype(bf16)
            own = grads[0:STEP, col]
            for k in range(4):
                out[k : k + 1, col] += jnp.sum(own * frame[5 + k : 5 + k + STEP, col], axis=0, keepdims=True)
            out[4:5, col] += jnp.sum(own, axis=0, keepdims=True)
    head_rows[0:8, :] = dp[0:8, :]
    head_rows[8:16, :] = jnp.concatenate([ds[0:8, :], jnp.zeros((8, CH - 2 * N), f32)], axis=1)
    if s == 2:
        out_msg[0:128, :] = dh[...].astype(bf16)
        out_msg[128:144, :] = jnp.concatenate([head_rows[0:8, :]] * 2, axis=0).astype(bf16)
        out_msg[144:160, :] = jnp.concatenate([head_rows[8:16, :]] * 2, axis=0).astype(bf16)


def feat_kernel(low, w, *refs):
    store_rows(pl.program_id(0), dot_nt(low[...], w[...]).astype(bf16), refs[-5:])


ANY = pl.BlockSpec(memory_space=pl.ANY)
VM = pl.BlockSpec(memory_space=pltpu.VMEM)


def params(mib):
    return pltpu.CompilerParams(vmem_limit_bytes=mib * 1024 * 1024)


def shape(*s, dtype=f32):
    return jax.ShapeDtypeStruct(s, dtype)


def cost(flops, moved_bytes):
    return pl.CostEstimate(flops=int(flops), bytes_accessed=int(moved_bytes), transcendentals=0)


ONCE = pl.Buffered(buffer_count=1)


def whole(*s):
    return pl.BlockSpec(s, lambda i: (0,) * len(s), pipeline_mode=ONCE)


def steps(width, column=0):
    return pl.BlockSpec((STEP, width), lambda i: (i, column))


def fixed(s, width, column=0):
    return pl.BlockSpec((STEP, width), lambda i: (s, column), pipeline_mode=ONCE)


def line_up(parts, deps):
    return pl.pallas_call(
        line_kernel,
        in_specs=[VM] * 4 + [ANY] * len(deps),
        out_specs=VM,
        out_shape=shape(384, FULL, dtype=bf16),
        compiler_params=params(4),
        cost_estimate=cost(1e6, 2e6),
        name="line_up",
    )(*parts, *deps)


def touch(a, deps):
    return pl.pallas_call(
        touch_kernel,
        in_specs=[ANY] * (1 + len(deps)),
        out_specs=ANY,
        out_shape=jax.ShapeDtypeStruct(a.shape, a.dtype),
        input_output_aliases={0: 0},
        compiler_params=params(1),
        cost_estimate=cost(1, 1),
        name="touch",
    )(a, *deps)


def normalize(rows, gain):
    return pl.pallas_call(
        norm_kernel,
        in_specs=[ANY] * 4 + [VM],
        out_specs=[VM, VM],
        out_shape=[shape(ROWS, D, dtype=bf16), shape(D, ROWS, dtype=bf16)],
        scratch_shapes=[pltpu.VMEM((ROWS, D), bf16), pltpu.SemaphoreType.DMA((N_ROW_COPIES,))],
        compiler_params=params(12),
        cost_estimate=cost(1e7, 5e6),
        name="normalize",
    )(*rows, gain)


def project(feat, weights):
    return pl.pallas_call(
        proj_kernel,
        grid=(4,),
        in_specs=[ANY] * 8 + [whole(ROWS, D)],
        out_specs=[ANY, ANY, pl.BlockSpec((ROWS, 512), lambda i: (0, i))],
        out_shape=[shape(D, 2 * LEFT, dtype=bf16), shape(D, CH, dtype=bf16), shape(ROWS, 2 * LEFT)],
        scratch_shapes=[
            pltpu.VMEM((D, 2 * LEFT), bf16),
            pltpu.VMEM((D, CH), bf16),
            pltpu.SemaphoreType.DMA((2,)),
            pltpu.SemaphoreType.DMA((2,)),
            pltpu.SemaphoreType.DMA((2,)),
        ],
        compiler_params=params(20),
        cost_estimate=cost(2 * ROWS * D * 2 * LEFT, 24e6),
        name="project",
    )(*weights, feat)


def prev_spec(s):
    return pl.BlockSpec((8, 2 * LEFT), lambda i: (32 * s - 1, 0))


def forward(s, pre, act, h, msg, prm, prs, heads, deps=()):
    ins, specs = [pre], [fixed(s, 2 * LEFT)]
    if s:
        ins += [pre, h]
        specs += [prev_spec(s), pl.BlockSpec((1, N, CH), lambda i: (2, 0, 0))]
    if s == 2:
        ins += [msg]
        specs += [whole(160, CH)]
    ins += [prm, prs, heads]
    specs += [whole(8, CH), whole(8, 2 * N), whole(8, 128)]
    aliases = {}
    if s:
        aliases = {len(ins): 0}
        ins += [act, *deps]
        specs += [ANY] * (1 + len(deps))
    outs = [shape(ROWS, 2 * CH + 2 * N), shape(3, N, CH)]
    out_specs = [fixed(s, 2 * CH + 2 * N), whole(3, N, CH)]
    if s == 0:
        outs += [shape(160, CH, dtype=bf16)]
        out_specs += [whole(160, CH)]
    return pl.pallas_call(
        functools.partial(fwd_kernel, s),
        grid=(1,),
        in_specs=specs,
        out_specs=out_specs,
        out_shape=outs,
        input_output_aliases=aliases,
        scratch_shapes=[pltpu.VMEM((264, CH), f32), pltpu.VMEM((264, 2 * N), f32)],
        compiler_params=params(12),
        cost_estimate=cost(1.5e9, 6e6),
        name=f"scan_rows_{s}",
    )(*ins)


def cotangent(rows, w, pre, act, prm):
    return pl.pallas_call(
        cot_kernel,
        grid=(3,),
        in_specs=[ANY] * 5 + [whole(D, CH), steps(512, 0), steps(512, 2), steps(CH), whole(8, CH)],
        out_specs=[ANY, steps(CH), steps(CH), pl.BlockSpec((8, STEP), lambda i: (0, i))],
        out_shape=[
            shape(ROWS, D, dtype=bf16),
            shape(ROWS, CH),
            shape(ROWS, CH, dtype=bf16),
            shape(8, ROWS),
        ],
        scratch_shapes=[
            pltpu.VMEM((ROWS, D), bf16),
            pltpu.SemaphoreType.DMA((N_ROW_COPIES,)),
            pltpu.SemaphoreType.DMA((1,)),
        ],
        compiler_params=params(16),
        cost_estimate=cost(2 * ROWS * D * CH, 20e6),
        name="cotangent",
    )(*rows, w, pre, pre, act, prm)


def out_partial(gb, w):
    return pl.pallas_call(
        out_kernel,
        grid=(3,),
        in_specs=[steps(CH), whole(D, CH)],
        out_specs=[whole(192, D)] * 3 + [whole(192, CH)] * 2,
        out_shape=[shape(192, D, dtype=bf16)] * 3 + [shape(192, CH, dtype=bf16)] * 2,
        compiler_params=params(12),
        cost_estimate=cost(2 * ROWS * D * CH, 6e6),
        name="out_partial",
    )(gb, w)


def gate_back(sums, gm, act, pre, prm, deps):
    row = pl.BlockSpec((8, STEP), lambda i: (0, i))
    return pl.pallas_call(
        gate_kernel,
        grid=(3,),
        in_specs=[row] * 4
        + [steps(CH), steps(CH), steps(512, 0), steps(512, 2), whole(8, CH)]
        + [ANY] * len(deps),
        out_specs=[steps(CH), steps(CH), steps(CH), whole(8, CH)],
        out_shape=[shape(ROWS, CH, dtype=bf16)] * 3 + [shape(8, CH)],
        compiler_params=params(11),
        cost_estimate=cost(1e7, 12e6),
        name="gate_back",
    )(*sums, gm, act, pre, pre, prm, *deps)


def early_grads(feat_t, cot, lowz, mixed, w):
    return pl.pallas_call(
        early_kernel,
        grid=(4,),
        in_specs=[
            pl.BlockSpec((HALF, ROWS), lambda m: (m, 0)),
            pl.BlockSpec((ROWS, HALF), lambda m: (0, m)),
            whole(ROWS, CH),
            whole(ROWS, CH),
            pl.BlockSpec((HALF, 2 * LEFT), lambda m: (m, 0)),
        ],
        out_specs=[ANY, ANY, pl.BlockSpec((8, HALF), lambda m: (0, m))],
        out_shape=[shape(2 * ROWS, CH, dtype=bf16)] * 2 + [shape(8, D)],
        scratch_shapes=[pltpu.VMEM((D, 2 * CH), bf16), pltpu.SemaphoreType.DMA((4,))],
        compiler_params=params(18),
        cost_estimate=cost(2 * ROWS * D * 2 * CH, 12e6),
        name="early_grads",
    )(feat_t, cot, lowz, mixed, w)


def late_grads(feat_t, low, w, gains, acc, accs, ggain, deps):
    return pl.pallas_call(
        late_kernel,
        grid=(4,),
        in_specs=[
            pl.BlockSpec((HALF, ROWS), lambda m: (m, 0)),
            whole(ROWS, 2 * LEFT),
            pl.BlockSpec((HALF, 2 * LEFT), lambda m: (m, 0)),
            pl.BlockSpec((8, HALF), lambda m: (0, m)),
            whole(8, CH),
            whole(8, 2 * N),
            whole(8, CH),
        ]
        + [ANY] * len(deps),
        out_specs=[ANY, ANY, whole(16, CH)],
        out_shape=[shape(2 * ROWS, CH, dtype=bf16), shape(2 * ROWS + 32, CH, dtype=bf16), shape(16, CH)],
        scratch_shapes=[
            pltpu.VMEM((D, 2 * CH), bf16),
            pltpu.VMEM((4, 8, HALF), f32),
            pltpu.VMEM((32, CH), bf16),
            pltpu.SemaphoreType.DMA((4,)),
            pltpu.SemaphoreType.DMA((1,)),
        ],
        compiler_params=params(18),
        cost_estimate=cost(2 * ROWS * D * 3 * HALF, 12e6),
        name="late_grads",
    )(feat_t, low, w, gains, acc, accs, ggain, *deps)


def tile_sums(kernel, ins, outs, deps, name, mib=6):
    return pl.pallas_call(
        kernel,
        in_specs=[VM] * len(ins) + [ANY] * len(deps),
        out_specs=[VM] * len(outs),
        out_shape=outs,
        compiler_params=params(mib),
        cost_estimate=cost(1e6, 4e6),
        name=name,
    )(*ins, *deps)


def core_sum(own, far, small, deps, name):
    more = 32 if small else 0
    return tile_sums(
        functools.partial(core_sum_kernel, bool(small)),
        [own, far] + list(small),
        [shape(384 + more, CH, dtype=bf16)] * 3 + [shape(192 + more, CH, dtype=bf16)] * 2,
        deps,
        name,
        10,
    )


def row_middle(ins, deps):
    return tile_sums(row_middle_kernel, ins, [shape(192, D, dtype=bf16)] * 2, deps, "row_middle")


def tile_middle(with_small, ins, deps):
    outs = [shape(416 if with_small else 384, CH, dtype=bf16)] * 2
    if with_small:
        outs = outs + [shape(32, CH, dtype=bf16)]
    return tile_sums(functools.partial(tile_middle_kernel, with_small), ins, outs, deps, "tile_middle")


def backward(s, pre, msg, act, hs, dssd, lowz, prm, prs, heads, carried, back, low, deps):
    ins, specs = [pre], [fixed(s, 2 * LEFT)]
    if s:
        ins += [pre]
        specs += [prev_spec(s)]
    if s == 2:
        ins += [msg]
        specs += [whole(160, CH)]
    ins += [act, hs, dssd, lowz, prm, prs, heads]
    specs += [fixed(s, 2 * CH + 2 * N), whole(3, N, CH), fixed(s, CH), fixed(s, CH)]
    specs += [whole(8, CH), whole(8, 2 * N), whole(8, 128)]
    aliases = {}
    if s < 2:
        ins += list(carried)
        specs += [whole(N, CH), whole(16, CH), whole(8, CH), whole(8, 2 * N)]
        if s == 0:
            ins += [back]
            specs += [whole(160, CH)]
        aliases = {len(ins): 0}
        ins += [low]
        specs += [ANY]
    ins += list(deps)
    specs += [ANY] * len(deps)
    outs = [shape(ROWS, 2 * LEFT, dtype=bf16), shape(N, CH), shape(16, CH), shape(8, CH), shape(8, 2 * N)]
    out_specs = [fixed(s, 2 * LEFT), whole(N, CH), whole(16, CH), whole(8, CH), whole(8, 2 * N)]
    if s == 2:
        outs += [shape(160, CH, dtype=bf16)]
        out_specs += [whole(160, CH)]
    return pl.pallas_call(
        functools.partial(bwd_kernel, s),
        grid=(1,),
        in_specs=specs,
        out_specs=out_specs,
        out_shape=outs,
        input_output_aliases=aliases,
        scratch_shapes=[
            pltpu.VMEM((264, CH), f32),
            pltpu.VMEM((264, 2 * N), f32),
            pltpu.VMEM((264, CH), f32),
            pltpu.VMEM((264, 2 * N), f32),
        ],
        compiler_params=params(16),
        cost_estimate=cost(4e9, 8e6),
        name=f"scan_back_{s}",
    )(*ins)


def feat_partial(low, w, deps):
    return pl.pallas_call(
        feat_kernel,
        grid=(3,),
        in_specs=[steps(2 * LEFT), whole(D, 2 * LEFT)] + [ANY] * len(deps),
        out_specs=[whole(192, D)] * 3 + [whole(192, CH)] * 2,
        out_shape=[shape(192, D, dtype=bf16)] * 3 + [shape(192, CH, dtype=bf16)] * 2,
        compiler_params=params(18),
        cost_estimate=cost(2 * ROWS * D * 2 * LEFT, 16e6),
        name="feat_partial",
    )(low, w, *deps)


def local(
    layer_input,
    input_gain,
    proj_inner,
    proj_step,
    proj_state,
    proj_output,
    conv_inner,
    conv_inner_bias,
    conv_state,
    conv_state_bias,
    inner_gain,
    decay_log,
    step_bias,
    skip_gain,
    out_cotangent,
):
    zl = lax.axis_index("zl")
    step_cols = jnp.where(
        zl == 0, jnp.pad(proj_step, ((0, 0), (0, 122))), jnp.pad(proj_step, ((0, 0), (6, 116)))
    )
    state_cols = jnp.where(zl == 0, proj_state[:, :N], proj_state[:, N:])
    shard = jnp.concatenate(
        [proj_inner[:, 0], proj_inner[:, 1], state_cols, step_cols, proj_output.T], axis=1
    )
    near = spread(shard, "first")

    coef = jnp.pad(jnp.stack([decay_log, step_bias, skip_gain]), ((0, 0), (0, 122))).reshape(1, HALF)
    small = jnp.concatenate(
        [touch(conv_inner, (near[0],)), conv_inner_bias[None], inner_gain[None], coef, jnp.zeros((1, HALF), f32)], axis=0
    )
    prm, heads = pl.pallas_call(
        param_kernel,
        in_specs=[VM, VM],
        out_specs=[VM, VM],
        out_shape=[shape(8, CH), shape(8, 128)],
        compiler_params=params(1),
        cost_estimate=cost(1, 1),
        name="parameters",
    )(small, send(small, "zl", 1))
    prs = jnp.concatenate([conv_state, conv_state_bias[None], jnp.zeros((3, 2 * N), f32)], axis=0)

    rows = (layer_input,) + spread(layer_input, "x")
    line = line_up((shard,) + near, (rows[1], rows[3], prm, heads, prs))
    far = spread(line, "second")
    first = touch(far[0], (rows[2],))
    feat, feat_t = normalize(rows, input_gain[None])
    third = touch(far[2], (feat,))
    mine = (line, first, far[1], third)
    weights = mine + tuple(send(a, "c", 1) for a in mine)
    w_in, w_o, pre = project(feat, weights)
    below, above = send(out_cotangent, "x", 1), send(out_cotangent, "x", 3)
    cot_rows = (out_cotangent, below, above, send(below[:, :CH], "x", 1), send(above[:, CH:], "x", 3))

    act, hs0, msg = forward(0, pre, None, None, None, prm, prs, heads)
    msg = send(msg, "zl", 1)
    act, hs1 = forward(1, pre, act, hs0, None, prm, prs, heads)
    act, hs2 = forward(2, pre, act, hs1, msg, prm, prs, heads)
    cot, gm, gb, sums = cotangent(cot_rows, w_o, pre, act, prm)
    all_sums = (sums,) + spread(sums, "x")
    parts = out_partial(gb, w_o)
    out_terms, (out_up,) = ring(parts, "x", row_middle)
    dssd, lowz, mixed, ggain = gate_back(all_sums, gm, act, pre, prm, (parts[0],))

    own, far, gains = early_grads(feat_t, cot, lowz, mixed, w_in)
    far = send(far, "c", 1)
    scan = (prm, prs, heads)
    low, *carried, back = backward(2, pre, msg, act, hs2, dssd, lowz, *scan, None, None, None, (own,))
    back = send(back, "zl", 1)
    parts = core_sum(own, far, (), (low,), "early_core_sum")
    early_terms, (early_up,) = ring(parts, "second", functools.partial(tile_middle, False))
    low, *carried = backward(1, pre, None, act, hs1, dssd, lowz, *scan, carried, None, low, (parts[0], out_up))
    deps = (early_up,)
    low, _, _, acc, accs = backward(0, pre, None, act, hs0, dssd, lowz, *scan, carried, back, low, deps)

    own, far, small = late_grads(feat_t, low, w_in, gains, acc, accs, ggain, out_terms[1:])
    far = send(far, "c", 1)
    feat_parts = feat_partial(low, w_in, (own,))
    parts = core_sum(own, far, (small,), (feat_parts[0],) + early_terms[1:], "late_core_sum")
    feat_terms, (feat_up,) = ring(feat_parts, "x", row_middle, (parts[0],))
    late_terms, (_, near) = ring(parts, "second", functools.partial(tile_middle, True))
    parts = tile_sums(
        axis_sum_kernel,
        early_terms + late_terms + (near,),
        [shape(224, CH, dtype=bf16)] * 4,
        (feat_up,),
        "axis_sum",
    )
    early, late, small, to_x = tile_sums(
        last_sum_kernel,
        deal(parts, "first"),
        [shape(96, CH), shape(96, CH), shape(16, CH), shape(48, CH, dtype=bf16)],
        feat_terms[1:],
        "last_sum",
    )
    g_state, g_input_gain, g_conv_state, g_conv_state_bias = tile_sums(
        x_sum_kernel,
        (to_x,) + spread(to_x, "x") + (input_gain[None],),
        [shape(96, 2 * N), shape(1, D), shape(4, 2 * N), shape(1, 2 * N)],
        (),
        "x_sum",
    )

    own = lambda a: jnp.where(zl == 0, a[..., :HALF], a[..., HALF:])
    six = lambda a: jnp.where(zl == 0, a[:6], a[6:12])
    conv = own(small[:7])
    g_skip = six(small[5].reshape(12, 64).sum(axis=1))
    g_decay, g_bias = six(small[7, :128]), six(small[7, 256:384])
    g_step = jnp.where(zl == 0, late[:, 512:518], late[:, 518:524])

    values = layer_input.astype(f32)
    squares = all_sums[0][0] + all_sums[1][0] + all_sums[2][0] + all_sums[3][0]
    at = lax.rem(192 * lax.axis_index("x") + 256 + 256 * zl, ROWS)
    squares = lax.dynamic_slice_in_dim(jnp.concatenate([squares, squares]), at, 192)
    scale = lax.rsqrt(squares / DI + EPS)[:, None]
    layer_output = (values + add3(out_terms) * scale).astype(bf16)
    inv = lax.rsqrt(jnp.mean(values * values, axis=1, keepdims=True) + EPS)
    weighted = add3(feat_terms) * input_gain
    input_grad = (
        out_cotangent.astype(f32)
        + weighted * inv
        - values * (inv * inv * inv) * jnp.mean(weighted * values, axis=1, keepdims=True)
    )
    return (
        layer_output,
        input_grad,
        g_input_gain[0],
        jnp.stack([early[:, :HALF], late[:, :HALF]], axis=1),
        g_step,
        g_state,
        early[:, HALF:].T,
        conv[:4],
        conv[4],
        g_conv_state,
        g_conv_state_bias[0],
        conv[6],
        g_decay,
        g_bias,
        g_skip,
    )


def solution(mesh):
    split = Mesh(mesh.devices.reshape(SIZES), AX)
    everything = FSDP + TP
    return jax.shard_map(
        local,
        mesh=split,
        in_specs=(
            P(everything, None),
            P(),
            P(FSDP, None, TP),
            P(FSDP, TP),
            P(FSDP, None),
            P(TP, FSDP),
            P(None, TP),
            P(TP),
            P(),
            P(),
            P(TP),
            P(TP),
            P(TP),
            P(TP),
            P(everything, None),
        ),
        out_specs=(
            P(everything, None),
            P(everything, None),
            P(),
            P(FSDP, None, TP),
            P(FSDP, TP),
            P(FSDP, None),
            P(TP, FSDP),
            P(None, TP),
            P(TP),
            P(),
            P(),
            P(TP),
            P(TP),
            P(TP),
            P(TP),
        ),
        check_vma=False,
    )
```

```python
import functools
import itertools

import jax
import jax.numpy as jnp
import numpy as np
from jax import lax
from jax.experimental import pallas as pl
from jax.experimental.pallas import tpu as pltpu
from jax.sharding import Mesh
from jax.sharding import PartitionSpec as P

D = 1536
DI = 3072
N = 128
Q = 128
STEP = 256
ROWS = 768
CH = 768
HALF = 384
PAIRS = 6
LEFT = 1024
FULL = LEFT + HALF
EPS = 1e-05
NEG = -1e30

AX = ("zh", "y", "c", "zl", "x")
SIZES = (2, 4, 2, 2, 4)
FSDP = ("zh", "y", "c")
TP = ("zl", "x")

bf16 = jnp.bfloat16
f32 = jnp.float32


def moved(d, axis, k):
    d = dict(d)
    if axis == "z":
        z = (2 * d["zh"] + d["zl"] + k) % 4
        d["zh"], d["zl"] = divmod(z, 2)
    elif axis == "first":
        return moved(d, "y" if d["c"] == 0 else "z", k)
    elif axis == "second":
        return moved(d, "z" if d["c"] == 0 else "y", k)
    else:
        d[axis] = (d[axis] + k) % SIZES[AX.index(axis)]
    return d


def send(a, axis, k):
    pairs = []
    for place in itertools.product(*map(range, SIZES)):
        to = moved(dict(zip(AX, place)), axis, k)
        pairs.append(
            (
                int(np.ravel_multi_index(place, SIZES)),
                int(np.ravel_multi_index([to[n] for n in AX], SIZES)),
            )
        )
    return lax.ppermute(a, AX, pairs)


def spread(a, axis):
    return tuple(send(a, axis, k) for k in (1, 2, 3))


def deal(parts, axis):
    return (parts[0],) + tuple(send(parts[k], axis, k) for k in (1, 2, 3))


def ring(parts, axis, middle, deps=()):
    own, up, down, one, two = parts
    one, two = send(one, axis, 1), send(two, axis, 3)
    up, down, *more = middle((up, down, one, two), deps)
    return (own, send(up, axis, 1), send(down, axis, 3)), (up, *more)


def add3(terms):
    a, b, c = (t.astype(f32) for t in terms)
    return a + (b + c)


def add4(terms):
    a, b, c, d = (t.astype(f32) for t in terms)
    return (a + b) + (c + d)


def dot(a, b):
    return lax.dot_general(a, b, (((1,), (0,)), ((), ())), preferred_element_type=f32)


def dot_nt(a, b):
    return lax.dot_general(a, b, (((1,), (1,)), ((), ())), preferred_element_type=f32)


def dot_tn(a, b):
    return lax.dot_general(a, b, (((0,), (0,)), ((), ())), preferred_element_type=f32)


def halves(a):
    hi = a.astype(bf16)
    return hi, (a - hi.astype(f32)).astype(bf16)


def thirds(a):
    hi = a.astype(bf16)
    rest = a - hi.astype(f32)
    mid = rest.astype(bf16)
    return hi, mid, (rest - mid.astype(f32)).astype(bf16)


def tri_dot(tri, a):
    return dot(jnp.concatenate([tri] * 3, axis=1), jnp.concatenate(thirds(a), axis=0))


def lanes_of(a, i):
    return jnp.broadcast_to(a[:, i : i + 1], (Q, 128))


def iota(shape, dim):
    return lax.broadcasted_iota(jnp.int32, shape, dim)


def softplus(v):
    return jnp.maximum(v, 0.0) + jnp.log1p(jnp.exp(-jnp.abs(v)))


def here():
    return {n: lax.axis_index(n) for n in AX}


def row_copies(pieces, dst, sems):
    me = here()
    places = ((0, 0, D), (1, 0, D), (2, 0, D), (3, 0, D))
    if len(pieces) == 5:
        places = ((0, 0, D), (1, 0, D), (3, 0, D), (2, 0, CH), (2, CH, CH))
    copies = []
    for ref, (k, col, width) in zip(pieces, places):
        x = lax.rem(me["x"] + 4 - k, 4)
        for g in range(3):
            at = lax.rem(3 * x + g + 4 + 4 * me["zl"], 12)
            to = dst.at[pl.ds(pl.multiple_of(64 * at, 64), 64), pl.ds(col, width)]
            copies.append((ref.at[pl.ds(64 * g, 64)], to))
    return [pltpu.make_async_copy(s, d, sems.at[i]) for i, (s, d) in enumerate(copies)]


N_ROW_COPIES = 15


def weight_copies(pieces, column, width, dst, sems):
    me = here()
    copies = []
    for k, ref in enumerate(pieces):
        core = lax.rem(me["c"] + k // 4, 2)
        rb = -k % 4
        for kk in range(4):
            ra = -kk % 4
            y = lax.rem(me["y"] + jnp.where(core == 0, ra, rb), 4)
            z = lax.rem(2 * me["zh"] + me["zl"] + jnp.where(core == 0, rb, ra), 4)
            f = (z // 2 * 4 + y) * 2 + core
            copies.append(
                (
                    ref.at[pl.ds(96 * kk, 96), pl.ds(column, width)],
                    dst.at[
                        pl.ds(pl.multiple_of(96 * f, 96), 96),
                        pl.ds(pl.multiple_of(width * lax.rem(z, 2), 128), width),
                    ],
                    lax.rem(z, 2),
                )
            )
    return [pltpu.make_async_copy(s, d, sems.at[g]) for s, d, g in copies]


def wait_half(g, width, dst, sems):
    half = dst.at[:, pl.ds(g * width, width)]
    pltpu.make_async_copy(half, half, sems.at[g]).wait()


def line_kernel(a, b, c, d, *rest):
    for k, ref in enumerate((a, b, c, d)):
        rest[-1][96 * k : 96 * k + 96, :] = ref[...]


def norm_kernel(*refs):
    rows, (gain, feat, feat_t, raw, sem) = refs[:4], refs[4:]
    copies = row_copies(rows, raw, sem)
    for c in copies:
        c.start()
    for c in copies:
        c.wait()
    for k in range(ROWS // 128):
        at = slice(128 * k, 128 * k + 128)
        v = raw[at, :].astype(f32)
        r = lax.rsqrt(jnp.mean(v * v, axis=1, keepdims=True) + EPS)
        normed = v * r * gain[...]
        feat[at, :] = normed.astype(bf16)
        for m in range(D // 128):
            col = slice(128 * m, 128 * m + 128)
            feat_t[col, at] = normed[:, col].T.astype(bf16)


def param_kernel(small, far, prm, heads):
    at_0 = lax.axis_index("zl") == 0
    lo = jnp.where(at_0, small[...], far[...])
    hi = jnp.where(at_0, far[...], small[...])
    prm[:, :HALF] = lo
    prm[:, HALF:] = hi
    lane = iota((1, 128), 1)

    def twelve(k):
        col = slice(128 * k, 128 * k + 128)
        return jnp.where(lane < 6, lo[6:7, col], pltpu.roll(hi[6:7, col], 6, 1))

    heads[...] = jnp.zeros_like(heads)
    heads[0:1, :] = jnp.where(lane < 12, jnp.exp(twelve(0)), 0.0)
    heads[1:2, :] = jnp.where(lane < 12, twelve(1), 0.0)
    skip = twelve(2)
    for i in range(PAIRS):
        pair = [jnp.broadcast_to(skip[:, 2 * i + k : 2 * i + k + 1], (1, 128)) for k in range(2)]
        prm[6:7, 128 * i : 128 * i + 128] = jnp.where(lane < 64, pair[0], pair[1])


def touch_kernel(*refs):
    pass


def proj_kernel(*refs):
    weights, (feat, w_out, wo_out, pre, w, wo, wsem, wosem, osem) = refs[:8], refs[8:]
    i = pl.program_id(0)
    outs = [
        pltpu.make_async_copy(w, w_out, osem.at[0]),
        pltpu.make_async_copy(wo, wo_out, osem.at[1]),
    ]

    @pl.when(i == 0)
    def _():
        for c in weight_copies(weights, 0, LEFT, w, wsem):
            c.start()
        for c in weight_copies(weights, LEFT, HALF, wo, wosem):
            c.start()
        wait_half(0, LEFT, w, wsem)

    @pl.when(i == 2)
    def _():
        wait_half(1, LEFT, w, wsem)
        outs[0].start()

    @pl.when(i == 3)
    def _():
        for g in range(2):
            wait_half(g, HALF, wo, wosem)
        outs[1].start()

    pre[...] = dot(feat[...], w[:, pl.ds(pl.multiple_of(512 * i, 512), 512)])

    @pl.when(i == pl.num_programs(0) - 1)
    def _():
        for c in outs:
            c.wait()


def pair_places(i):
    g, p = divmod(i, 3)
    return slice(128 * i, 128 * i + 128), g * LEFT + HALF + 128 * p


def step_sizes(pre, heads):
    raw = pre[:, 896:1024] + pre[:, LEFT + 896 : LEFT + 1024] + heads[1:2, :]
    return raw, softplus(raw)


def framed_inputs(s, zl, pre, prev, msg, vx, vs):
    for g in range(2):
        base = g * LEFT + HALF
        vx[8:264, g * HALF : (g + 1) * HALF] = pre[:, base : base + HALF]
        vs[8:264, g * N : (g + 1) * N] = pre[:, base + HALF : base + HALF + N]
        if s == 0:
            vx[0:8, g * HALF : (g + 1) * HALF] = jnp.zeros((8, HALF), f32)
            vs[0:8, g * N : (g + 1) * N] = jnp.zeros((8, N), f32)
            continue
        hx, hs = prev[:, base : base + HALF], prev[:, base + HALF : base + HALF + N]
        if s == 1:
            hx, hs = jnp.where(zl == 1, hx, 0.0), jnp.where(zl == 1, hs, 0.0)
        else:
            mx = msg[128:144, g * HALF : (g + 1) * HALF].astype(f32)[:8]
            ms = msg[144:160, g * N : (g + 1) * N].astype(f32)[:8]
            hx, hs = jnp.where(zl == 0, hx, mx), jnp.where(zl == 0, hs, ms)
        vx[0:8, g * HALF : (g + 1) * HALF] = hx
        vs[0:8, g * N : (g + 1) * N] = hs


def fwd_kernel(s, *refs):
    refs = list(refs)
    pre = refs.pop(0)
    rows_here = pl.ds(STEP * s, STEP)
    prev = pre.at[pl.ds(STEP * s - 8, 8)] if s else None
    pre = pre.at[rows_here]
    h_in = refs.pop(0) if s else None
    msg = refs.pop(0) if s == 2 else None
    prm, prs, heads = refs[:3]
    refs = refs[3:]
    refs = refs[len(refs) - (5 if s == 0 else 4) :]
    act, hs = refs[:2]
    act = act.at[rows_here]
    refs = refs[2:]
    out_msg = refs.pop(0) if s == 0 else None
    vx, vs = refs
    zl = lax.axis_index("zl")
    framed_inputs(s, zl, pre, prev, msg, vx, vs)
    if s == 0:
        hs[0] = jnp.zeros((N, CH), f32)
    elif s == 1:
        hs[0] = jnp.where(zl == 1, h_in[2], 0.0)
    else:
        hs[0] = jnp.where(zl == 0, h_in[2], msg[0:128, :].astype(f32))
    _, dt_all = step_sizes(pre, heads)
    a_all = -heads[0:1, :] * dt_all
    sub, lane = iota((Q, 128), 0), iota((Q, 128), 1)
    low_mask = sub >= lane
    tri = jnp.where(low_mask, 1.0, 0.0).astype(bf16)
    left = lane < 64
    for j in range(2):
        r0 = Q * j
        bc = []
        for g in range(2):
            col = slice(g * N, (g + 1) * N)
            cs = prs[4:5, col] + sum(
                prs[k : k + 1, col] * vs[5 + k + r0 : 5 + k + r0 + Q, col] for k in range(4)
            )
            act[r0 : r0 + Q, 2 * CH + g * N : 2 * CH + (g + 1) * N] = cs
            bc.append((cs * jax.nn.sigmoid(cs)).astype(bf16))
        b, c = bc
        bt = b.astype(f32).T.astype(bf16)
        scores = dot_nt(c, b)
        dt = dt_all[r0 : r0 + Q]
        cum = tri_dot(tri, a_all[r0 : r0 + Q])
        cum_t = cum.T
        for i in range(PAIRS):
            col, _ = pair_places(i)
            cx = prm[4:5, col] + sum(
                prm[k : k + 1, col] * vx[5 + k + r0 : 5 + k + r0 + Q, col] for k in range(4)
            )
            act[r0 : r0 + Q, CH + 128 * i : CH + 128 * i + 128] = cx
            x = (cx * jax.nn.sigmoid(cx)).astype(bf16).astype(f32)
            c0, c1 = lanes_of(cum, 2 * i), lanes_of(cum, 2 * i + 1)
            m0 = scores * jnp.exp(jnp.where(low_mask, c0 - cum_t[2 * i : 2 * i + 1, :], NEG))
            m1 = scores * jnp.exp(jnp.where(low_mask, c1 - cum_t[2 * i + 1 : 2 * i + 2, :], NEG))
            cp = jnp.where(left, c0, c1)
            xdt = x * jnp.where(left, lanes_of(dt, 2 * i), lanes_of(dt, 2 * i + 1))
            xdtb = xdt.astype(bf16)
            zero = jnp.zeros_like(xdtb)
            last = cp[Q - 1 : Q, :]
            inside = dot(
                jnp.concatenate([m0.astype(bf16), m1.astype(bf16)], axis=1),
                jnp.concatenate([jnp.where(left, xdtb, zero), jnp.where(left, zero, xdtb)], axis=0),
            )
            h = hs[j, :, col]
            y = inside + jnp.exp(cp) * dot(c, h.astype(bf16)) + prm[6:7, col] * x
            act[r0 : r0 + Q, col] = y
            hs[j + 1, :, col] = h * jnp.exp(last) + dot(bt, (xdt * jnp.exp(last - cp)).astype(bf16))
    if s == 0:
        out_msg[0:128, :] = hs[2].astype(bf16)
        out_msg[128:144, :] = jnp.concatenate([vx[256:264, :]] * 2, axis=0).astype(bf16)
        out_msg[144:160, :] = jnp.concatenate(
            [jnp.concatenate([vs[256:264, :]] * 2, axis=0), jnp.zeros((16, CH - 2 * N), f32)], axis=1
        ).astype(bf16)


def cot_kernel(*refs):
    rows, (w, z0, z1, ssd, prm, cot_out, gm, gb, sums, cot, rsem, osem) = refs[:5], refs[5:]
    i = pl.program_id(0)
    out = pltpu.make_async_copy(cot, cot_out, osem.at[0])

    @pl.when(i == 0)
    def _():
        cs = row_copies(rows, cot, rsem)
        for c in cs:
            c.start()
        for c in cs:
            c.wait()
        out.start()

    at = pl.ds(pl.multiple_of(STEP * i, STEP), STEP)
    grad = dot(cot[at, :], w[...])
    gm[...] = grad
    squares = jnp.zeros((STEP, 1), f32)
    dots = jnp.zeros((STEP, 1), f32)
    for g, z in ((0, z0), (1, z1)):
        col = slice(g * HALF, (g + 1) * HALF)
        gate = z[:, 0:HALF]
        gated = ssd[:, col] * (gate * jax.nn.sigmoid(gate))
        scaled = gated * prm[5:6, col]
        gb[:, col] = scaled.astype(bf16)
        squares = squares + jnp.sum(gated * gated, axis=1, keepdims=True)
        dots = dots + jnp.sum(grad[:, col] * scaled, axis=1, keepdims=True)
    lane = iota((STEP, 128), 1)
    both = jnp.where(lane == 0, squares, jnp.where(lane == 1, dots, 0.0))
    sums[...] = both.T[0:8, :]

    @pl.when(i == pl.num_programs(0) - 1)
    def _():
        out.wait()


def store_rows(i, value, outs):
    own, up, down, one, two = outs
    me = here()
    for g in range(4):
        natural = lax.rem(4 * i + g + 8 - 4 * me["zl"] + 12, 12)
        rel = lax.rem(natural // 3 - me["x"] + 4, 4)
        at = pl.ds(pl.multiple_of(64 * lax.rem(natural, 3), 64), 64)
        rows = slice(64 * g, 64 * g + 64)
        for k, out in ((0, own), (1, up), (3, down)):

            @pl.when(rel == k)
            def _(out=out, rows=rows, at=at):
                out[at, :] = value[rows, :]

        @pl.when(rel == 2)
        def _(rows=rows, at=at):
            one[at, :] = value[rows, :CH]
            two[at, :] = value[rows, CH:]


def add(a, b):
    return (a.astype(f32) + b.astype(f32)).astype(bf16)


def row_middle_kernel(up, down, one, two, *refs):
    up_out, down_out = refs[-2:]
    up_out[:, :CH] = add(up[:, :CH], one[...])
    up_out[:, CH:] = up[:, CH:]
    down_out[:, :CH] = down[:, :CH]
    down_out[:, CH:] = add(down[:, CH:], two[...])


def out_kernel(gb, w, *outs):
    store_rows(pl.program_id(0), dot_nt(gb[...], w[...]).astype(bf16), outs)


def gate_kernel(s0, s1, s2, s3, gm, ssd, z0, z1, prm, *refs):
    dssd, lowz, mixed, ggain = refs[-4:]
    i = pl.program_id(0)
    total = (s0[...] + s1[...] + s2[...] + s3[...]).T
    inv = lax.rsqrt(total[:, 0:1] / DI + EPS)
    pull = inv * inv * inv * (total[:, 1:2] / DI)

    @pl.when(i == 0)
    def _():
        ggain[...] = jnp.zeros_like(ggain)

    for g, z in ((0, z0), (1, z1)):
        col = slice(g * HALF, (g + 1) * HALF)
        gate = z[:, 0:HALF]
        sig = jax.nn.sigmoid(gate)
        silu = gate * sig
        y = ssd[:, col]
        gated = y * silu
        grad = gm[:, col]
        gain = prm[5:6, col]
        normal = gated * inv
        mixed[:, col] = (normal * gain).astype(bf16)
        dg = grad * gain * inv - gated * pull
        dssd[:, col] = (dg * silu).astype(bf16)
        lowz[:, col] = (dg * y * (sig * (1.0 + gate * (1.0 - sig)))).astype(bf16)
        part = jnp.sum(grad * normal, axis=0, keepdims=True)
        ggain[:, col] += jnp.where(iota((8, HALF), 0) == 0, part, 0.0)


def send_tiles(buf, own, far, sem):
    me = here()
    m = pl.program_id(0)
    z0 = 2 * me["zh"] + me["zl"]
    for core in range(2):

        @pl.when(me["c"] == core)
        def _(core=core):
            for k in range(4):
                dy = lax.rem(lax.rem(2 * m + k // 2, 4) - me["y"] + 4, 4)
                for g in range(2):
                    dz = lax.rem(2 * (m // 2) + g - z0 + 4, 4)
                    at = 4 * dz + dy if k % 2 == 0 else 4 * dy + dz
                    pltpu.make_async_copy(
                        buf.at[pl.ds(pl.multiple_of(384 * m + 96 * k, 96), 96), pl.ds(g * CH, CH)],
                        (own if k % 2 == core else far).at[pl.ds(pl.multiple_of(96 * at, 96), 96)],
                        sem.at[m],
                    ).start()


def row_gain(part, w):
    lanes = sum(part[:, k : k + 128] * w[:, k : k + 128].astype(f32) for k in range(0, part.shape[1], 128))
    ones = jnp.ones((8, 128), bf16)
    hi, lo = halves(lanes)
    return dot_nt(ones, hi) + dot_nt(ones, lo)


def wait_tiles(own, sem):
    for m in range(4):
        block = own.at[pl.ds(0, ROWS)]
        pltpu.make_async_copy(block, block, sem.at[m]).wait()


def early_kernel(feat_t, cot, lowz, mixed, w, own, far, gains, buf, sem):
    m = pl.program_id(0)
    rows = pl.ds(pl.multiple_of(384 * m, 384), 384)
    part = dot(feat_t[...], lowz[...])
    out = dot_tn(cot[...], mixed[...]).astype(bf16)
    low = part.astype(bf16)
    for g in range(2):
        col = slice(g * HALF, (g + 1) * HALF)
        buf[rows, g * CH : g * CH + HALF] = low[:, col]
        buf[rows, g * CH + HALF : (g + 1) * CH] = out[:, col]
    send_tiles(buf, own, far, sem)
    gains[...] = row_gain(part, jnp.concatenate([w[:, :HALF], w[:, LEFT : LEFT + HALF]], axis=1))

    @pl.when(m == 3)
    def _():
        wait_tiles(own, sem)


def late_kernel(feat_t, low, w, gains_in, acc, accs, ggain, *refs):
    own, far, small, buf, gains, tail, sem, tail_sem = refs[-8:]
    m = pl.program_id(0)
    rows = pl.ds(pl.multiple_of(384 * m, 384), 384)
    both = w[:, LEFT - N : LEFT].astype(f32) + w[:, 2 * LEFT - N :].astype(f32)
    rhs = jnp.concatenate(
        [low[:, HALF:LEFT], low[:, LEFT + HALF : LEFT + CH], low[:, LEFT + CH : LEFT + CH + N]], axis=1
    )
    taps = jnp.concatenate(
        [w[:, HALF : CH + N], both.astype(bf16), w[:, LEFT + HALF : LEFT + CH], w[:, LEFT + CH : LEFT + CH + N]],
        axis=1,
    )
    part = dot(feat_t[...], rhs)
    low_part = part.astype(bf16)
    shared = jnp.concatenate([low_part[:, HALF : HALF + 2 * N], low_part[:, 1024:1152]], axis=1)
    buf[rows, 0:HALF] = low_part[:, 0:HALF]
    buf[rows, CH : CH + HALF] = low_part[:, 640:1024]
    for g in range(2):
        buf[rows, g * CH + HALF : (g + 1) * CH] = shared
    send_tiles(buf, own, far, sem)
    gain = gains_in[...] + row_gain(part, taps)
    gains[m] = gain

    @pl.when(m == 3)
    def _():
        small[...] = jnp.zeros_like(small)
        small[0:6, :] = acc[0:6, :]
        small[6:7, :] = ggain[0:1, :]
        small[8:9, :] = jnp.concatenate([gains[0, 0:1, :], gains[1, 0:1, :]], axis=1)
        small[9:10, :] = jnp.concatenate([gains[2, 0:1, :], gains[3, 0:1, :]], axis=1)
        for row, rs in ((7, (5, 6)), (10, (0, 1, 2)), (11, (3, 4))):
            for k, r in enumerate(rs):
                small[row : row + 1, 256 * k : 256 * k + 256] = accs[r : r + 1, :]
        tail[...] = split_small(small[...])
        copy = pltpu.make_async_copy(tail, far.at[pl.ds(2 * ROWS, 32)], tail_sem.at[0])
        copy.start()
        wait_tiles(own, sem)
        copy.wait()


def split_small(total):
    return jnp.concatenate(halves(total), axis=0)


def sum_small(block):
    return block[:16].astype(f32) + block[16:].astype(f32)


def core_sum_kernel(with_small, *refs):
    own, far = refs[:2]
    outs = refs[-5:]
    if with_small:
        small = split_small(refs[2][...] + sum_small(far[2 * ROWS : 2 * ROWS + 32, :]))
    for out, first, count in zip(outs, (0, 384, 1152, 768, 960), (384, 384, 384, 192, 192)):
        rows = slice(first, first + count)
        out[0:count, :] = add(own[rows, :], far[rows, :])
        if with_small:
            out[count : count + 32, :] = small


def tile_middle_kernel(with_small, up, down, one, two, *refs):
    outs = refs[-3:] if with_small else refs[-2:]
    up_out, down_out = outs[:2]
    up_out[0:192, :] = add(up[0:192, :], one[0:192, :])
    up_out[192:384, :] = up[192:384, :]
    down_out[0:192, :] = down[0:192, :]
    down_out[192:384, :] = add(down[192:384, :], two[0:192, :])
    if with_small:
        up_out[384:416, :] = one[192:224, :]
        down_out[384:416, :] = down[384:416, :]
        outs[2][...] = split_small(sum_small(one[192:224, :]) + sum_small(two[192:224, :]))


def axis_sum_kernel(*refs):
    early, late, near, outs = refs[:3], refs[3:6], refs[6], refs[-4:]
    own, up = late[:2]
    small = split_small(sum_small(own[384:416, :]) + sum_small(up[384:416, :]) + sum_small(near[...]))
    for k, out in enumerate(outs):
        rows = slice(96 * k, 96 * k + 96)
        out[0:96, :] = add3([t[rows, :] for t in early]).astype(bf16)
        out[96:192, :] = add3([t[rows, :] for t in late]).astype(bf16)
        out[192:224, :] = small


def last_sum_kernel(*refs):
    terms, (early, tile, small, to_x) = refs[:4], refs[-4:]
    early[...] = add4([t[0:96, :] for t in terms])
    total = add4([t[96:192, :] for t in terms])
    tile[...] = total
    every = sum(sum_small(t[192:224, :]) for t in terms)
    small[...] = every
    for k in range(3):
        rows = slice(32 * k, 32 * k + 32)
        to_x[0:32, 256 * k : 256 * k + 128] = total[rows, HALF : HALF + N].astype(bf16)
        to_x[0:32, 256 * k + 128 : 256 * k + 256] = total[rows, HALF + 2 * N : HALF + 3 * N].astype(bf16)
    hi, lo = halves(every[8:16, :])
    to_x[32:48, :] = jnp.concatenate([hi.astype(f32), lo.astype(f32)], axis=0).astype(bf16)


def x_sum_kernel(a, b, c, d, gain, *refs):
    state, g_gain, g_conv, g_bias = refs[-4:]
    total = add4([a[...], b[...], c[...], d[...]])
    for k in range(3):
        state[32 * k : 32 * k + 32, :] = total[0:32, 256 * k : 256 * k + 256]
    small = total[32:40, :] + total[40:48, :]
    g_gain[:, :CH] = small[0:1, :] / gain[:, :CH]
    g_gain[:, CH:] = small[1:2, :] / gain[:, CH:]
    for k in range(3):
        g_conv[k : k + 1, :] = small[2:3, 256 * k : 256 * k + 256]
    g_conv[3:4, :] = small[3:4, 0:256]
    g_bias[...] = small[3:4, 256:512]


def bwd_kernel(s, *refs):
    refs = list(refs)
    pre = refs.pop(0)
    rows_here = pl.ds(STEP * s, STEP)
    prev = pre.at[pl.ds(STEP * s - 8, 8)] if s else None
    msg = refs.pop(0) if s == 2 else None
    act, hs, dssd, lowz, prm, prs, heads = refs[:7]
    pre, act, dssd, lowz = (ref.at[rows_here] for ref in (pre, act, dssd, lowz))
    refs = refs[7:]
    if s < 2:
        dh_in, tail, acc_in, accs_in = refs[:4]
        refs = refs[4:]
        back = refs.pop(0) if s == 0 else None
    refs = refs[len(refs) - (10 if s == 2 else 9) :]
    low, dh, head_rows, acc, accs = refs[:5]
    low = low.at[rows_here]
    refs = refs[5:]
    for g in range(2):
        low[:, g * LEFT : g * LEFT + HALF] = lowz[:, g * HALF : (g + 1) * HALF]
    out_msg = refs.pop(0) if s == 2 else None
    vx, vs, dp, ds = refs
    zl = lax.axis_index("zl")
    framed_inputs(s, zl, pre, prev, msg, vx, vs)
    if s == 2:
        dh[...] = jnp.zeros_like(dh)
        dp[256:264, :] = jnp.zeros((8, CH), f32)
        ds[256:264, :] = jnp.zeros((8, 2 * N), f32)
        acc[...] = jnp.zeros_like(acc)
        accs[...] = jnp.zeros_like(accs)
    else:
        hd, hp, hq = dh_in[...], tail[0:8, :], tail[8:16, 0 : 2 * N]
        if s == 1:
            hd, hp, hq = (jnp.where(zl == 0, v, 0.0) for v in (hd, hp, hq))
        else:
            hd = jnp.where(zl == 1, hd, back[0:128, :].astype(f32))
            hp = jnp.where(zl == 1, hp, back[128:144, :].astype(f32)[:8])
            hq = jnp.where(zl == 1, hq, back[144:160, 0 : 2 * N].astype(f32)[:8])
        dh[...], dp[256:264, :], ds[256:264, :] = hd, hp, hq
        acc[...] = acc_in[...]
        accs[...] = accs_in[...]
    raw_all, dt_all = step_sizes(pre, heads)
    rate = heads[0:1, :]
    a_all = -rate * dt_all
    sub, lane = iota((Q, 128), 0), iota((Q, 128), 1)
    tri = jnp.where(sub >= lane, 1.0, 0.0).astype(bf16)
    up_mask = lane >= sub
    tri_up = jnp.where(up_mask, 1.0, 0.0).astype(bf16)
    below = jnp.where(lane < sub, 1.0, 0.0).astype(bf16)
    left = lane < 64
    for j in (1, 0):
        r0 = Q * j
        rows = slice(r0, r0 + Q)
        pre_s = [act[rows, 2 * CH + g * N : 2 * CH + (g + 1) * N] for g in range(2)]
        sig_s = [jax.nn.sigmoid(v) for v in pre_s]
        bf, cf = [(v * w).astype(bf16).astype(f32) for v, w in zip(pre_s, sig_s)]
        b, c = bf.astype(bf16), cf.astype(bf16)
        ct = cf.T.astype(bf16)
        scores_t = dot_nt(c, b).T
        dt, a = dt_all[rows], a_all[rows]
        cum = tri_dot(tri, a)
        cum_t = cum.T
        d_scores_t = jnp.zeros((Q, Q), f32)
        d_b = jnp.zeros((Q, N), f32)
        d_c = jnp.zeros((Q, N), f32)
        per_head = jnp.zeros((3 * Q, 128), f32)
        for i in range(PAIRS):
            col, _ = pair_places(i)
            cx = act[rows, CH + 128 * i : CH + 128 * i + 128]
            sig = jax.nn.sigmoid(cx)
            x = (cx * sig).astype(bf16).astype(f32)
            dyb = dssd[rows, col]
            dy = dyb.astype(f32)
            skip = prm[6:7, col]
            c0, c1 = lanes_of(cum, 2 * i), lanes_of(cum, 2 * i + 1)
            l0 = jnp.exp(jnp.where(up_mask, cum_t[2 * i : 2 * i + 1, :] - c0, NEG))
            l1 = jnp.exp(jnp.where(up_mask, cum_t[2 * i + 1 : 2 * i + 2, :] - c1, NEG))
            cp = jnp.where(left, c0, c1)
            dtp = jnp.where(left, lanes_of(dt, 2 * i), lanes_of(dt, 2 * i + 1))
            last = cp[Q - 1 : Q, :]
            fade = jnp.exp(last - cp)
            xdt = x * dtp
            xdtb = xdt.astype(bf16)
            zero = jnp.zeros_like(xdtb)
            dy_split = jnp.concatenate([jnp.where(left, dyb, zero), jnp.where(left, zero, dyb)], axis=0)
            x_split = jnp.concatenate([jnp.where(left, xdtb, zero), jnp.where(left, zero, xdtb)], axis=0)
            dhp = dh[:, col]
            dhb = dhp.astype(bf16)
            m_t = jnp.concatenate([(scores_t * l0).astype(bf16), (scores_t * l1).astype(bf16)], axis=1)
            inside = dot(m_t, dy_split)
            beyond = fade * dot(b, dhb)
            dxdt = inside + beyond
            dx = dxdt * dtp + skip * dy
            acc[5:6, col] += jnp.sum(dy * x, axis=0, keepdims=True)
            d_m_t = dot_nt(x_split, dyb)
            d_scores_t = d_scores_t + d_m_t[:Q] * l0 + d_m_t[Q:] * l1
            h = hs[j, :, col]
            crossing = jnp.sum(dhp * h, axis=0, keepdims=True) * jnp.exp(last)
            t1 = dxdt * x
            t2 = dy * (act[rows, col] - skip * x) - xdtb.astype(f32) * inside
            t2 = t2 + jnp.where(sub == Q - 1, crossing, 0.0)
            t3 = xdt * beyond
            pick = (lane == jnp.where(sub < 64, 2 * i, 2 * i + 1)).astype(f32).astype(bf16)
            hi, lo = halves(jnp.concatenate([t1, t2, t3], axis=0))
            per_head = per_head + dot(
                jnp.concatenate([hi, lo], axis=1), jnp.concatenate([pick, pick], axis=0)
            )
            dye = (dy * jnp.exp(cp)).astype(bf16)
            d_c = d_c + dot_nt(dye, h.astype(bf16))
            d_b = d_b + dot_nt((xdt * fade).astype(bf16), dhb)
            dh[:, col] = dhp * jnp.exp(last) + dot(ct, dye)
            dp[rows, col] = dx * (sig * (1.0 + cx * (1.0 - sig)))
        d_b = d_b + dot(d_scores_t.astype(bf16), c)
        d_c = d_c + dot(d_scores_t.T.astype(bf16), b)
        for g, grad in ((0, d_b), (1, d_c)):
            ds[rows, g * N : (g + 1) * N] = grad * (sig_s[g] * (1.0 + pre_s[g] * (1.0 - sig_s[g])))
        da = tri_dot(tri_up, per_head[Q : 2 * Q]) + tri_dot(below, per_head[2 * Q :])
        ddt = per_head[:Q] - rate * da
        dstep = ddt * jax.nn.sigmoid(raw_all[rows])
        accs[5:6, 0:128] += jnp.sum(a * da, axis=0, keepdims=True)
        accs[6:7, 0:128] += jnp.sum(dstep, axis=0, keepdims=True)
        for g in range(2):
            low[rows, (g + 1) * LEFT - N : (g + 1) * LEFT] = dstep.astype(bf16)
    for frame, grads, taps, out, width in ((vx, dp, prm, acc, CH), (vs, ds, prs, accs, 2 * N)):
        for i in range(width // 128):
            col = slice(128 * i, 128 * i + 128)
            g, p = divmod(i, width // 256)
            to = g * LEFT + HALF + 128 * p + (HALF if width == 2 * N else 0)
            back_v = sum(taps[k : k + 1, col] * grads[3 - k : 3 - k + STEP, col] for k in range(4))
            low[:, to : to + 128] = back_v.astype(bf16)
            own = grads[0:STEP, col]
            for k in range(4):
                out[k : k + 1, col] += jnp.sum(own * frame[5 + k : 5 + k + STEP, col], axis=0, keepdims=True)
            out[4:5, col] += jnp.sum(own, axis=0, keepdims=True)
    head_rows[0:8, :] = dp[0:8, :]
    head_rows[8:16, :] = jnp.concatenate([ds[0:8, :], jnp.zeros((8, CH - 2 * N), f32)], axis=1)
    if s == 2:
        out_msg[0:128, :] = dh[...].astype(bf16)
        out_msg[128:144, :] = jnp.concatenate([head_rows[0:8, :]] * 2, axis=0).astype(bf16)
        out_msg[144:160, :] = jnp.concatenate([head_rows[8:16, :]] * 2, axis=0).astype(bf16)


def feat_kernel(low, w, *refs):
    store_rows(pl.program_id(0), dot_nt(low[...], w[...]).astype(bf16), refs[-5:])


ANY = pl.BlockSpec(memory_space=pl.ANY)
VM = pl.BlockSpec(memory_space=pltpu.VMEM)


def params(mib):
    return pltpu.CompilerParams(vmem_limit_bytes=mib * 1024 * 1024)


def shape(*s, dtype=f32):
    return jax.ShapeDtypeStruct(s, dtype)


def cost(flops, moved_bytes):
    return pl.CostEstimate(flops=int(flops), bytes_accessed=int(moved_bytes), transcendentals=0)


def steps(width, column=0):
    return pl.BlockSpec((STEP, width), lambda i: (i, column))


def line_up(parts, deps):
    return pl.pallas_call(
        line_kernel,
        in_specs=[VM] * 4 + [ANY] * len(deps),
        out_specs=VM,
        out_shape=shape(384, FULL, dtype=bf16),
        compiler_params=params(4),
        cost_estimate=cost(1e6, 2e6),
        name="line_up",
    )(*parts, *deps)


def touch(a, deps):
    return pl.pallas_call(
        touch_kernel,
        in_specs=[ANY] * (1 + len(deps)),
        out_specs=ANY,
        out_shape=jax.ShapeDtypeStruct(a.shape, a.dtype),
        input_output_aliases={0: 0},
        compiler_params=params(1),
        cost_estimate=cost(1, 1),
        name="touch",
    )(a, *deps)


def normalize(rows, gain):
    return pl.pallas_call(
        norm_kernel,
        in_specs=[ANY] * 4 + [VM],
        out_specs=[VM, VM],
        out_shape=[shape(ROWS, D, dtype=bf16), shape(D, ROWS, dtype=bf16)],
        scratch_shapes=[pltpu.VMEM((ROWS, D), bf16), pltpu.SemaphoreType.DMA((N_ROW_COPIES,))],
        compiler_params=params(12),
        cost_estimate=cost(1e7, 5e6),
        name="normalize",
    )(*rows, gain)


def project(feat, weights):
    return pl.pallas_call(
        proj_kernel,
        grid=(4,),
        in_specs=[ANY] * 8 + [VM],
        out_specs=[ANY, ANY, pl.BlockSpec((ROWS, 512), lambda i: (0, i))],
        out_shape=[shape(D, 2 * LEFT, dtype=bf16), shape(D, CH, dtype=bf16), shape(ROWS, 2 * LEFT)],
        scratch_shapes=[
            pltpu.VMEM((D, 2 * LEFT), bf16),
            pltpu.VMEM((D, CH), bf16),
            pltpu.SemaphoreType.DMA((2,)),
            pltpu.SemaphoreType.DMA((2,)),
            pltpu.SemaphoreType.DMA((2,)),
        ],
        compiler_params=params(16),
        cost_estimate=cost(2 * ROWS * D * 2 * LEFT, 24e6),
        name="project",
    )(*weights, feat)


def forward(s, pre, act, h, msg, prm, prs, heads):
    ins = [pre] + ([h] if s else []) + ([msg] if s == 2 else []) + [prm, prs, heads]
    aliases = {}
    if s:
        aliases = {len(ins): 0}
        ins += [act]
    outs = [shape(ROWS, 2 * CH + 2 * N), shape(3, N, CH)]
    if s == 0:
        outs += [shape(160, CH, dtype=bf16)]
    return pl.pallas_call(
        functools.partial(fwd_kernel, s),
        in_specs=[VM] * len(ins),
        out_specs=[VM] * len(outs),
        out_shape=outs,
        input_output_aliases=aliases,
        scratch_shapes=[pltpu.VMEM((264, CH), f32), pltpu.VMEM((264, 2 * N), f32)],
        compiler_params=params(6),
        cost_estimate=cost(1.5e9, 6e6),
        name=f"scan_rows_{s}",
    )(*ins)


def cotangent(rows, w, pre, act, prm):
    return pl.pallas_call(
        cot_kernel,
        grid=(3,),
        in_specs=[ANY] * 5 + [VM, steps(512, 0), steps(512, 2), steps(CH), VM],
        out_specs=[ANY, steps(CH), steps(CH), pl.BlockSpec((8, STEP), lambda i: (0, i))],
        out_shape=[
            shape(ROWS, D, dtype=bf16),
            shape(ROWS, CH),
            shape(ROWS, CH, dtype=bf16),
            shape(8, ROWS),
        ],
        scratch_shapes=[
            pltpu.VMEM((ROWS, D), bf16),
            pltpu.SemaphoreType.DMA((N_ROW_COPIES,)),
            pltpu.SemaphoreType.DMA((1,)),
        ],
        compiler_params=params(14),
        cost_estimate=cost(2 * ROWS * D * CH, 20e6),
        name="cotangent",
    )(*rows, w, pre, pre, act, prm)


def out_partial(gb, w):
    return pl.pallas_call(
        out_kernel,
        grid=(3,),
        in_specs=[steps(CH), VM],
        out_specs=[VM] * 3 + [VM] * 2,
        out_shape=[shape(192, D, dtype=bf16)] * 3 + [shape(192, CH, dtype=bf16)] * 2,
        compiler_params=params(6),
        cost_estimate=cost(2 * ROWS * D * CH, 6e6),
        name="out_partial",
    )(gb, w)


def gate_back(sums, gm, act, pre, prm, deps):
    row = pl.BlockSpec((8, STEP), lambda i: (0, i))
    return pl.pallas_call(
        gate_kernel,
        grid=(3,),
        in_specs=[row] * 4
        + [steps(CH), steps(CH), steps(512, 0), steps(512, 2), VM]
        + [ANY] * len(deps),
        out_specs=[steps(CH), steps(CH), steps(CH), VM],
        out_shape=[shape(ROWS, CH, dtype=bf16)] * 3 + [shape(8, CH)],
        compiler_params=params(11),
        cost_estimate=cost(1e7, 12e6),
        name="gate_back",
    )(*sums, gm, act, pre, pre, prm, *deps)


def early_grads(feat_t, cot, lowz, mixed, w):
    return pl.pallas_call(
        early_kernel,
        grid=(4,),
        in_specs=[
            pl.BlockSpec((HALF, ROWS), lambda m: (m, 0)),
            pl.BlockSpec((ROWS, HALF), lambda m: (0, m)),
            VM,
            VM,
            pl.BlockSpec((HALF, 2 * LEFT), lambda m: (m, 0)),
        ],
        out_specs=[ANY, ANY, pl.BlockSpec((8, HALF), lambda m: (0, m))],
        out_shape=[shape(2 * ROWS, CH, dtype=bf16)] * 2 + [shape(8, D)],
        scratch_shapes=[pltpu.VMEM((D, 2 * CH), bf16), pltpu.SemaphoreType.DMA((4,))],
        compiler_params=params(14),
        cost_estimate=cost(2 * ROWS * D * 2 * CH, 12e6),
        name="early_grads",
    )(feat_t, cot, lowz, mixed, w)


def late_grads(feat_t, low, w, gains, acc, accs, ggain, deps):
    return pl.pallas_call(
        late_kernel,
        grid=(4,),
        in_specs=[
            pl.BlockSpec((HALF, ROWS), lambda m: (m, 0)),
            VM,
            pl.BlockSpec((HALF, 2 * LEFT), lambda m: (m, 0)),
            pl.BlockSpec((8, HALF), lambda m: (0, m)),
            VM,
            VM,
            VM,
        ]
        + [ANY] * len(deps),
        out_specs=[ANY, ANY, VM],
        out_shape=[shape(2 * ROWS, CH, dtype=bf16), shape(2 * ROWS + 32, CH, dtype=bf16), shape(16, CH)],
        scratch_shapes=[
            pltpu.VMEM((D, 2 * CH), bf16),
            pltpu.VMEM((4, 8, HALF), f32),
            pltpu.VMEM((32, CH), bf16),
            pltpu.SemaphoreType.DMA((4,)),
            pltpu.SemaphoreType.DMA((1,)),
        ],
        compiler_params=params(14),
        cost_estimate=cost(2 * ROWS * D * 3 * HALF, 12e6),
        name="late_grads",
    )(feat_t, low, w, gains, acc, accs, ggain, *deps)


def tile_sums(kernel, ins, outs, deps, name, mib=6):
    return pl.pallas_call(
        kernel,
        in_specs=[VM] * len(ins) + [ANY] * len(deps),
        out_specs=[VM] * len(outs),
        out_shape=outs,
        compiler_params=params(mib),
        cost_estimate=cost(1e6, 4e6),
        name=name,
    )(*ins, *deps)


def core_sum(own, far, small, deps, name):
    more = 32 if small else 0
    return tile_sums(
        functools.partial(core_sum_kernel, bool(small)),
        [own, far] + list(small),
        [shape(384 + more, CH, dtype=bf16)] * 3 + [shape(192 + more, CH, dtype=bf16)] * 2,
        deps,
        name,
        10,
    )


def row_middle(ins, deps):
    return tile_sums(row_middle_kernel, ins, [shape(192, D, dtype=bf16)] * 2, deps, "row_middle")


def tile_middle(with_small, ins, deps):
    outs = [shape(416 if with_small else 384, CH, dtype=bf16)] * 2
    if with_small:
        outs = outs + [shape(32, CH, dtype=bf16)]
    return tile_sums(functools.partial(tile_middle_kernel, with_small), ins, outs, deps, "tile_middle")


def backward(s, pre, msg, act, hs, dssd, lowz, prm, prs, heads, carried, back, low, deps):
    ins = [pre] + ([msg] if s == 2 else []) + [act, hs, dssd, lowz, prm, prs, heads]
    aliases = {}
    if s < 2:
        ins += list(carried)
        if s == 0:
            ins += [back]
        aliases = {len(ins): 0}
        ins += [low]
    outs = [shape(ROWS, 2 * LEFT, dtype=bf16), shape(N, CH), shape(16, CH), shape(8, CH), shape(8, 2 * N)]
    if s == 2:
        outs += [shape(160, CH, dtype=bf16)]
    return pl.pallas_call(
        functools.partial(bwd_kernel, s),
        in_specs=[VM] * len(ins) + [ANY] * len(deps),
        out_specs=[VM] * len(outs),
        out_shape=outs,
        input_output_aliases=aliases,
        scratch_shapes=[
            pltpu.VMEM((264, CH), f32),
            pltpu.VMEM((264, 2 * N), f32),
            pltpu.VMEM((264, CH), f32),
            pltpu.VMEM((264, 2 * N), f32),
        ],
        compiler_params=params(8),
        cost_estimate=cost(4e9, 8e6),
        name=f"scan_back_{s}",
    )(*ins, *deps)


def feat_partial(low, w, deps):
    return pl.pallas_call(
        feat_kernel,
        grid=(3,),
        in_specs=[steps(2 * LEFT), VM] + [ANY] * len(deps),
        out_specs=[VM] * 3 + [VM] * 2,
        out_shape=[shape(192, D, dtype=bf16)] * 3 + [shape(192, CH, dtype=bf16)] * 2,
        compiler_params=params(8),
        cost_estimate=cost(2 * ROWS * D * 2 * LEFT, 16e6),
        name="feat_partial",
    )(low, w, *deps)


def local(
    layer_input,
    input_gain,
    proj_inner,
    proj_step,
    proj_state,
    proj_output,
    conv_inner,
    conv_inner_bias,
    conv_state,
    conv_state_bias,
    inner_gain,
    decay_log,
    step_bias,
    skip_gain,
    out_cotangent,
):
    zl = lax.axis_index("zl")
    step_cols = jnp.where(
        zl == 0, jnp.pad(proj_step, ((0, 0), (0, 122))), jnp.pad(proj_step, ((0, 0), (6, 116)))
    )
    state_cols = jnp.where(zl == 0, proj_state[:, :N], proj_state[:, N:])
    shard = jnp.concatenate(
        [proj_inner[:, 0], proj_inner[:, 1], state_cols, step_cols, proj_output.T], axis=1
    )
    near = spread(shard, "first")

    coef = jnp.pad(jnp.stack([decay_log, step_bias, skip_gain]), ((0, 0), (0, 122))).reshape(1, HALF)
    small = jnp.concatenate(
        [touch(conv_inner, (near[0],)), conv_inner_bias[None], inner_gain[None], coef, jnp.zeros((1, HALF), f32)], axis=0
    )
    prm, heads = pl.pallas_call(
        param_kernel,
        in_specs=[VM, VM],
        out_specs=[VM, VM],
        out_shape=[shape(8, CH), shape(8, 128)],
        compiler_params=params(1),
        cost_estimate=cost(1, 1),
        name="parameters",
    )(small, send(small, "zl", 1))
    prs = jnp.concatenate([conv_state, conv_state_bias[None], jnp.zeros((3, 2 * N), f32)], axis=0)

    rows = (layer_input,) + spread(layer_input, "x")
    line = line_up((shard,) + near, (rows[1], rows[3], prm, heads, prs))
    far = spread(line, "second")
    first = touch(far[0], (rows[2],))
    feat, feat_t = normalize(rows, input_gain[None])
    third = touch(far[2], (feat,))
    mine = (line, first, far[1], third)
    weights = mine + tuple(send(a, "c", 1) for a in mine)
    w_in, w_o, pre = project(feat, weights)
    below, above = send(out_cotangent, "x", 1), send(out_cotangent, "x", 3)
    cot_rows = (out_cotangent, below, above, send(below[:, :CH], "x", 1), send(above[:, CH:], "x", 3))

    act, hs0, msg = forward(0, pre, None, None, None, prm, prs, heads)
    msg = send(msg, "zl", 1)
    act, hs1 = forward(1, pre, act, hs0, None, prm, prs, heads)
    act, hs2 = forward(2, pre, act, hs1, msg, prm, prs, heads)
    cot, gm, gb, sums = cotangent(cot_rows, w_o, pre, act, prm)
    all_sums = (sums,) + spread(sums, "x")
    parts = out_partial(gb, w_o)
    out_terms, (out_up,) = ring(parts, "x", row_middle)
    dssd, lowz, mixed, ggain = gate_back(all_sums, gm, act, pre, prm, (parts[0],))

    own, far, gains = early_grads(feat_t, cot, lowz, mixed, w_in)
    far = send(far, "c", 1)
    scan = (prm, prs, heads)
    low, *carried, back = backward(2, pre, msg, act, hs2, dssd, lowz, *scan, None, None, None, (own,))
    back = send(back, "zl", 1)
    parts = core_sum(own, far, (), (low,), "early_core_sum")
    early_terms, (early_up,) = ring(parts, "second", functools.partial(tile_middle, False))
    low, *carried = backward(1, pre, None, act, hs1, dssd, lowz, *scan, carried, None, low, (parts[0], out_up))
    deps = (early_up,)
    low, _, _, acc, accs = backward(0, pre, None, act, hs0, dssd, lowz, *scan, carried, back, low, deps)

    own, far, small = late_grads(feat_t, low, w_in, gains, acc, accs, ggain, out_terms[1:] + early_terms[1:])
    far = send(far, "c", 1)
    feat_parts = feat_partial(low, w_in, (own,))
    parts = core_sum(own, far, (small,), (feat_parts[0],), "late_core_sum")
    late_terms, (late_up, near) = ring(parts, "second", functools.partial(tile_middle, True))
    feat_terms, (feat_up,) = ring(feat_parts, "x", row_middle, (late_up,))
    parts = tile_sums(
        axis_sum_kernel,
        early_terms + late_terms + (near,),
        [shape(224, CH, dtype=bf16)] * 4,
        (),
        "axis_sum",
    )
    early, late, small, to_x = tile_sums(
        last_sum_kernel,
        deal(parts, "first"),
        [shape(96, CH), shape(96, CH), shape(16, CH), shape(48, CH, dtype=bf16)],
        (),
        "last_sum",
    )
    g_state, g_input_gain, g_conv_state, g_conv_state_bias = tile_sums(
        x_sum_kernel,
        (to_x,) + spread(to_x, "x") + (input_gain[None],),
        [shape(96, 2 * N), shape(1, D), shape(4, 2 * N), shape(1, 2 * N)],
        feat_terms[1:],
        "x_sum",
    )

    own = lambda a: jnp.where(zl == 0, a[..., :HALF], a[..., HALF:])
    six = lambda a: jnp.where(zl == 0, a[:6], a[6:12])
    conv = own(small[:7])
    g_skip = six(small[5].reshape(12, 64).sum(axis=1))
    g_decay, g_bias = six(small[7, :128]), six(small[7, 256:384])
    g_step = jnp.where(zl == 0, late[:, 512:518], late[:, 518:524])

    values = layer_input.astype(f32)
    squares = all_sums[0][0] + all_sums[1][0] + all_sums[2][0] + all_sums[3][0]
    at = lax.rem(192 * lax.axis_index("x") + 256 + 256 * zl, ROWS)
    squares = lax.dynamic_slice_in_dim(jnp.concatenate([squares, squares]), at, 192)
    scale = lax.rsqrt(squares / DI + EPS)[:, None]
    layer_output = (values + add3(out_terms) * scale).astype(bf16)
    inv = lax.rsqrt(jnp.mean(values * values, axis=1, keepdims=True) + EPS)
    weighted = add3(feat_terms) * input_gain
    input_grad = (
        out_cotangent.astype(f32)
        + weighted * inv
        - values * (inv * inv * inv) * jnp.mean(weighted * values, axis=1, keepdims=True)
    )
    return (
        layer_output,
        input_grad,
        g_input_gain[0],
        jnp.stack([early[:, :HALF], late[:, :HALF]], axis=1),
        g_step,
        g_state,
        early[:, HALF:].T,
        conv[:4],
        conv[4],
        g_conv_state,
        g_conv_state_bias[0],
        conv[6],
        g_decay,
        g_bias,
        g_skip,
    )


def solution(mesh):
    split = Mesh(mesh.devices.reshape(SIZES), AX)
    everything = FSDP + TP
    return jax.shard_map(
        local,
        mesh=split,
        in_specs=(
            P(everything, None),
            P(),
            P(FSDP, None, TP),
            P(FSDP, TP),
            P(FSDP, None),
            P(TP, FSDP),
            P(None, TP),
            P(TP),
            P(),
            P(),
            P(TP),
            P(TP),
            P(TP),
            P(TP),
            P(everything, None),
        ),
        out_specs=(
            P(everything, None),
            P(everything, None),
            P(),
            P(FSDP, None, TP),
            P(FSDP, TP),
            P(FSDP, None),
            P(TP, FSDP),
            P(None, TP),
            P(TP),
            P(),
            P(),
            P(TP),
            P(TP),
            P(TP),
            P(TP),
        ),
        check_vma=False,
    )
```

```python
import functools
import itertools

import jax
import jax.numpy as jnp
import numpy as np
from jax import lax
from jax.experimental import pallas as pl
from jax.experimental.pallas import tpu as pltpu
from jax.sharding import Mesh
from jax.sharding import PartitionSpec as P

D = 1536
DI = 3072
N = 128
Q = 128
STEP = 256
ROWS = 768
CH = 768
HALF = 384
PAIRS = 6
LEFT = 1024
FULL = LEFT + HALF
EPS = 1e-05
NEG = -1e30

AX = ("zh", "y", "c", "zl", "x")
SIZES = (2, 4, 2, 2, 4)
FSDP = ("zh", "y", "c")
TP = ("zl", "x")

bf16 = jnp.bfloat16
f32 = jnp.float32


def moved(d, axis, k):
    d = dict(d)
    if axis == "z":
        z = (2 * d["zh"] + d["zl"] + k) % 4
        d["zh"], d["zl"] = divmod(z, 2)
    elif axis == "first":
        return moved(d, "y" if d["c"] == 0 else "z", k)
    elif axis == "second":
        return moved(d, "z" if d["c"] == 0 else "y", k)
    else:
        d[axis] = (d[axis] + k) % SIZES[AX.index(axis)]
    return d


def send(a, axis, k):
    pairs = []
    for place in itertools.product(*map(range, SIZES)):
        to = moved(dict(zip(AX, place)), axis, k)
        pairs.append(
            (
                int(np.ravel_multi_index(place, SIZES)),
                int(np.ravel_multi_index([to[n] for n in AX], SIZES)),
            )
        )
    return lax.ppermute(a, AX, pairs)


def spread(a, axis):
    return tuple(send(a, axis, k) for k in (1, 2, 3))


def deal(parts, axis):
    return (parts[0],) + tuple(send(parts[k], axis, k) for k in (1, 2, 3))


def ring(parts, axis, middle, deps=()):
    own, up, down, one, two = parts
    one, two = send(one, axis, 1), send(two, axis, 3)
    up, down, *more = middle((up, down, one, two), deps)
    return (own, send(up, axis, 1), send(down, axis, 3)), (up, *more)


def add3(terms):
    a, b, c = (t.astype(f32) for t in terms)
    return a + (b + c)


def add4(terms):
    a, b, c, d = (t.astype(f32) for t in terms)
    return (a + b) + (c + d)


def dot(a, b):
    return lax.dot_general(a, b, (((1,), (0,)), ((), ())), preferred_element_type=f32)


def dot_nt(a, b):
    return lax.dot_general(a, b, (((1,), (1,)), ((), ())), preferred_element_type=f32)


def dot_tn(a, b):
    return lax.dot_general(a, b, (((0,), (0,)), ((), ())), preferred_element_type=f32)


def halves(a):
    hi = a.astype(bf16)
    return hi, (a - hi.astype(f32)).astype(bf16)


def thirds(a):
    hi = a.astype(bf16)
    rest = a - hi.astype(f32)
    mid = rest.astype(bf16)
    return hi, mid, (rest - mid.astype(f32)).astype(bf16)


def tri_dot(tri, a):
    return dot(jnp.concatenate([tri] * 3, axis=1), jnp.concatenate(thirds(a), axis=0))


def lanes_of(a, i):
    return jnp.broadcast_to(a[:, i : i + 1], (Q, 128))


def iota(shape, dim):
    return lax.broadcasted_iota(jnp.int32, shape, dim)


def softplus(v):
    return jnp.maximum(v, 0.0) + jnp.log1p(jnp.exp(-jnp.abs(v)))


def here():
    return {n: lax.axis_index(n) for n in AX}


def row_copies(pieces, dst, sems, by_step=False):
    me = here()
    places = ((0, 0, D), (1, 0, D), (2, 0, D), (3, 0, D))
    if len(pieces) == 5:
        places = ((0, 0, D), (1, 0, D), (3, 0, D), (2, 0, CH), (2, CH, CH))
    copies = []
    for ref, (k, col, width) in zip(pieces, places):
        x = lax.rem(me["x"] + 4 - k, 4)
        for g in range(3):
            at = lax.rem(3 * x + g + 4 + 4 * me["zl"], 12)
            to = dst.at[pl.ds(pl.multiple_of(64 * at, 64), 64), pl.ds(col, width)]
            copies.append((ref.at[pl.ds(64 * g, 64)], to, at // 4 if by_step else len(copies)))
    return [pltpu.make_async_copy(s, d, sems.at[i]) for s, d, i in copies]


N_ROW_COPIES = 15


def weight_copies(pieces, column, width, dst, sems):
    me = here()
    copies = []
    four = ((0, 0), (96, 3), (192, 2), (288, 1))
    hops = ((0, four), (3, four), (1, four), (2, four[:2]), (2, ((0, 2), (96, 1))))
    for k, ref in enumerate(pieces):
        core = lax.rem(me["c"] + k // 5, 2)
        rb, rows = hops[k % 5]
        for row, ra in rows:
            y = lax.rem(me["y"] + jnp.where(core == 0, ra, rb), 4)
            z = lax.rem(2 * me["zh"] + me["zl"] + jnp.where(core == 0, rb, ra), 4)
            f = (z // 2 * 4 + y) * 2 + core
            copies.append(
                (
                    ref.at[pl.ds(row, 96), pl.ds(column, width)],
                    dst.at[
                        pl.ds(pl.multiple_of(96 * f, 96), 96),
                        pl.ds(pl.multiple_of(width * lax.rem(z, 2), 128), width),
                    ],
                    lax.rem(z, 2),
                )
            )
    return [pltpu.make_async_copy(s, d, sems.at[g]) for s, d, g in copies]


def wait_half(g, width, dst, sems):
    half = dst.at[:, pl.ds(g * width, width)]
    pltpu.make_async_copy(half, half, sems.at[g]).wait()


def line_kernel(a, b, c, d, *rest):
    for k, ref in enumerate((a, b, c, d)):
        rest[-1][96 * k : 96 * k + 96, :] = ref[...]


def norm_kernel(*refs):
    rows, (gain, feat, feat_t, raw, sem) = refs[:5], refs[5:]
    copies = row_copies(rows, raw, sem)
    for c in copies:
        c.start()
    for c in copies:
        c.wait()
    for k in range(ROWS // 128):
        at = slice(128 * k, 128 * k + 128)
        v = raw[at, :].astype(f32)
        r = lax.rsqrt(jnp.mean(v * v, axis=1, keepdims=True) + EPS)
        normed = v * r * gain[...]
        feat[at, :] = normed.astype(bf16)
        for m in range(D // 128):
            col = slice(128 * m, 128 * m + 128)
            feat_t[col, at] = normed[:, col].T.astype(bf16)


def param_kernel(small, far, prm, heads):
    at_0 = lax.axis_index("zl") == 0
    lo = jnp.where(at_0, small[...], far[...])
    hi = jnp.where(at_0, far[...], small[...])
    prm[:, :HALF] = lo
    prm[:, HALF:] = hi
    lane = iota((1, 128), 1)

    def twelve(k):
        col = slice(128 * k, 128 * k + 128)
        return jnp.where(lane < 6, lo[6:7, col], pltpu.roll(hi[6:7, col], 6, 1))

    heads[...] = jnp.zeros_like(heads)
    heads[0:1, :] = jnp.where(lane < 12, jnp.exp(twelve(0)), 0.0)
    heads[1:2, :] = jnp.where(lane < 12, twelve(1), 0.0)
    skip = twelve(2)
    for i in range(PAIRS):
        pair = [jnp.broadcast_to(skip[:, 2 * i + k : 2 * i + k + 1], (1, 128)) for k in range(2)]
        prm[6:7, 128 * i : 128 * i + 128] = jnp.where(lane < 64, pair[0], pair[1])


def touch_kernel(*refs):
    pass


def proj_kernel(*refs):
    weights, (feat, w_out, wo_out, pre, w, wo, wsem, wosem, osem) = refs[:10], refs[10:]
    i = pl.program_id(0)
    outs = [
        pltpu.make_async_copy(w, w_out, osem.at[0]),
        pltpu.make_async_copy(wo, wo_out, osem.at[1]),
    ]

    @pl.when(i == 0)
    def _():
        for c in weight_copies(weights, 0, LEFT, w, wsem):
            c.start()
        for c in weight_copies(weights, LEFT, HALF, wo, wosem):
            c.start()
        wait_half(0, LEFT, w, wsem)

    @pl.when(i == 2)
    def _():
        wait_half(1, LEFT, w, wsem)
        outs[0].start()

    @pl.when(i == 3)
    def _():
        for g in range(2):
            wait_half(g, HALF, wo, wosem)
        outs[1].start()

    pre[...] = dot(feat[...], w[:, pl.ds(pl.multiple_of(512 * i, 512), 512)])

    @pl.when(i == pl.num_programs(0) - 1)
    def _():
        for c in outs:
            c.wait()


def pair_places(i):
    g, p = divmod(i, 3)
    return slice(128 * i, 128 * i + 128), g * LEFT + HALF + 128 * p


def step_sizes(pre, heads):
    raw = pre[:, 896:1024] + pre[:, LEFT + 896 : LEFT + 1024] + heads[1:2, :]
    return raw, softplus(raw)


def framed_inputs(s, zl, pre, prev, msg, vx, vs):
    for g in range(2):
        base = g * LEFT + HALF
        vx[8:264, g * HALF : (g + 1) * HALF] = pre[:, base : base + HALF]
        vs[8:264, g * N : (g + 1) * N] = pre[:, base + HALF : base + HALF + N]
        if s == 0:
            vx[0:8, g * HALF : (g + 1) * HALF] = jnp.zeros((8, HALF), f32)
            vs[0:8, g * N : (g + 1) * N] = jnp.zeros((8, N), f32)
            continue
        hx, hs = prev[:, base : base + HALF], prev[:, base + HALF : base + HALF + N]
        if s == 1:
            hx, hs = jnp.where(zl == 1, hx, 0.0), jnp.where(zl == 1, hs, 0.0)
        else:
            mx = msg[128:144, g * HALF : (g + 1) * HALF].astype(f32)[:8]
            ms = msg[144:160, g * N : (g + 1) * N].astype(f32)[:8]
            hx, hs = jnp.where(zl == 0, hx, mx), jnp.where(zl == 0, hs, ms)
        vx[0:8, g * HALF : (g + 1) * HALF] = hx
        vs[0:8, g * N : (g + 1) * N] = hs


def fwd_kernel(s, *refs):
    refs = list(refs)
    pre = refs.pop(0)
    rows_here = pl.ds(STEP * s, STEP)
    prev = pre.at[pl.ds(STEP * s - 8, 8)] if s else None
    pre = pre.at[rows_here]
    h_in = refs.pop(0) if s else None
    msg = refs.pop(0) if s == 2 else None
    prm, prs, heads = refs[:3]
    refs = refs[3:]
    refs = refs[len(refs) - (5 if s == 0 else 4) :]
    act, hs = refs[:2]
    act = act.at[rows_here]
    refs = refs[2:]
    out_msg = refs.pop(0) if s == 0 else None
    vx, vs = refs
    zl = lax.axis_index("zl")
    framed_inputs(s, zl, pre, prev, msg, vx, vs)
    if s == 0:
        hs[0] = jnp.zeros((N, CH), f32)
    elif s == 1:
        hs[0] = jnp.where(zl == 1, h_in[2], 0.0)
    else:
        hs[0] = jnp.where(zl == 0, h_in[2], msg[0:128, :].astype(f32))
    _, dt_all = step_sizes(pre, heads)
    a_all = -heads[0:1, :] * dt_all
    sub, lane = iota((Q, 128), 0), iota((Q, 128), 1)
    low_mask = sub >= lane
    tri = jnp.where(low_mask, 1.0, 0.0).astype(bf16)
    left = lane < 64
    for j in range(2):
        r0 = Q * j
        bc = []
        for g in range(2):
            col = slice(g * N, (g + 1) * N)
            cs = prs[4:5, col] + sum(
                prs[k : k + 1, col] * vs[5 + k + r0 : 5 + k + r0 + Q, col] for k in range(4)
            )
            act[r0 : r0 + Q, 2 * CH + g * N : 2 * CH + (g + 1) * N] = cs
            bc.append((cs * jax.nn.sigmoid(cs)).astype(bf16))
        b, c = bc
        bt = b.astype(f32).T.astype(bf16)
        scores = dot_nt(c, b)
        dt = dt_all[r0 : r0 + Q]
        cum = tri_dot(tri, a_all[r0 : r0 + Q])
        cum_t = cum.T
        for i in range(PAIRS):
            col, _ = pair_places(i)
            cx = prm[4:5, col] + sum(
                prm[k : k + 1, col] * vx[5 + k + r0 : 5 + k + r0 + Q, col] for k in range(4)
            )
            act[r0 : r0 + Q, CH + 128 * i : CH + 128 * i + 128] = cx
            x = (cx * jax.nn.sigmoid(cx)).astype(bf16).astype(f32)
            c0, c1 = lanes_of(cum, 2 * i), lanes_of(cum, 2 * i + 1)
            m0 = scores * jnp.exp(jnp.where(low_mask, c0 - cum_t[2 * i : 2 * i + 1, :], NEG))
            m1 = scores * jnp.exp(jnp.where(low_mask, c1 - cum_t[2 * i + 1 : 2 * i + 2, :], NEG))
            cp = jnp.where(left, c0, c1)
            xdt = x * jnp.where(left, lanes_of(dt, 2 * i), lanes_of(dt, 2 * i + 1))
            xdtb = xdt.astype(bf16)
            zero = jnp.zeros_like(xdtb)
            last = cp[Q - 1 : Q, :]
            inside = dot(
                jnp.concatenate([m0.astype(bf16), m1.astype(bf16)], axis=1),
                jnp.concatenate([jnp.where(left, xdtb, zero), jnp.where(left, zero, xdtb)], axis=0),
            )
            h = hs[j, :, col]
            y = inside + jnp.exp(cp) * dot(c, h.astype(bf16)) + prm[6:7, col] * x
            act[r0 : r0 + Q, col] = y
            hs[j + 1, :, col] = h * jnp.exp(last) + dot(bt, (xdt * jnp.exp(last - cp)).astype(bf16))
    if s == 0:
        out_msg[0:128, :] = hs[2].astype(bf16)
        out_msg[128:144, :] = jnp.concatenate([vx[256:264, :]] * 2, axis=0).astype(bf16)
        out_msg[144:160, :] = jnp.concatenate(
            [jnp.concatenate([vs[256:264, :]] * 2, axis=0), jnp.zeros((16, CH - 2 * N), f32)], axis=1
        ).astype(bf16)


def cot_kernel(*refs):
    rows, (w, pre, act, prm, cot, gm, gb, sums, rsem) = refs[:5], refs[5:]
    for c in row_copies(rows, cot, rsem, True):
        c.start()
    lane = iota((STEP, 128), 1)
    for i in range(3):
        at = slice(STEP * i, STEP * i + STEP)
        step = cot.at[pl.ds(STEP * i, STEP)]
        pltpu.make_async_copy(step, step, rsem.at[i]).wait()
        grad = dot(cot[at, :], w[...])
        gm[at, :] = grad
        squares = jnp.zeros((STEP, 128), f32)
        dots = jnp.zeros((STEP, 128), f32)
        for c in range(PAIRS):
            col = slice(128 * c, 128 * c + 128)
            first = c // 3 * LEFT + c % 3 * 128
            gate = pre[at, first : first + 128]
            gated = act[at, col] * (gate * jax.nn.sigmoid(gate))
            scaled = gated * prm[5:6, col]
            gb[at, col] = scaled.astype(bf16)
            squares = squares + gated * gated
            dots = dots + grad[:, col] * scaled
        squares = jnp.sum(squares, axis=1, keepdims=True)
        dots = jnp.sum(dots, axis=1, keepdims=True)
        both = jnp.where(lane == 0, squares, jnp.where(lane == 1, dots, 0.0))
        sums[:, at] = both.T[0:8, :]


def store_rows(i, value, outs):
    own, up, down, one, two = outs
    me = here()
    for g in range(4):
        natural = lax.rem(4 * i + g + 8 - 4 * me["zl"] + 12, 12)
        rel = lax.rem(natural // 3 - me["x"] + 4, 4)
        at = pl.ds(pl.multiple_of(64 * lax.rem(natural, 3), 64), 64)
        rows = slice(64 * g, 64 * g + 64)
        for k, out in ((0, own), (1, up), (3, down)):

            @pl.when(rel == k)
            def _(out=out, rows=rows, at=at):
                out[at, :] = value[rows, :]

        @pl.when(rel == 2)
        def _(rows=rows, at=at):
            one[at, :] = value[rows, :CH]
            two[at, :] = value[rows, CH:]


def add(a, b):
    return (a.astype(f32) + b.astype(f32)).astype(bf16)


def row_middle_kernel(up, down, one, two, *refs):
    up_out, down_out = refs[-2:]
    up_out[:, :CH] = add(up[:, :CH], one[...])
    up_out[:, CH:] = up[:, CH:]
    down_out[:, :CH] = down[:, :CH]
    down_out[:, CH:] = add(down[:, CH:], two[...])


def out_kernel(gb, w, *outs):
    store_rows(pl.program_id(0), dot_nt(gb[...], w[...]).astype(bf16), outs)


def gate_kernel(s0, s1, s2, s3, gm, act, pre, prm, *refs):
    dssd, lowz, mixed, ggain, cols = refs[-5:]
    cols[...] = (s0[...] + s1[...] + s2[...] + s3[...]).T
    ggain[...] = jnp.zeros_like(ggain)

    def block(k, carry):
        at = pl.ds(pl.multiple_of(64 * k, 64), 64)
        total = cols[at, :]
        inv = lax.rsqrt(total[:, 0:1] / DI + EPS)
        pull = inv * inv * inv * (total[:, 1:2] / DI)
        for c in range(PAIRS):
            col = slice(128 * c, 128 * c + 128)
            first = c // 3 * LEFT + c % 3 * 128
            gate = pre[at, first : first + 128]
            sig = jax.nn.sigmoid(gate)
            silu = gate * sig
            y = act[at, col]
            gated = y * silu
            grad = gm[at, col]
            gain = prm[5:6, col]
            normal = gated * inv
            mixed[at, col] = (normal * gain).astype(bf16)
            dg = grad * gain * inv - gated * pull
            dssd[at, col] = (dg * silu).astype(bf16)
            lowz[at, col] = (dg * y * (sig * (1.0 + gate * (1.0 - sig)))).astype(bf16)
            ggain[0:1, col] += jnp.sum(grad * normal, axis=0, keepdims=True)
        return carry

    lax.fori_loop(0, ROWS // 64, block, 0)


def send_tiles(buf, own, far, sem):
    me = here()
    m = pl.program_id(0)
    z0 = 2 * me["zh"] + me["zl"]
    for core in range(2):

        @pl.when(me["c"] == core)
        def _(core=core):
            for k in range(4):
                dy = lax.rem(lax.rem(2 * m + k // 2, 4) - me["y"] + 4, 4)
                for g in range(2):
                    dz = lax.rem(2 * (m // 2) + g - z0 + 4, 4)
                    at = 4 * dz + dy if k % 2 == 0 else 4 * dy + dz
                    pltpu.make_async_copy(
                        buf.at[pl.ds(pl.multiple_of(384 * m + 96 * k, 96), 96), pl.ds(g * CH, CH)],
                        (own if k % 2 == core else far).at[pl.ds(pl.multiple_of(96 * at, 96), 96)],
                        sem.at[m],
                    ).start()


def row_gain(part, w):
    lanes = sum(part[:, k : k + 128] * w[:, k : k + 128].astype(f32) for k in range(0, part.shape[1], 128))
    ones = jnp.ones((8, 128), bf16)
    hi, lo = halves(lanes)
    return dot_nt(ones, hi) + dot_nt(ones, lo)


def wait_tiles(own, sem):
    for m in range(4):
        block = own.at[pl.ds(0, ROWS)]
        pltpu.make_async_copy(block, block, sem.at[m]).wait()


def early_kernel(feat_t, cot, lowz, mixed, w, own, far, gains, buf, sem):
    m = pl.program_id(0)
    rows = pl.ds(pl.multiple_of(384 * m, 384), 384)
    part = dot(feat_t[...], lowz[...])
    out = dot_tn(cot[...], mixed[...]).astype(bf16)
    low = part.astype(bf16)
    for g in range(2):
        col = slice(g * HALF, (g + 1) * HALF)
        buf[rows, g * CH : g * CH + HALF] = low[:, col]
        buf[rows, g * CH + HALF : (g + 1) * CH] = out[:, col]
    send_tiles(buf, own, far, sem)
    gains[...] = row_gain(part, jnp.concatenate([w[:, :HALF], w[:, LEFT : LEFT + HALF]], axis=1))

    @pl.when(m == 3)
    def _():
        wait_tiles(own, sem)


def late_kernel(feat_t, low, w, gains_in, acc, accs, ggain, *refs):
    own, far, small, buf, gains, tail, sem, tail_sem = refs[-8:]
    m = pl.program_id(0)
    rows = pl.ds(pl.multiple_of(384 * m, 384), 384)
    both = w[:, LEFT - N : LEFT].astype(f32) + w[:, 2 * LEFT - N :].astype(f32)
    rhs = jnp.concatenate(
        [low[:, HALF:LEFT], low[:, LEFT + HALF : LEFT + CH], low[:, LEFT + CH : LEFT + CH + N]], axis=1
    )
    taps = jnp.concatenate(
        [w[:, HALF : CH + N], both.astype(bf16), w[:, LEFT + HALF : LEFT + CH], w[:, LEFT + CH : LEFT + CH + N]],
        axis=1,
    )
    part = dot(feat_t[...], rhs)
    low_part = part.astype(bf16)
    shared = jnp.concatenate([low_part[:, HALF : HALF + 2 * N], low_part[:, 1024:1152]], axis=1)
    buf[rows, 0:HALF] = low_part[:, 0:HALF]
    buf[rows, CH : CH + HALF] = low_part[:, 640:1024]
    for g in range(2):
        buf[rows, g * CH + HALF : (g + 1) * CH] = shared
    send_tiles(buf, own, far, sem)
    gain = gains_in[...] + row_gain(part, taps)
    gains[m] = gain

    @pl.when(m == 3)
    def _():
        small[...] = jnp.zeros_like(small)
        small[0:6, :] = acc[0:6, :]
        small[6:7, :] = ggain[0:1, :]
        small[8:9, :] = jnp.concatenate([gains[0, 0:1, :], gains[1, 0:1, :]], axis=1)
        small[9:10, :] = jnp.concatenate([gains[2, 0:1, :], gains[3, 0:1, :]], axis=1)
        for row, rs in ((7, (5, 6)), (10, (0, 1, 2)), (11, (3, 4))):
            for k, r in enumerate(rs):
                small[row : row + 1, 256 * k : 256 * k + 256] = accs[r : r + 1, :]
        tail[...] = split_small(small[...])
        copy = pltpu.make_async_copy(tail, far.at[pl.ds(2 * ROWS, 32)], tail_sem.at[0])
        copy.start()
        wait_tiles(own, sem)
        copy.wait()


def split_small(total):
    return jnp.concatenate(halves(total), axis=0)


def sum_small(block):
    return block[:16].astype(f32) + block[16:].astype(f32)


def core_sum_kernel(with_small, *refs):
    own, far = refs[:2]
    outs = refs[-5:]
    if with_small:
        small = split_small(refs[2][...] + sum_small(far[2 * ROWS : 2 * ROWS + 32, :]))
    for out, first, count in zip(outs, (0, 384, 1152, 768, 960), (384, 384, 384, 192, 192)):
        rows = slice(first, first + count)
        out[0:count, :] = add(own[rows, :], far[rows, :])
        if with_small:
            out[count : count + 32, :] = small


def tile_middle_kernel(with_small, up, down, one, two, *refs):
    outs = refs[-3:] if with_small else refs[-2:]
    up_out, down_out = outs[:2]
    up_out[0:192, :] = add(up[0:192, :], one[0:192, :])
    up_out[192:384, :] = up[192:384, :]
    down_out[0:192, :] = down[0:192, :]
    down_out[192:384, :] = add(down[192:384, :], two[0:192, :])
    if with_small:
        up_out[384:416, :] = one[192:224, :]
        down_out[384:416, :] = down[384:416, :]
        outs[2][...] = split_small(sum_small(one[192:224, :]) + sum_small(two[192:224, :]))


def axis_sum_kernel(*refs):
    early, late, near, outs = refs[:3], refs[3:6], refs[6], refs[-4:]
    own, up = late[:2]
    small = split_small(sum_small(own[384:416, :]) + sum_small(up[384:416, :]) + sum_small(near[...]))
    for k, out in enumerate(outs):
        rows = slice(96 * k, 96 * k + 96)
        out[0:96, :] = add3([t[rows, :] for t in early]).astype(bf16)
        out[96:192, :] = add3([t[rows, :] for t in late]).astype(bf16)
        out[192:224, :] = small


def last_sum_kernel(*refs):
    terms, (early, tile, small, to_x) = refs[:4], refs[-4:]
    early[...] = add4([t[0:96, :] for t in terms])
    total = add4([t[96:192, :] for t in terms])
    tile[...] = total
    every = sum(sum_small(t[192:224, :]) for t in terms)
    small[...] = every
    for k in range(3):
        rows = slice(32 * k, 32 * k + 32)
        to_x[0:32, 256 * k : 256 * k + 128] = total[rows, HALF : HALF + N].astype(bf16)
        to_x[0:32, 256 * k + 128 : 256 * k + 256] = total[rows, HALF + 2 * N : HALF + 3 * N].astype(bf16)
    hi, lo = halves(every[8:16, :])
    to_x[32:48, :] = jnp.concatenate([hi.astype(f32), lo.astype(f32)], axis=0).astype(bf16)


def x_sum_kernel(a, b, c, d, gain, *refs):
    state, g_gain, g_conv, g_bias = refs[-4:]
    total = add4([a[...], b[...], c[...], d[...]])
    for k in range(3):
        state[32 * k : 32 * k + 32, :] = total[0:32, 256 * k : 256 * k + 256]
    small = total[32:40, :] + total[40:48, :]
    g_gain[:, :CH] = small[0:1, :] / gain[:, :CH]
    g_gain[:, CH:] = small[1:2, :] / gain[:, CH:]
    for k in range(3):
        g_conv[k : k + 1, :] = small[2:3, 256 * k : 256 * k + 256]
    g_conv[3:4, :] = small[3:4, 0:256]
    g_bias[...] = small[3:4, 256:512]


def bwd_kernel(s, *refs):
    refs = list(refs)
    pre = refs.pop(0)
    rows_here = pl.ds(STEP * s, STEP)
    prev = pre.at[pl.ds(STEP * s - 8, 8)] if s else None
    msg = refs.pop(0) if s == 2 else None
    act, hs, dssd, lowz, prm, prs, heads = refs[:7]
    pre, act, dssd, lowz = (ref.at[rows_here] for ref in (pre, act, dssd, lowz))
    refs = refs[7:]
    if s < 2:
        dh_in, tail, acc_in, accs_in = refs[:4]
        refs = refs[4:]
        back = refs.pop(0) if s == 0 else None
    refs = refs[len(refs) - (10 if s == 2 else 9) :]
    low, dh, head_rows, acc, accs = refs[:5]
    low = low.at[rows_here]
    refs = refs[5:]
    for g in range(2):
        low[:, g * LEFT : g * LEFT + HALF] = lowz[:, g * HALF : (g + 1) * HALF]
    out_msg = refs.pop(0) if s == 2 else None
    vx, vs, dp, ds = refs
    zl = lax.axis_index("zl")
    framed_inputs(s, zl, pre, prev, msg, vx, vs)
    if s == 2:
        dh[...] = jnp.zeros_like(dh)
        dp[256:264, :] = jnp.zeros((8, CH), f32)
        ds[256:264, :] = jnp.zeros((8, 2 * N), f32)
        acc[...] = jnp.zeros_like(acc)
        accs[...] = jnp.zeros_like(accs)
    else:
        hd, hp, hq = dh_in[...], tail[0:8, :], tail[8:16, 0 : 2 * N]
        if s == 1:
            hd, hp, hq = (jnp.where(zl == 0, v, 0.0) for v in (hd, hp, hq))
        else:
            hd = jnp.where(zl == 1, hd, back[0:128, :].astype(f32))
            hp = jnp.where(zl == 1, hp, back[128:144, :].astype(f32)[:8])
            hq = jnp.where(zl == 1, hq, back[144:160, 0 : 2 * N].astype(f32)[:8])
        dh[...], dp[256:264, :], ds[256:264, :] = hd, hp, hq
        acc[...] = acc_in[...]
        accs[...] = accs_in[...]
    raw_all, dt_all = step_sizes(pre, heads)
    rate = heads[0:1, :]
    a_all = -rate * dt_all
    sub, lane = iota((Q, 128), 0), iota((Q, 128), 1)
    tri = jnp.where(sub >= lane, 1.0, 0.0).astype(bf16)
    up_mask = lane >= sub
    tri_up = jnp.where(up_mask, 1.0, 0.0).astype(bf16)
    below = jnp.where(lane < sub, 1.0, 0.0).astype(bf16)
    left = lane < 64
    for j in (1, 0):
        r0 = Q * j
        rows = slice(r0, r0 + Q)
        pre_s = [act[rows, 2 * CH + g * N : 2 * CH + (g + 1) * N] for g in range(2)]
        sig_s = [jax.nn.sigmoid(v) for v in pre_s]
        bf, cf = [(v * w).astype(bf16).astype(f32) for v, w in zip(pre_s, sig_s)]
        b, c = bf.astype(bf16), cf.astype(bf16)
        ct = cf.T.astype(bf16)
        scores_t = dot_nt(c, b).T
        dt, a = dt_all[rows], a_all[rows]
        cum = tri_dot(tri, a)
        cum_t = cum.T
        d_scores_t = jnp.zeros((Q, Q), f32)
        d_b = jnp.zeros((Q, N), f32)
        d_c = jnp.zeros((Q, N), f32)
        per_head = jnp.zeros((3 * Q, 128), f32)
        for i in range(PAIRS):
            col, _ = pair_places(i)
            cx = act[rows, CH + 128 * i : CH + 128 * i + 128]
            sig = jax.nn.sigmoid(cx)
            x = (cx * sig).astype(bf16).astype(f32)
            dyb = dssd[rows, col]
            dy = dyb.astype(f32)
            skip = prm[6:7, col]
            c0, c1 = lanes_of(cum, 2 * i), lanes_of(cum, 2 * i + 1)
            l0 = jnp.exp(jnp.where(up_mask, cum_t[2 * i : 2 * i + 1, :] - c0, NEG))
            l1 = jnp.exp(jnp.where(up_mask, cum_t[2 * i + 1 : 2 * i + 2, :] - c1, NEG))
            cp = jnp.where(left, c0, c1)
            dtp = jnp.where(left, lanes_of(dt, 2 * i), lanes_of(dt, 2 * i + 1))
            last = cp[Q - 1 : Q, :]
            fade = jnp.exp(last - cp)
            xdt = x * dtp
            xdtb = xdt.astype(bf16)
            zero = jnp.zeros_like(xdtb)
            dy_split = jnp.concatenate([jnp.where(left, dyb, zero), jnp.where(left, zero, dyb)], axis=0)
            x_split = jnp.concatenate([jnp.where(left, xdtb, zero), jnp.where(left, zero, xdtb)], axis=0)
            dhp = dh[:, col]
            dhb = dhp.astype(bf16)
            m_t = jnp.concatenate([(scores_t * l0).astype(bf16), (scores_t * l1).astype(bf16)], axis=1)
            inside = dot(m_t, dy_split)
            beyond = fade * dot(b, dhb)
            dxdt = inside + beyond
            dx = dxdt * dtp + skip * dy
            acc[5:6, col] += jnp.sum(dy * x, axis=0, keepdims=True)
            d_m_t = dot_nt(x_split, dyb)
            d_scores_t = d_scores_t + d_m_t[:Q] * l0 + d_m_t[Q:] * l1
            h = hs[j, :, col]
            crossing = jnp.sum(dhp * h, axis=0, keepdims=True) * jnp.exp(last)
            t1 = dxdt * x
            t2 = dy * (act[rows, col] - skip * x) - xdtb.astype(f32) * inside
            t2 = t2 + jnp.where(sub == Q - 1, crossing, 0.0)
            t3 = xdt * beyond
            pick = (lane == jnp.where(sub < 64, 2 * i, 2 * i + 1)).astype(f32).astype(bf16)
            hi, lo = halves(jnp.concatenate([t1, t2, t3], axis=0))
            per_head = per_head + dot(
                jnp.concatenate([hi, lo], axis=1), jnp.concatenate([pick, pick], axis=0)
            )
            dye = (dy * jnp.exp(cp)).astype(bf16)
            d_c = d_c + dot_nt(dye, h.astype(bf16))
            d_b = d_b + dot_nt((xdt * fade).astype(bf16), dhb)
            dh[:, col] = dhp * jnp.exp(last) + dot(ct, dye)
            dp[rows, col] = dx * (sig * (1.0 + cx * (1.0 - sig)))
        d_b = d_b + dot(d_scores_t.astype(bf16), c)
        d_c = d_c + dot(d_scores_t.T.astype(bf16), b)
        for g, grad in ((0, d_b), (1, d_c)):
            ds[rows, g * N : (g + 1) * N] = grad * (sig_s[g] * (1.0 + pre_s[g] * (1.0 - sig_s[g])))
        da = tri_dot(tri_up, per_head[Q : 2 * Q]) + tri_dot(below, per_head[2 * Q :])
        ddt = per_head[:Q] - rate * da
        dstep = ddt * jax.nn.sigmoid(raw_all[rows])
        accs[5:6, 0:128] += jnp.sum(a * da, axis=0, keepdims=True)
        accs[6:7, 0:128] += jnp.sum(dstep, axis=0, keepdims=True)
        for g in range(2):
            low[rows, (g + 1) * LEFT - N : (g + 1) * LEFT] = dstep.astype(bf16)
    for frame, grads, taps, out, width in ((vx, dp, prm, acc, CH), (vs, ds, prs, accs, 2 * N)):
        for i in range(width // 128):
            col = slice(128 * i, 128 * i + 128)
            g, p = divmod(i, width // 256)
            to = g * LEFT + HALF + 128 * p + (HALF if width == 2 * N else 0)
            back_v = sum(taps[k : k + 1, col] * grads[3 - k : 3 - k + STEP, col] for k in range(4))
            low[:, to : to + 128] = back_v.astype(bf16)
            own = grads[0:STEP, col]
            for k in range(4):
                out[k : k + 1, col] += jnp.sum(own * frame[5 + k : 5 + k + STEP, col], axis=0, keepdims=True)
            out[4:5, col] += jnp.sum(own, axis=0, keepdims=True)
    head_rows[0:8, :] = dp[0:8, :]
    head_rows[8:16, :] = jnp.concatenate([ds[0:8, :], jnp.zeros((8, CH - 2 * N), f32)], axis=1)
    if s == 2:
        out_msg[0:128, :] = dh[...].astype(bf16)
        out_msg[128:144, :] = jnp.concatenate([head_rows[0:8, :]] * 2, axis=0).astype(bf16)
        out_msg[144:160, :] = jnp.concatenate([head_rows[8:16, :]] * 2, axis=0).astype(bf16)


def feat_kernel(low, w, *refs):
    store_rows(pl.program_id(0), dot_nt(low[...], w[...]).astype(bf16), refs[-5:])


ANY = pl.BlockSpec(memory_space=pl.ANY)
VM = pl.BlockSpec(memory_space=pltpu.VMEM)


def params(mib):
    return pltpu.CompilerParams(vmem_limit_bytes=mib * 1024 * 1024)


def shape(*s, dtype=f32):
    return jax.ShapeDtypeStruct(s, dtype)


def cost(flops, moved_bytes):
    return pl.CostEstimate(flops=int(flops), bytes_accessed=int(moved_bytes), transcendentals=0)


def steps(width, column=0):
    return pl.BlockSpec((STEP, width), lambda i: (i, column))


def line_up(parts, deps):
    return pl.pallas_call(
        line_kernel,
        in_specs=[VM] * 4 + [ANY] * len(deps),
        out_specs=VM,
        out_shape=shape(384, FULL, dtype=bf16),
        compiler_params=params(4),
        cost_estimate=cost(1e6, 2e6),
        name="line_up",
    )(*parts, *deps)


def touch(a, deps):
    return pl.pallas_call(
        touch_kernel,
        in_specs=[ANY] * (1 + len(deps)),
        out_specs=ANY,
        out_shape=jax.ShapeDtypeStruct(a.shape, a.dtype),
        input_output_aliases={0: 0},
        compiler_params=params(1),
        cost_estimate=cost(1, 1),
        name="touch",
    )(a, *deps)


def normalize(rows, gain):
    return pl.pallas_call(
        norm_kernel,
        in_specs=[ANY] * 5 + [VM],
        out_specs=[VM, VM],
        out_shape=[shape(ROWS, D, dtype=bf16), shape(D, ROWS, dtype=bf16)],
        scratch_shapes=[pltpu.VMEM((ROWS, D), bf16), pltpu.SemaphoreType.DMA((N_ROW_COPIES,))],
        compiler_params=params(12),
        cost_estimate=cost(1e7, 5e6),
        name="normalize",
    )(*rows, gain)


def project(feat, weights):
    return pl.pallas_call(
        proj_kernel,
        grid=(4,),
        in_specs=[ANY] * 10 + [VM],
        out_specs=[ANY, ANY, pl.BlockSpec((ROWS, 512), lambda i: (0, i))],
        out_shape=[shape(D, 2 * LEFT, dtype=bf16), shape(D, CH, dtype=bf16), shape(ROWS, 2 * LEFT)],
        scratch_shapes=[
            pltpu.VMEM((D, 2 * LEFT), bf16),
            pltpu.VMEM((D, CH), bf16),
            pltpu.SemaphoreType.DMA((2,)),
            pltpu.SemaphoreType.DMA((2,)),
            pltpu.SemaphoreType.DMA((2,)),
        ],
        compiler_params=params(16),
        cost_estimate=cost(2 * ROWS * D * 2 * LEFT, 24e6),
        name="project",
    )(*weights, feat)


def forward(s, pre, act, h, msg, prm, prs, heads):
    ins = [pre] + ([h] if s else []) + ([msg] if s == 2 else []) + [prm, prs, heads]
    aliases = {}
    if s:
        aliases = {len(ins): 0}
        ins += [act]
    outs = [shape(ROWS, 2 * CH + 2 * N), shape(3, N, CH)]
    if s == 0:
        outs += [shape(160, CH, dtype=bf16)]
    return pl.pallas_call(
        functools.partial(fwd_kernel, s),
        in_specs=[VM] * len(ins),
        out_specs=[VM] * len(outs),
        out_shape=outs,
        input_output_aliases=aliases,
        scratch_shapes=[pltpu.VMEM((264, CH), f32), pltpu.VMEM((264, 2 * N), f32)],
        compiler_params=params(6),
        cost_estimate=cost(1.5e9, 6e6),
        name=f"scan_rows_{s}",
    )(*ins)


def cotangent(rows, w, pre, act, prm):
    return pl.pallas_call(
        cot_kernel,
        in_specs=[ANY] * 5 + [VM] * 4,
        out_specs=[VM] * 4,
        out_shape=[
            shape(ROWS, D, dtype=bf16),
            shape(ROWS, CH),
            shape(ROWS, CH, dtype=bf16),
            shape(8, ROWS),
        ],
        scratch_shapes=[pltpu.SemaphoreType.DMA((3,))],
        compiler_params=params(6),
        cost_estimate=cost(2 * ROWS * D * CH, 20e6),
        name="cotangent",
    )(*rows, w, pre, act, prm)


def out_partial(gb, w):
    return pl.pallas_call(
        out_kernel,
        grid=(3,),
        in_specs=[steps(CH), VM],
        out_specs=[VM] * 3 + [VM] * 2,
        out_shape=[shape(192, D, dtype=bf16)] * 3 + [shape(192, CH, dtype=bf16)] * 2,
        compiler_params=params(6),
        cost_estimate=cost(2 * ROWS * D * CH, 6e6),
        name="out_partial",
    )(gb, w)


def gate_back(sums, gm, act, pre, prm, deps):
    return pl.pallas_call(
        gate_kernel,
        in_specs=[VM] * 8 + [ANY] * len(deps),
        out_specs=[VM] * 4,
        out_shape=[shape(ROWS, CH, dtype=bf16)] * 3 + [shape(8, CH)],
        scratch_shapes=[pltpu.VMEM((ROWS, 8), f32)],
        compiler_params=params(4),
        cost_estimate=cost(1e7, 12e6),
        name="gate_back",
    )(*sums, gm, act, pre, prm, *deps)


def early_grads(feat_t, cot, lowz, mixed, w):
    return pl.pallas_call(
        early_kernel,
        grid=(4,),
        in_specs=[
            pl.BlockSpec((HALF, ROWS), lambda m: (m, 0)),
            pl.BlockSpec((ROWS, HALF), lambda m: (0, m)),
            VM,
            VM,
            pl.BlockSpec((HALF, 2 * LEFT), lambda m: (m, 0)),
        ],
        out_specs=[ANY, ANY, pl.BlockSpec((8, HALF), lambda m: (0, m))],
        out_shape=[shape(2 * ROWS, CH, dtype=bf16)] * 2 + [shape(8, D)],
        scratch_shapes=[pltpu.VMEM((D, 2 * CH), bf16), pltpu.SemaphoreType.DMA((4,))],
        compiler_params=params(14),
        cost_estimate=cost(2 * ROWS * D * 2 * CH, 12e6),
        name="early_grads",
    )(feat_t, cot, lowz, mixed, w)


def late_grads(feat_t, low, w, gains, acc, accs, ggain, deps):
    return pl.pallas_call(
        late_kernel,
        grid=(4,),
        in_specs=[
            pl.BlockSpec((HALF, ROWS), lambda m: (m, 0)),
            VM,
            pl.BlockSpec((HALF, 2 * LEFT), lambda m: (m, 0)),
            pl.BlockSpec((8, HALF), lambda m: (0, m)),
            VM,
            VM,
            VM,
        ]
        + [ANY] * len(deps),
        out_specs=[ANY, ANY, VM],
        out_shape=[shape(2 * ROWS, CH, dtype=bf16), shape(2 * ROWS + 32, CH, dtype=bf16), shape(16, CH)],
        scratch_shapes=[
            pltpu.VMEM((D, 2 * CH), bf16),
            pltpu.VMEM((4, 8, HALF), f32),
            pltpu.VMEM((32, CH), bf16),
            pltpu.SemaphoreType.DMA((4,)),
            pltpu.SemaphoreType.DMA((1,)),
        ],
        compiler_params=params(14),
        cost_estimate=cost(2 * ROWS * D * 3 * HALF, 12e6),
        name="late_grads",
    )(feat_t, low, w, gains, acc, accs, ggain, *deps)


def tile_sums(kernel, ins, outs, deps, name, mib=6):
    return pl.pallas_call(
        kernel,
        in_specs=[VM] * len(ins) + [ANY] * len(deps),
        out_specs=[VM] * len(outs),
        out_shape=outs,
        compiler_params=params(mib),
        cost_estimate=cost(1e6, 4e6),
        name=name,
    )(*ins, *deps)


def core_sum(own, far, small, deps, name):
    more = 32 if small else 0
    return tile_sums(
        functools.partial(core_sum_kernel, bool(small)),
        [own, far] + list(small),
        [shape(384 + more, CH, dtype=bf16)] * 3 + [shape(192 + more, CH, dtype=bf16)] * 2,
        deps,
        name,
        10,
    )


def row_middle(ins, deps):
    return tile_sums(row_middle_kernel, ins, [shape(192, D, dtype=bf16)] * 2, deps, "row_middle")


def tile_middle(with_small, ins, deps):
    outs = [shape(416 if with_small else 384, CH, dtype=bf16)] * 2
    if with_small:
        outs = outs + [shape(32, CH, dtype=bf16)]
    return tile_sums(functools.partial(tile_middle_kernel, with_small), ins, outs, deps, "tile_middle")


def backward(s, pre, msg, act, hs, dssd, lowz, prm, prs, heads, carried, back, low, deps):
    ins = [pre] + ([msg] if s == 2 else []) + [act, hs, dssd, lowz, prm, prs, heads]
    aliases = {}
    if s < 2:
        ins += list(carried)
        if s == 0:
            ins += [back]
        aliases = {len(ins): 0}
        ins += [low]
    outs = [shape(ROWS, 2 * LEFT, dtype=bf16), shape(N, CH), shape(16, CH), shape(8, CH), shape(8, 2 * N)]
    if s == 2:
        outs += [shape(160, CH, dtype=bf16)]
    return pl.pallas_call(
        functools.partial(bwd_kernel, s),
        in_specs=[VM] * len(ins) + [ANY] * len(deps),
        out_specs=[VM] * len(outs),
        out_shape=outs,
        input_output_aliases=aliases,
        scratch_shapes=[
            pltpu.VMEM((264, CH), f32),
            pltpu.VMEM((264, 2 * N), f32),
            pltpu.VMEM((264, CH), f32),
            pltpu.VMEM((264, 2 * N), f32),
        ],
        compiler_params=params(8),
        cost_estimate=cost(4e9, 8e6),
        name=f"scan_back_{s}",
    )(*ins, *deps)


def feat_partial(low, w, deps):
    return pl.pallas_call(
        feat_kernel,
        grid=(3,),
        in_specs=[steps(2 * LEFT), VM] + [ANY] * len(deps),
        out_specs=[VM] * 3 + [VM] * 2,
        out_shape=[shape(192, D, dtype=bf16)] * 3 + [shape(192, CH, dtype=bf16)] * 2,
        compiler_params=params(8),
        cost_estimate=cost(2 * ROWS * D * 2 * LEFT, 16e6),
        name="feat_partial",
    )(low, w, *deps)


def local(
    layer_input,
    input_gain,
    proj_inner,
    proj_step,
    proj_state,
    proj_output,
    conv_inner,
    conv_inner_bias,
    conv_state,
    conv_state_bias,
    inner_gain,
    decay_log,
    step_bias,
    skip_gain,
    out_cotangent,
):
    zl = lax.axis_index("zl")
    step_cols = jnp.where(
        zl == 0, jnp.pad(proj_step, ((0, 0), (0, 122))), jnp.pad(proj_step, ((0, 0), (6, 116)))
    )
    state_cols = jnp.where(zl == 0, proj_state[:, :N], proj_state[:, N:])
    shard = jnp.concatenate(
        [proj_inner[:, 0], proj_inner[:, 1], state_cols, step_cols, proj_output.T], axis=1
    )
    near = spread(shard, "first")

    coef = jnp.pad(jnp.stack([decay_log, step_bias, skip_gain]), ((0, 0), (0, 122))).reshape(1, HALF)
    small = jnp.concatenate(
        [touch(conv_inner, (near[0],)), conv_inner_bias[None], inner_gain[None], coef, jnp.zeros((1, HALF), f32)], axis=0
    )
    prm, heads = pl.pallas_call(
        param_kernel,
        in_specs=[VM, VM],
        out_specs=[VM, VM],
        out_shape=[shape(8, CH), shape(8, 128)],
        compiler_params=params(1),
        cost_estimate=cost(1, 1),
        name="parameters",
    )(small, send(small, "zl", 1))
    prs = jnp.concatenate([conv_state, conv_state_bias[None], jnp.zeros((3, 2 * N), f32)], axis=0)

    rows = (layer_input, send(layer_input, "x", 1), send(layer_input, "x", 3))
    rows = rows + (send(rows[1][:, :CH], "x", 1), send(rows[2][:, CH:], "x", 3))
    line = line_up((shard,) + near, (rows[1], rows[2], prm, heads, prs))
    under, over = send(line, "second", 1), send(line, "second", 3)
    one, two = send(under[:192], "second", 1), send(over[192:], "second", 3)
    feat, feat_t = normalize(rows, input_gain[None])
    mine = (line, under, over, touch(one, (feat,)), two)
    weights = mine + tuple(send(a, "c", 1) for a in mine)
    w_in, w_o, pre = project(feat, weights)
    below, above = send(out_cotangent, "x", 1), send(out_cotangent, "x", 3)
    cot_rows = (out_cotangent, below, above, send(below[:, :CH], "x", 1), send(above[:, CH:], "x", 3))

    act, hs0, msg = forward(0, pre, None, None, None, prm, prs, heads)
    msg = send(msg, "zl", 1)
    act, hs1 = forward(1, pre, act, hs0, None, prm, prs, heads)
    act, hs2 = forward(2, pre, act, hs1, msg, prm, prs, heads)
    cot, gm, gb, sums = cotangent(cot_rows, w_o, pre, act, prm)
    all_sums = (sums,) + spread(sums, "x")
    parts = out_partial(gb, w_o)
    out_terms, (out_up,) = ring(parts, "x", row_middle)
    dssd, lowz, mixed, ggain = gate_back(all_sums, gm, act, pre, prm, (parts[0],))

    own, far, gains = early_grads(feat_t, cot, lowz, mixed, w_in)
    far = send(far, "c", 1)
    scan = (prm, prs, heads)
    low, *carried, back = backward(2, pre, msg, act, hs2, dssd, lowz, *scan, None, None, None, (own,))
    back = send(back, "zl", 1)
    parts = core_sum(own, far, (), (low,), "early_core_sum")
    early_terms, (early_up,) = ring(parts, "second", functools.partial(tile_middle, False))
    low, *carried = backward(1, pre, None, act, hs1, dssd, lowz, *scan, carried, None, low, (parts[0], out_up))
    deps = (early_up,)
    low, _, _, acc, accs = backward(0, pre, None, act, hs0, dssd, lowz, *scan, carried, back, low, deps)

    own, far, small = late_grads(feat_t, low, w_in, gains, acc, accs, ggain, out_terms[1:] + early_terms[1:])
    far = send(far, "c", 1)
    feat_parts = feat_partial(low, w_in, (own,))
    parts = core_sum(own, far, (small,), (feat_parts[0],), "late_core_sum")
    late_terms, (late_up, near) = ring(parts, "second", functools.partial(tile_middle, True))
    feat_terms, (feat_up,) = ring(feat_parts, "x", row_middle, (late_up,))
    parts = tile_sums(
        axis_sum_kernel,
        early_terms + late_terms + (near,),
        [shape(224, CH, dtype=bf16)] * 4,
        (),
        "axis_sum",
    )
    early, late, small, to_x = tile_sums(
        last_sum_kernel,
        deal(parts, "first"),
        [shape(96, CH), shape(96, CH), shape(16, CH), shape(48, CH, dtype=bf16)],
        (),
        "last_sum",
    )
    g_state, g_input_gain, g_conv_state, g_conv_state_bias = tile_sums(
        x_sum_kernel,
        (to_x,) + spread(to_x, "x") + (input_gain[None],),
        [shape(96, 2 * N), shape(1, D), shape(4, 2 * N), shape(1, 2 * N)],
        feat_terms[1:],
        "x_sum",
    )

    own = lambda a: jnp.where(zl == 0, a[..., :HALF], a[..., HALF:])
    six = lambda a: jnp.where(zl == 0, a[:6], a[6:12])
    conv = own(small[:7])
    g_skip = six(small[5].reshape(12, 64).sum(axis=1))
    g_decay, g_bias = six(small[7, :128]), six(small[7, 256:384])
    g_step = jnp.where(zl == 0, late[:, 512:518], late[:, 518:524])

    values = layer_input.astype(f32)
    squares = all_sums[0][0] + all_sums[1][0] + all_sums[2][0] + all_sums[3][0]
    at = lax.rem(192 * lax.axis_index("x") + 256 + 256 * zl, ROWS)
    squares = lax.dynamic_slice_in_dim(jnp.concatenate([squares, squares]), at, 192)
    scale = lax.rsqrt(squares / DI + EPS)[:, None]
    layer_output = (values + add3(out_terms) * scale).astype(bf16)
    inv = lax.rsqrt(jnp.mean(values * values, axis=1, keepdims=True) + EPS)
    weighted = add3(feat_terms) * input_gain
    input_grad = (
        out_cotangent.astype(f32)
        + weighted * inv
        - values * (inv * inv * inv) * jnp.mean(weighted * values, axis=1, keepdims=True)
    )
    return (
        layer_output,
        input_grad,
        g_input_gain[0],
        jnp.stack([early[:, :HALF], late[:, :HALF]], axis=1),
        g_step,
        g_state,
        early[:, HALF:].T,
        conv[:4],
        conv[4],
        g_conv_state,
        g_conv_state_bias[0],
        conv[6],
        g_decay,
        g_bias,
        g_skip,
    )


def solution(mesh):
    split = Mesh(mesh.devices.reshape(SIZES), AX)
    everything = FSDP + TP
    return jax.shard_map(
        local,
        mesh=split,
        in_specs=(
            P(everything, None),
            P(),
            P(FSDP, None, TP),
            P(FSDP, TP),
            P(FSDP, None),
            P(TP, FSDP),
            P(None, TP),
            P(TP),
            P(),
            P(),
            P(TP),
            P(TP),
            P(TP),
            P(TP),
            P(everything, None),
        ),
        out_specs=(
            P(everything, None),
            P(everything, None),
            P(),
            P(FSDP, None, TP),
            P(FSDP, TP),
            P(FSDP, None),
            P(TP, FSDP),
            P(None, TP),
            P(TP),
            P(),
            P(),
            P(TP),
            P(TP),
            P(TP),
            P(TP),
        ),
        check_vma=False,
    )
```

```python
import functools
import itertools

import jax
import jax.numpy as jnp
import numpy as np
from jax import lax
from jax.experimental import pallas as pl
from jax.experimental.pallas import tpu as pltpu
from jax.sharding import Mesh
from jax.sharding import PartitionSpec as P

D = 1536
DI = 3072
N = 128
Q = 128
STEP = 256
ROWS = 768
CH = 768
HALF = 384
PAIRS = 6
LEFT = 1024
FULL = LEFT + HALF
EPS = 1e-05
NEG = -1e30

AX = ("zh", "y", "c", "zl", "x")
SIZES = (2, 4, 2, 2, 4)
FSDP = ("zh", "y", "c")
TP = ("zl", "x")

bf16 = jnp.bfloat16
f32 = jnp.float32


def moved(d, axis, k):
    d = dict(d)
    if axis == "z":
        z = (2 * d["zh"] + d["zl"] + k) % 4
        d["zh"], d["zl"] = divmod(z, 2)
    elif axis == "first":
        return moved(d, "y" if d["c"] == 0 else "z", k)
    elif axis == "second":
        return moved(d, "z" if d["c"] == 0 else "y", k)
    else:
        d[axis] = (d[axis] + k) % SIZES[AX.index(axis)]
    return d


def send(a, axis, k):
    pairs = []
    for place in itertools.product(*map(range, SIZES)):
        to = moved(dict(zip(AX, place)), axis, k)
        pairs.append(
            (
                int(np.ravel_multi_index(place, SIZES)),
                int(np.ravel_multi_index([to[n] for n in AX], SIZES)),
            )
        )
    return lax.ppermute(a, AX, pairs)


def spread(a, axis):
    return tuple(send(a, axis, k) for k in (1, 2, 3))


def deal(parts, axis):
    return (parts[0],) + tuple(send(parts[k], axis, k) for k in (1, 2, 3))


def ring(parts, axis, middle, deps=()):
    own, up, down, one, two = parts
    one, two = send(one, axis, 1), send(two, axis, 3)
    up, down, *more = middle((up, down, one, two), deps)
    return (own, send(up, axis, 1), send(down, axis, 3)), (up, *more)


def add3(terms):
    a, b, c = (t.astype(f32) for t in terms)
    return a + (b + c)


def add4(terms):
    a, b, c, d = (t.astype(f32) for t in terms)
    return (a + b) + (c + d)


def dot(a, b):
    return lax.dot_general(a, b, (((1,), (0,)), ((), ())), preferred_element_type=f32)


def dot_nt(a, b):
    return lax.dot_general(a, b, (((1,), (1,)), ((), ())), preferred_element_type=f32)


def dot_tn(a, b):
    return lax.dot_general(a, b, (((0,), (0,)), ((), ())), preferred_element_type=f32)


def halves(a):
    hi = a.astype(bf16)
    return hi, (a - hi.astype(f32)).astype(bf16)


def thirds(a):
    hi = a.astype(bf16)
    rest = a - hi.astype(f32)
    mid = rest.astype(bf16)
    return hi, mid, (rest - mid.astype(f32)).astype(bf16)


def tri_dot(tri, a):
    return dot(jnp.concatenate([tri] * 3, axis=1), jnp.concatenate(thirds(a), axis=0))


def lanes_of(a, i):
    return jnp.broadcast_to(a[:, i : i + 1], (Q, 128))


def iota(shape, dim):
    return lax.broadcasted_iota(jnp.int32, shape, dim)


def softplus(v):
    return jnp.maximum(v, 0.0) + jnp.log1p(jnp.exp(-jnp.abs(v)))


def here():
    return {n: lax.axis_index(n) for n in AX}


def row_copies(pieces, dst, sems, by_step=False):
    me = here()
    places = ((0, 0, D), (1, 0, D), (2, 0, D), (3, 0, D))
    if len(pieces) == 5:
        places = ((0, 0, D), (1, 0, D), (3, 0, D), (2, 0, CH), (2, CH, CH))
    copies = []
    for ref, (k, col, width) in zip(pieces, places):
        x = lax.rem(me["x"] + 4 - k, 4)
        for g in range(3):
            at = lax.rem(3 * x + g + 4 + 4 * me["zl"], 12)
            to = dst.at[pl.ds(pl.multiple_of(64 * at, 64), 64), pl.ds(col, width)]
            copies.append((ref.at[pl.ds(64 * g, 64)], to, at // 4 if by_step else len(copies)))
    return [pltpu.make_async_copy(s, d, sems.at[i]) for s, d, i in copies]


N_ROW_COPIES = 15


def weight_copies(pieces, column, width, dst, sems):
    me = here()
    copies = []
    four = ((0, 0), (96, 3), (192, 2), (288, 1))
    hops = ((0, four), (3, four), (1, four), (2, four[:2]), (2, ((0, 2), (96, 1))))
    for k, ref in enumerate(pieces):
        core = lax.rem(me["c"] + k // 5, 2)
        rb, rows = hops[k % 5]
        for row, ra in rows:
            y = lax.rem(me["y"] + jnp.where(core == 0, ra, rb), 4)
            z = lax.rem(2 * me["zh"] + me["zl"] + jnp.where(core == 0, rb, ra), 4)
            f = (z // 2 * 4 + y) * 2 + core
            copies.append(
                (
                    ref.at[pl.ds(row, 96), pl.ds(column, width)],
                    dst.at[
                        pl.ds(pl.multiple_of(96 * f, 96), 96),
                        pl.ds(pl.multiple_of(width * lax.rem(z, 2), 128), width),
                    ],
                    lax.rem(z, 2),
                )
            )
    return [pltpu.make_async_copy(s, d, sems.at[g]) for s, d, g in copies]


def wait_half(g, width, dst, sems):
    half = dst.at[:, pl.ds(g * width, width)]
    pltpu.make_async_copy(half, half, sems.at[g]).wait()


def line_kernel(a, b, c, d, *rest):
    for k, ref in enumerate((a, b, c, d)):
        rest[-1][96 * k : 96 * k + 96, :] = ref[...]


def norm_kernel(*refs):
    rows, (gain, feat, feat_t, raw, sem) = refs[:5], refs[5:]
    copies = row_copies(rows, raw, sem)
    for c in copies:
        c.start()
    for c in copies:
        c.wait()
    for k in range(ROWS // 128):
        at = slice(128 * k, 128 * k + 128)
        v = raw[at, :].astype(f32)
        r = lax.rsqrt(jnp.mean(v * v, axis=1, keepdims=True) + EPS)
        normed = v * r * gain[...]
        feat[at, :] = normed.astype(bf16)
        for m in range(D // 128):
            col = slice(128 * m, 128 * m + 128)
            feat_t[col, at] = normed[:, col].T.astype(bf16)


def param_kernel(small, far, prm, heads):
    at_0 = lax.axis_index("zl") == 0
    lo = jnp.where(at_0, small[...], far[...])
    hi = jnp.where(at_0, far[...], small[...])
    prm[:, :HALF] = lo
    prm[:, HALF:] = hi
    lane = iota((1, 128), 1)

    def twelve(k):
        col = slice(128 * k, 128 * k + 128)
        return jnp.where(lane < 6, lo[6:7, col], pltpu.roll(hi[6:7, col], 6, 1))

    heads[...] = jnp.zeros_like(heads)
    heads[0:1, :] = jnp.where(lane < 12, jnp.exp(twelve(0)), 0.0)
    heads[1:2, :] = jnp.where(lane < 12, twelve(1), 0.0)
    skip = twelve(2)
    for i in range(PAIRS):
        pair = [jnp.broadcast_to(skip[:, 2 * i + k : 2 * i + k + 1], (1, 128)) for k in range(2)]
        prm[6:7, 128 * i : 128 * i + 128] = jnp.where(lane < 64, pair[0], pair[1])


def touch_kernel(*refs):
    pass


def proj_kernel(*refs):
    weights, (feat, w, wo, pre, wsem, wosem) = refs[:10], refs[10:]
    for c in weight_copies(weights, 0, LEFT, w, wsem):
        c.start()
    for c in weight_copies(weights, LEFT, HALF, wo, wosem):
        c.start()
    for i in range(4):
        if i % 2 == 0:
            wait_half(i // 2, LEFT, w, wsem)
        col = slice(512 * i, 512 * i + 512)
        pre[:, col] = dot(feat[...], w[:, col])
    for g in range(2):
        wait_half(g, HALF, wo, wosem)


def pair_places(i):
    g, p = divmod(i, 3)
    return slice(128 * i, 128 * i + 128), g * LEFT + HALF + 128 * p


def step_sizes(pre, heads):
    raw = pre[:, 896:1024] + pre[:, LEFT + 896 : LEFT + 1024] + heads[1:2, :]
    return raw, softplus(raw)


def framed_inputs(s, zl, pre, prev, msg, vx, vs):
    for g in range(2):
        base = g * LEFT + HALF
        vx[8:264, g * HALF : (g + 1) * HALF] = pre[:, base : base + HALF]
        vs[8:264, g * N : (g + 1) * N] = pre[:, base + HALF : base + HALF + N]
        if s == 0:
            vx[0:8, g * HALF : (g + 1) * HALF] = jnp.zeros((8, HALF), f32)
            vs[0:8, g * N : (g + 1) * N] = jnp.zeros((8, N), f32)
            continue
        hx, hs = prev[:, base : base + HALF], prev[:, base + HALF : base + HALF + N]
        if s == 1:
            hx, hs = jnp.where(zl == 1, hx, 0.0), jnp.where(zl == 1, hs, 0.0)
        else:
            mx = msg[128:144, g * HALF : (g + 1) * HALF].astype(f32)[:8]
            ms = msg[144:160, g * N : (g + 1) * N].astype(f32)[:8]
            hx, hs = jnp.where(zl == 0, hx, mx), jnp.where(zl == 0, hs, ms)
        vx[0:8, g * HALF : (g + 1) * HALF] = hx
        vs[0:8, g * N : (g + 1) * N] = hs


def fwd_kernel(s, *refs):
    refs = list(refs)
    pre = refs.pop(0)
    rows_here = pl.ds(STEP * s, STEP)
    prev = pre.at[pl.ds(STEP * s - 8, 8)] if s else None
    pre = pre.at[rows_here]
    h_in = refs.pop(0) if s else None
    msg = refs.pop(0) if s == 2 else None
    prm, prs, heads = refs[:3]
    refs = refs[3:]
    refs = refs[len(refs) - (5 if s == 0 else 4) :]
    act, hs = refs[:2]
    act = act.at[rows_here]
    refs = refs[2:]
    out_msg = refs.pop(0) if s == 0 else None
    vx, vs = refs
    zl = lax.axis_index("zl")
    framed_inputs(s, zl, pre, prev, msg, vx, vs)
    if s == 0:
        hs[0] = jnp.zeros((N, CH), f32)
    elif s == 1:
        hs[0] = jnp.where(zl == 1, h_in[2], 0.0)
    else:
        hs[0] = jnp.where(zl == 0, h_in[2], msg[0:128, :].astype(f32))
    _, dt_all = step_sizes(pre, heads)
    a_all = -heads[0:1, :] * dt_all
    sub, lane = iota((Q, 128), 0), iota((Q, 128), 1)
    low_mask = sub >= lane
    tri = jnp.where(low_mask, 1.0, 0.0).astype(bf16)
    left = lane < 64
    for j in range(2):
        r0 = Q * j
        bc = []
        for g in range(2):
            col = slice(g * N, (g + 1) * N)
            cs = prs[4:5, col] + sum(
                prs[k : k + 1, col] * vs[5 + k + r0 : 5 + k + r0 + Q, col] for k in range(4)
            )
            act[r0 : r0 + Q, 2 * CH + g * N : 2 * CH + (g + 1) * N] = cs
            bc.append((cs * jax.nn.sigmoid(cs)).astype(bf16))
        b, c = bc
        bt = b.astype(f32).T.astype(bf16)
        scores = dot_nt(c, b)
        dt = dt_all[r0 : r0 + Q]
        cum = tri_dot(tri, a_all[r0 : r0 + Q])
        cum_t = cum.T
        for i in range(PAIRS):
            col, _ = pair_places(i)
            cx = prm[4:5, col] + sum(
                prm[k : k + 1, col] * vx[5 + k + r0 : 5 + k + r0 + Q, col] for k in range(4)
            )
            act[r0 : r0 + Q, CH + 128 * i : CH + 128 * i + 128] = cx
            x = (cx * jax.nn.sigmoid(cx)).astype(bf16).astype(f32)
            c0, c1 = lanes_of(cum, 2 * i), lanes_of(cum, 2 * i + 1)
            m0 = scores * jnp.exp(jnp.where(low_mask, c0 - cum_t[2 * i : 2 * i + 1, :], NEG))
            m1 = scores * jnp.exp(jnp.where(low_mask, c1 - cum_t[2 * i + 1 : 2 * i + 2, :], NEG))
            cp = jnp.where(left, c0, c1)
            xdt = x * jnp.where(left, lanes_of(dt, 2 * i), lanes_of(dt, 2 * i + 1))
            xdtb = xdt.astype(bf16)
            zero = jnp.zeros_like(xdtb)
            last = cp[Q - 1 : Q, :]
            inside = dot(
                jnp.concatenate([m0.astype(bf16), m1.astype(bf16)], axis=1),
                jnp.concatenate([jnp.where(left, xdtb, zero), jnp.where(left, zero, xdtb)], axis=0),
            )
            h = hs[j, :, col]
            y = inside + jnp.exp(cp) * dot(c, h.astype(bf16)) + prm[6:7, col] * x
            act[r0 : r0 + Q, col] = y
            hs[j + 1, :, col] = h * jnp.exp(last) + dot(bt, (xdt * jnp.exp(last - cp)).astype(bf16))
    if s == 0:
        out_msg[0:128, :] = hs[2].astype(bf16)
        out_msg[128:144, :] = jnp.concatenate([vx[256:264, :]] * 2, axis=0).astype(bf16)
        out_msg[144:160, :] = jnp.concatenate(
            [jnp.concatenate([vs[256:264, :]] * 2, axis=0), jnp.zeros((16, CH - 2 * N), f32)], axis=1
        ).astype(bf16)


def cot_kernel(*refs):
    rows, (w, pre, act, prm, cot, gm, gb, sums, rsem) = refs[:5], refs[5:]
    for c in row_copies(rows, cot, rsem, True):
        c.start()
    lane = iota((STEP, 128), 1)
    for i in range(3):
        at = slice(STEP * i, STEP * i + STEP)
        step = cot.at[pl.ds(STEP * i, STEP)]
        pltpu.make_async_copy(step, step, rsem.at[i]).wait()
        grad = dot(cot[at, :], w[...])
        gm[at, :] = grad
        squares = jnp.zeros((STEP, 128), f32)
        dots = jnp.zeros((STEP, 128), f32)
        for c in range(PAIRS):
            col = slice(128 * c, 128 * c + 128)
            first = c // 3 * LEFT + c % 3 * 128
            gate = pre[at, first : first + 128]
            gated = act[at, col] * (gate * jax.nn.sigmoid(gate))
            scaled = gated * prm[5:6, col]
            gb[at, col] = scaled.astype(bf16)
            squares = squares + gated * gated
            dots = dots + grad[:, col] * scaled
        squares = jnp.sum(squares, axis=1, keepdims=True)
        dots = jnp.sum(dots, axis=1, keepdims=True)
        both = jnp.where(lane == 0, squares, jnp.where(lane == 1, dots, 0.0))
        sums[:, at] = both.T[0:8, :]


def store_rows(i, value, outs):
    own, up, down, one, two = outs
    me = here()
    for g in range(4):
        natural = lax.rem(4 * i + g + 8 - 4 * me["zl"] + 12, 12)
        rel = lax.rem(natural // 3 - me["x"] + 4, 4)
        at = pl.ds(pl.multiple_of(64 * lax.rem(natural, 3), 64), 64)
        rows = slice(64 * g, 64 * g + 64)
        for k, out in ((0, own), (1, up), (3, down)):

            @pl.when(rel == k)
            def _(out=out, rows=rows, at=at):
                out[at, :] = value[rows, :]

        @pl.when(rel == 2)
        def _(rows=rows, at=at):
            one[at, :] = value[rows, :CH]
            two[at, :] = value[rows, CH:]


def add(a, b):
    return (a.astype(f32) + b.astype(f32)).astype(bf16)


def row_middle_kernel(up, down, one, two, *refs):
    up_out, down_out = refs[-2:]
    up_out[:, :CH] = add(up[:, :CH], one[...])
    up_out[:, CH:] = up[:, CH:]
    down_out[:, :CH] = down[:, :CH]
    down_out[:, CH:] = add(down[:, CH:], two[...])


def out_kernel(gb, w, *outs):
    store_rows(pl.program_id(0), dot_nt(gb[...], w[...]).astype(bf16), outs)


def gate_kernel(s0, s1, s2, s3, gm, act, pre, prm, *refs):
    dssd, lowz, mixed, ggain, cols = refs[-5:]
    cols[...] = (s0[...] + s1[...] + s2[...] + s3[...]).T
    ggain[...] = jnp.zeros_like(ggain)

    def block(k, carry):
        at = pl.ds(pl.multiple_of(64 * k, 64), 64)
        total = cols[at, :]
        inv = lax.rsqrt(total[:, 0:1] / DI + EPS)
        pull = inv * inv * inv * (total[:, 1:2] / DI)
        for c in range(PAIRS):
            col = slice(128 * c, 128 * c + 128)
            first = c // 3 * LEFT + c % 3 * 128
            gate = pre[at, first : first + 128]
            sig = jax.nn.sigmoid(gate)
            silu = gate * sig
            y = act[at, col]
            gated = y * silu
            grad = gm[at, col]
            gain = prm[5:6, col]
            normal = gated * inv
            mixed[at, col] = (normal * gain).astype(bf16)
            dg = grad * gain * inv - gated * pull
            dssd[at, col] = (dg * silu).astype(bf16)
            lowz[at, col] = (dg * y * (sig * (1.0 + gate * (1.0 - sig)))).astype(bf16)
            ggain[0:1, col] += jnp.sum(grad * normal, axis=0, keepdims=True)
        return carry

    lax.fori_loop(0, ROWS // 64, block, 0)


def send_tiles(buf, own, far, sem):
    me = here()
    m = pl.program_id(0)
    z0 = 2 * me["zh"] + me["zl"]
    for core in range(2):

        @pl.when(me["c"] == core)
        def _(core=core):
            for k in range(4):
                dy = lax.rem(lax.rem(2 * m + k // 2, 4) - me["y"] + 4, 4)
                for g in range(2):
                    dz = lax.rem(2 * (m // 2) + g - z0 + 4, 4)
                    at = 4 * dz + dy if k % 2 == 0 else 4 * dy + dz
                    pltpu.make_async_copy(
                        buf.at[pl.ds(pl.multiple_of(384 * m + 96 * k, 96), 96), pl.ds(g * CH, CH)],
                        (own if k % 2 == core else far).at[pl.ds(pl.multiple_of(96 * at, 96), 96)],
                        sem.at[m],
                    ).start()


def row_gain(part, w):
    lanes = sum(part[:, k : k + 128] * w[:, k : k + 128].astype(f32) for k in range(0, part.shape[1], 128))
    ones = jnp.ones((8, 128), bf16)
    hi, lo = halves(lanes)
    return dot_nt(ones, hi) + dot_nt(ones, lo)


def wait_tiles(own, sem):
    for m in range(4):
        block = own.at[pl.ds(0, ROWS)]
        pltpu.make_async_copy(block, block, sem.at[m]).wait()


def early_kernel(feat_t, cot, lowz, mixed, w, own, far, gains, buf, sem):
    m = pl.program_id(0)
    rows = pl.ds(pl.multiple_of(384 * m, 384), 384)
    part = dot(feat_t[...], lowz[...])
    out = dot_tn(cot[...], mixed[...]).astype(bf16)
    low = part.astype(bf16)
    for g in range(2):
        col = slice(g * HALF, (g + 1) * HALF)
        buf[rows, g * CH : g * CH + HALF] = low[:, col]
        buf[rows, g * CH + HALF : (g + 1) * CH] = out[:, col]
    send_tiles(buf, own, far, sem)
    gains[...] = row_gain(part, jnp.concatenate([w[:, :HALF], w[:, LEFT : LEFT + HALF]], axis=1))

    @pl.when(m == 3)
    def _():
        wait_tiles(own, sem)


def late_kernel(feat_t, low, w, gains_in, acc, accs, ggain, *refs):
    own, far, small, buf, gains, tail, sem, tail_sem = refs[-8:]
    m = pl.program_id(0)
    rows = pl.ds(pl.multiple_of(384 * m, 384), 384)
    both = w[:, LEFT - N : LEFT].astype(f32) + w[:, 2 * LEFT - N :].astype(f32)
    rhs = jnp.concatenate(
        [low[:, HALF:LEFT], low[:, LEFT + HALF : LEFT + CH], low[:, LEFT + CH : LEFT + CH + N]], axis=1
    )
    taps = jnp.concatenate(
        [w[:, HALF : CH + N], both.astype(bf16), w[:, LEFT + HALF : LEFT + CH], w[:, LEFT + CH : LEFT + CH + N]],
        axis=1,
    )
    part = dot(feat_t[...], rhs)
    low_part = part.astype(bf16)
    shared = jnp.concatenate([low_part[:, HALF : HALF + 2 * N], low_part[:, 1024:1152]], axis=1)
    buf[rows, 0:HALF] = low_part[:, 0:HALF]
    buf[rows, CH : CH + HALF] = low_part[:, 640:1024]
    for g in range(2):
        buf[rows, g * CH + HALF : (g + 1) * CH] = shared
    send_tiles(buf, own, far, sem)
    gain = gains_in[...] + row_gain(part, taps)
    gains[m] = gain

    @pl.when(m == 3)
    def _():
        small[...] = jnp.zeros_like(small)
        small[0:6, :] = acc[0:6, :]
        small[6:7, :] = ggain[0:1, :]
        small[8:9, :] = jnp.concatenate([gains[0, 0:1, :], gains[1, 0:1, :]], axis=1)
        small[9:10, :] = jnp.concatenate([gains[2, 0:1, :], gains[3, 0:1, :]], axis=1)
        for row, rs in ((7, (5, 6)), (10, (0, 1, 2)), (11, (3, 4))):
            for k, r in enumerate(rs):
                small[row : row + 1, 256 * k : 256 * k + 256] = accs[r : r + 1, :]
        tail[...] = split_small(small[...])
        copy = pltpu.make_async_copy(tail, far.at[pl.ds(2 * ROWS, 32)], tail_sem.at[0])
        copy.start()
        wait_tiles(own, sem)
        copy.wait()


def split_small(total):
    return jnp.concatenate(halves(total), axis=0)


def sum_small(block):
    return block[:16].astype(f32) + block[16:].astype(f32)


def core_sum_kernel(with_small, *refs):
    own, far = refs[:2]
    outs = refs[-5:]
    if with_small:
        small = split_small(refs[2][...] + sum_small(far[2 * ROWS : 2 * ROWS + 32, :]))
    for out, first, count in zip(outs, (0, 384, 1152, 768, 960), (384, 384, 384, 192, 192)):
        rows = slice(first, first + count)
        out[0:count, :] = add(own[rows, :], far[rows, :])
        if with_small:
            out[count : count + 32, :] = small


def tile_middle_kernel(with_small, up, down, one, two, *refs):
    outs = refs[-3:] if with_small else refs[-2:]
    up_out, down_out = outs[:2]
    up_out[0:192, :] = add(up[0:192, :], one[0:192, :])
    up_out[192:384, :] = up[192:384, :]
    down_out[0:192, :] = down[0:192, :]
    down_out[192:384, :] = add(down[192:384, :], two[0:192, :])
    if with_small:
        up_out[384:416, :] = one[192:224, :]
        down_out[384:416, :] = down[384:416, :]
        outs[2][...] = split_small(sum_small(one[192:224, :]) + sum_small(two[192:224, :]))


def axis_sum_kernel(*refs):
    early, late, near, outs = refs[:3], refs[3:6], refs[6], refs[-4:]
    own, up = late[:2]
    small = split_small(sum_small(own[384:416, :]) + sum_small(up[384:416, :]) + sum_small(near[...]))
    for k, out in enumerate(outs):
        rows = slice(96 * k, 96 * k + 96)
        out[0:96, :] = add3([t[rows, :] for t in early]).astype(bf16)
        out[96:192, :] = add3([t[rows, :] for t in late]).astype(bf16)
        out[192:224, :] = small


def last_sum_kernel(*refs):
    terms, (early, tile, small, to_x) = refs[:4], refs[-4:]
    early[...] = add4([t[0:96, :] for t in terms])
    total = add4([t[96:192, :] for t in terms])
    tile[...] = total
    every = sum(sum_small(t[192:224, :]) for t in terms)
    small[...] = every
    for k in range(3):
        rows = slice(32 * k, 32 * k + 32)
        to_x[0:32, 256 * k : 256 * k + 128] = total[rows, HALF : HALF + N].astype(bf16)
        to_x[0:32, 256 * k + 128 : 256 * k + 256] = total[rows, HALF + 2 * N : HALF + 3 * N].astype(bf16)
    hi, lo = halves(every[8:16, :])
    to_x[32:48, :] = jnp.concatenate([hi.astype(f32), lo.astype(f32)], axis=0).astype(bf16)


def x_sum_kernel(a, b, c, d, gain, *refs):
    state, g_gain, g_conv, g_bias = refs[-4:]
    total = add4([a[...], b[...], c[...], d[...]])
    for k in range(3):
        state[32 * k : 32 * k + 32, :] = total[0:32, 256 * k : 256 * k + 256]
    small = total[32:40, :] + total[40:48, :]
    g_gain[:, :CH] = small[0:1, :] / gain[:, :CH]
    g_gain[:, CH:] = small[1:2, :] / gain[:, CH:]
    for k in range(3):
        g_conv[k : k + 1, :] = small[2:3, 256 * k : 256 * k + 256]
    g_conv[3:4, :] = small[3:4, 0:256]
    g_bias[...] = small[3:4, 256:512]


def bwd_kernel(s, *refs):
    refs = list(refs)
    pre = refs.pop(0)
    rows_here = pl.ds(STEP * s, STEP)
    prev = pre.at[pl.ds(STEP * s - 8, 8)] if s else None
    msg = refs.pop(0) if s == 2 else None
    act, hs, dssd, lowz, prm, prs, heads = refs[:7]
    pre, act, dssd, lowz = (ref.at[rows_here] for ref in (pre, act, dssd, lowz))
    refs = refs[7:]
    if s < 2:
        dh_in, tail, acc_in, accs_in = refs[:4]
        refs = refs[4:]
        back = refs.pop(0) if s == 0 else None
    refs = refs[len(refs) - (10 if s == 2 else 9) :]
    low, dh, head_rows, acc, accs = refs[:5]
    low = low.at[rows_here]
    refs = refs[5:]
    for g in range(2):
        low[:, g * LEFT : g * LEFT + HALF] = lowz[:, g * HALF : (g + 1) * HALF]
    out_msg = refs.pop(0) if s == 2 else None
    vx, vs, dp, ds = refs
    zl = lax.axis_index("zl")
    framed_inputs(s, zl, pre, prev, msg, vx, vs)
    if s == 2:
        dh[...] = jnp.zeros_like(dh)
        dp[256:264, :] = jnp.zeros((8, CH), f32)
        ds[256:264, :] = jnp.zeros((8, 2 * N), f32)
        acc[...] = jnp.zeros_like(acc)
        accs[...] = jnp.zeros_like(accs)
    else:
        hd, hp, hq = dh_in[...], tail[0:8, :], tail[8:16, 0 : 2 * N]
        if s == 1:
            hd, hp, hq = (jnp.where(zl == 0, v, 0.0) for v in (hd, hp, hq))
        else:
            hd = jnp.where(zl == 1, hd, back[0:128, :].astype(f32))
            hp = jnp.where(zl == 1, hp, back[128:144, :].astype(f32)[:8])
            hq = jnp.where(zl == 1, hq, back[144:160, 0 : 2 * N].astype(f32)[:8])
        dh[...], dp[256:264, :], ds[256:264, :] = hd, hp, hq
        acc[...] = acc_in[...]
        accs[...] = accs_in[...]
    raw_all, dt_all = step_sizes(pre, heads)
    rate = heads[0:1, :]
    a_all = -rate * dt_all
    sub, lane = iota((Q, 128), 0), iota((Q, 128), 1)
    tri = jnp.where(sub >= lane, 1.0, 0.0).astype(bf16)
    up_mask = lane >= sub
    tri_up = jnp.where(up_mask, 1.0, 0.0).astype(bf16)
    below = jnp.where(lane < sub, 1.0, 0.0).astype(bf16)
    left = lane < 64
    for j in (1, 0):
        r0 = Q * j
        rows = slice(r0, r0 + Q)
        pre_s = [act[rows, 2 * CH + g * N : 2 * CH + (g + 1) * N] for g in range(2)]
        sig_s = [jax.nn.sigmoid(v) for v in pre_s]
        bf, cf = [(v * w).astype(bf16).astype(f32) for v, w in zip(pre_s, sig_s)]
        b, c = bf.astype(bf16), cf.astype(bf16)
        ct = cf.T.astype(bf16)
        scores_t = dot_nt(c, b).T
        dt, a = dt_all[rows], a_all[rows]
        cum = tri_dot(tri, a)
        cum_t = cum.T
        d_scores_t = jnp.zeros((Q, Q), f32)
        d_b = jnp.zeros((Q, N), f32)
        d_c = jnp.zeros((Q, N), f32)
        per_head = jnp.zeros((3 * Q, 128), f32)
        for i in range(PAIRS):
            col, _ = pair_places(i)
            cx = act[rows, CH + 128 * i : CH + 128 * i + 128]
            sig = jax.nn.sigmoid(cx)
            x = (cx * sig).astype(bf16).astype(f32)
            dyb = dssd[rows, col]
            dy = dyb.astype(f32)
            skip = prm[6:7, col]
            c0, c1 = lanes_of(cum, 2 * i), lanes_of(cum, 2 * i + 1)
            l0 = jnp.exp(jnp.where(up_mask, cum_t[2 * i : 2 * i + 1, :] - c0, NEG))
            l1 = jnp.exp(jnp.where(up_mask, cum_t[2 * i + 1 : 2 * i + 2, :] - c1, NEG))
            cp = jnp.where(left, c0, c1)
            dtp = jnp.where(left, lanes_of(dt, 2 * i), lanes_of(dt, 2 * i + 1))
            last = cp[Q - 1 : Q, :]
            fade = jnp.exp(last - cp)
            xdt = x * dtp
            xdtb = xdt.astype(bf16)
            zero = jnp.zeros_like(xdtb)
            dy_split = jnp.concatenate([jnp.where(left, dyb, zero), jnp.where(left, zero, dyb)], axis=0)
            x_split = jnp.concatenate([jnp.where(left, xdtb, zero), jnp.where(left, zero, xdtb)], axis=0)
            dhp = dh[:, col]
            dhb = dhp.astype(bf16)
            m_t = jnp.concatenate([(scores_t * l0).astype(bf16), (scores_t * l1).astype(bf16)], axis=1)
            inside = dot(m_t, dy_split)
            beyond = fade * dot(b, dhb)
            dxdt = inside + beyond
            dx = dxdt * dtp + skip * dy
            acc[5:6, col] += jnp.sum(dy * x, axis=0, keepdims=True)
            d_m_t = dot_nt(x_split, dyb)
            d_scores_t = d_scores_t + d_m_t[:Q] * l0 + d_m_t[Q:] * l1
            h = hs[j, :, col]
            crossing = jnp.sum(dhp * h, axis=0, keepdims=True) * jnp.exp(last)
            t1 = dxdt * x
            t2 = dy * (act[rows, col] - skip * x) - xdtb.astype(f32) * inside
            t2 = t2 + jnp.where(sub == Q - 1, crossing, 0.0)
            t3 = xdt * beyond
            pick = (lane == jnp.where(sub < 64, 2 * i, 2 * i + 1)).astype(f32).astype(bf16)
            hi, lo = halves(jnp.concatenate([t1, t2, t3], axis=0))
            per_head = per_head + dot(
                jnp.concatenate([hi, lo], axis=1), jnp.concatenate([pick, pick], axis=0)
            )
            dye = (dy * jnp.exp(cp)).astype(bf16)
            d_c = d_c + dot_nt(dye, h.astype(bf16))
            d_b = d_b + dot_nt((xdt * fade).astype(bf16), dhb)
            dh[:, col] = dhp * jnp.exp(last) + dot(ct, dye)
            dp[rows, col] = dx * (sig * (1.0 + cx * (1.0 - sig)))
        d_b = d_b + dot(d_scores_t.astype(bf16), c)
        d_c = d_c + dot(d_scores_t.T.astype(bf16), b)
        for g, grad in ((0, d_b), (1, d_c)):
            ds[rows, g * N : (g + 1) * N] = grad * (sig_s[g] * (1.0 + pre_s[g] * (1.0 - sig_s[g])))
        da = tri_dot(tri_up, per_head[Q : 2 * Q]) + tri_dot(below, per_head[2 * Q :])
        ddt = per_head[:Q] - rate * da
        dstep = ddt * jax.nn.sigmoid(raw_all[rows])
        accs[5:6, 0:128] += jnp.sum(a * da, axis=0, keepdims=True)
        accs[6:7, 0:128] += jnp.sum(dstep, axis=0, keepdims=True)
        for g in range(2):
            low[rows, (g + 1) * LEFT - N : (g + 1) * LEFT] = dstep.astype(bf16)
    for frame, grads, taps, out, width in ((vx, dp, prm, acc, CH), (vs, ds, prs, accs, 2 * N)):
        for i in range(width // 128):
            col = slice(128 * i, 128 * i + 128)
            g, p = divmod(i, width // 256)
            to = g * LEFT + HALF + 128 * p + (HALF if width == 2 * N else 0)
            back_v = sum(taps[k : k + 1, col] * grads[3 - k : 3 - k + STEP, col] for k in range(4))
            low[:, to : to + 128] = back_v.astype(bf16)
            own = grads[0:STEP, col]
            for k in range(4):
                out[k : k + 1, col] += jnp.sum(own * frame[5 + k : 5 + k + STEP, col], axis=0, keepdims=True)
            out[4:5, col] += jnp.sum(own, axis=0, keepdims=True)
    head_rows[0:8, :] = dp[0:8, :]
    head_rows[8:16, :] = jnp.concatenate([ds[0:8, :], jnp.zeros((8, CH - 2 * N), f32)], axis=1)
    if s == 2:
        out_msg[0:128, :] = dh[...].astype(bf16)
        out_msg[128:144, :] = jnp.concatenate([head_rows[0:8, :]] * 2, axis=0).astype(bf16)
        out_msg[144:160, :] = jnp.concatenate([head_rows[8:16, :]] * 2, axis=0).astype(bf16)


def feat_kernel(low, w, *refs):
    store_rows(pl.program_id(0), dot_nt(low[...], w[...]).astype(bf16), refs[-5:])


ANY = pl.BlockSpec(memory_space=pl.ANY)
VM = pl.BlockSpec(memory_space=pltpu.VMEM)


def params(mib):
    return pltpu.CompilerParams(vmem_limit_bytes=mib * 1024 * 1024)


def shape(*s, dtype=f32):
    return jax.ShapeDtypeStruct(s, dtype)


def cost(flops, moved_bytes):
    return pl.CostEstimate(flops=int(flops), bytes_accessed=int(moved_bytes), transcendentals=0)


def steps(width, column=0):
    return pl.BlockSpec((STEP, width), lambda i: (i, column))


def line_up(parts, deps):
    return pl.pallas_call(
        line_kernel,
        in_specs=[VM] * 4 + [ANY] * len(deps),
        out_specs=VM,
        out_shape=shape(384, FULL, dtype=bf16),
        compiler_params=params(4),
        cost_estimate=cost(1e6, 2e6),
        name="line_up",
    )(*parts, *deps)


def touch(a, deps):
    return pl.pallas_call(
        touch_kernel,
        in_specs=[ANY] * (1 + len(deps)),
        out_specs=ANY,
        out_shape=jax.ShapeDtypeStruct(a.shape, a.dtype),
        input_output_aliases={0: 0},
        compiler_params=params(1),
        cost_estimate=cost(1, 1),
        name="touch",
    )(a, *deps)


def normalize(rows, gain):
    return pl.pallas_call(
        norm_kernel,
        in_specs=[ANY] * 5 + [VM],
        out_specs=[VM, VM],
        out_shape=[shape(ROWS, D, dtype=bf16), shape(D, ROWS, dtype=bf16)],
        scratch_shapes=[pltpu.VMEM((ROWS, D), bf16), pltpu.SemaphoreType.DMA((N_ROW_COPIES,))],
        compiler_params=params(12),
        cost_estimate=cost(1e7, 5e6),
        name="normalize",
    )(*rows, gain)


def project(feat, weights):
    return pl.pallas_call(
        proj_kernel,
        in_specs=[ANY] * 10 + [VM],
        out_specs=[VM] * 3,
        out_shape=[shape(D, 2 * LEFT, dtype=bf16), shape(D, CH, dtype=bf16), shape(ROWS, 2 * LEFT)],
        scratch_shapes=[pltpu.SemaphoreType.DMA((2,)), pltpu.SemaphoreType.DMA((2,))],
        compiler_params=params(20),
        cost_estimate=cost(2 * ROWS * D * 2 * LEFT, 24e6),
        name="project",
    )(*weights, feat)


def forward(s, pre, act, h, msg, prm, prs, heads):
    ins = [pre] + ([h] if s else []) + ([msg] if s == 2 else []) + [prm, prs, heads]
    aliases = {}
    if s:
        aliases = {len(ins): 0}
        ins += [act]
    outs = [shape(ROWS, 2 * CH + 2 * N), shape(3, N, CH)]
    if s == 0:
        outs += [shape(160, CH, dtype=bf16)]
    return pl.pallas_call(
        functools.partial(fwd_kernel, s),
        in_specs=[VM] * len(ins),
        out_specs=[VM] * len(outs),
        out_shape=outs,
        input_output_aliases=aliases,
        scratch_shapes=[pltpu.VMEM((264, CH), f32), pltpu.VMEM((264, 2 * N), f32)],
        compiler_params=params(6),
        cost_estimate=cost(1.5e9, 6e6),
        name=f"scan_rows_{s}",
    )(*ins)


def cotangent(rows, w, pre, act, prm):
    return pl.pallas_call(
        cot_kernel,
        in_specs=[ANY] * 5 + [VM] * 4,
        out_specs=[VM] * 4,
        out_shape=[
            shape(ROWS, D, dtype=bf16),
            shape(ROWS, CH),
            shape(ROWS, CH, dtype=bf16),
            shape(8, ROWS),
        ],
        scratch_shapes=[pltpu.SemaphoreType.DMA((3,))],
        compiler_params=params(6),
        cost_estimate=cost(2 * ROWS * D * CH, 20e6),
        name="cotangent",
    )(*rows, w, pre, act, prm)


def out_partial(gb, w):
    return pl.pallas_call(
        out_kernel,
        grid=(3,),
        in_specs=[steps(CH), VM],
        out_specs=[VM] * 3 + [VM] * 2,
        out_shape=[shape(192, D, dtype=bf16)] * 3 + [shape(192, CH, dtype=bf16)] * 2,
        compiler_params=params(6),
        cost_estimate=cost(2 * ROWS * D * CH, 6e6),
        name="out_partial",
    )(gb, w)


def gate_back(sums, gm, act, pre, prm, deps):
    return pl.pallas_call(
        gate_kernel,
        in_specs=[VM] * 8 + [ANY] * len(deps),
        out_specs=[VM] * 4,
        out_shape=[shape(ROWS, CH, dtype=bf16)] * 3 + [shape(8, CH)],
        scratch_shapes=[pltpu.VMEM((ROWS, 8), f32)],
        compiler_params=params(4),
        cost_estimate=cost(1e7, 12e6),
        name="gate_back",
    )(*sums, gm, act, pre, prm, *deps)


def early_grads(feat_t, cot, lowz, mixed, w):
    return pl.pallas_call(
        early_kernel,
        grid=(4,),
        in_specs=[
            pl.BlockSpec((HALF, ROWS), lambda m: (m, 0)),
            pl.BlockSpec((ROWS, HALF), lambda m: (0, m)),
            VM,
            VM,
            pl.BlockSpec((HALF, 2 * LEFT), lambda m: (m, 0)),
        ],
        out_specs=[ANY, ANY, pl.BlockSpec((8, HALF), lambda m: (0, m))],
        out_shape=[shape(2 * ROWS, CH, dtype=bf16)] * 2 + [shape(8, D)],
        scratch_shapes=[pltpu.VMEM((D, 2 * CH), bf16), pltpu.SemaphoreType.DMA((4,))],
        compiler_params=params(14),
        cost_estimate=cost(2 * ROWS * D * 2 * CH, 12e6),
        name="early_grads",
    )(feat_t, cot, lowz, mixed, w)


def late_grads(feat_t, low, w, gains, acc, accs, ggain, deps):
    return pl.pallas_call(
        late_kernel,
        grid=(4,),
        in_specs=[
            pl.BlockSpec((HALF, ROWS), lambda m: (m, 0)),
            VM,
            pl.BlockSpec((HALF, 2 * LEFT), lambda m: (m, 0)),
            pl.BlockSpec((8, HALF), lambda m: (0, m)),
            VM,
            VM,
            VM,
        ]
        + [ANY] * len(deps),
        out_specs=[ANY, ANY, VM],
        out_shape=[shape(2 * ROWS, CH, dtype=bf16), shape(2 * ROWS + 32, CH, dtype=bf16), shape(16, CH)],
        scratch_shapes=[
            pltpu.VMEM((D, 2 * CH), bf16),
            pltpu.VMEM((4, 8, HALF), f32),
            pltpu.VMEM((32, CH), bf16),
            pltpu.SemaphoreType.DMA((4,)),
            pltpu.SemaphoreType.DMA((1,)),
        ],
        compiler_params=params(14),
        cost_estimate=cost(2 * ROWS * D * 3 * HALF, 12e6),
        name="late_grads",
    )(feat_t, low, w, gains, acc, accs, ggain, *deps)


def tile_sums(kernel, ins, outs, deps, name, mib=6):
    return pl.pallas_call(
        kernel,
        in_specs=[VM] * len(ins) + [ANY] * len(deps),
        out_specs=[VM] * len(outs),
        out_shape=outs,
        compiler_params=params(mib),
        cost_estimate=cost(1e6, 4e6),
        name=name,
    )(*ins, *deps)


def core_sum(own, far, small, deps, name):
    more = 32 if small else 0
    return tile_sums(
        functools.partial(core_sum_kernel, bool(small)),
        [own, far] + list(small),
        [shape(384 + more, CH, dtype=bf16)] * 3 + [shape(192 + more, CH, dtype=bf16)] * 2,
        deps,
        name,
        10,
    )


def row_middle(ins, deps):
    return tile_sums(row_middle_kernel, ins, [shape(192, D, dtype=bf16)] * 2, deps, "row_middle")


def tile_middle(with_small, ins, deps):
    outs = [shape(416 if with_small else 384, CH, dtype=bf16)] * 2
    if with_small:
        outs = outs + [shape(32, CH, dtype=bf16)]
    return tile_sums(functools.partial(tile_middle_kernel, with_small), ins, outs, deps, "tile_middle")


def backward(s, pre, msg, act, hs, dssd, lowz, prm, prs, heads, carried, back, low, deps):
    ins = [pre] + ([msg] if s == 2 else []) + [act, hs, dssd, lowz, prm, prs, heads]
    aliases = {}
    if s < 2:
        ins += list(carried)
        if s == 0:
            ins += [back]
        aliases = {len(ins): 0}
        ins += [low]
    outs = [shape(ROWS, 2 * LEFT, dtype=bf16), shape(N, CH), shape(16, CH), shape(8, CH), shape(8, 2 * N)]
    if s == 2:
        outs += [shape(160, CH, dtype=bf16)]
    return pl.pallas_call(
        functools.partial(bwd_kernel, s),
        in_specs=[VM] * len(ins) + [ANY] * len(deps),
        out_specs=[VM] * len(outs),
        out_shape=outs,
        input_output_aliases=aliases,
        scratch_shapes=[
            pltpu.VMEM((264, CH), f32),
            pltpu.VMEM((264, 2 * N), f32),
            pltpu.VMEM((264, CH), f32),
            pltpu.VMEM((264, 2 * N), f32),
        ],
        compiler_params=params(8),
        cost_estimate=cost(4e9, 8e6),
        name=f"scan_back_{s}",
    )(*ins, *deps)


def feat_partial(low, w, deps):
    return pl.pallas_call(
        feat_kernel,
        grid=(3,),
        in_specs=[steps(2 * LEFT), VM] + [ANY] * len(deps),
        out_specs=[VM] * 3 + [VM] * 2,
        out_shape=[shape(192, D, dtype=bf16)] * 3 + [shape(192, CH, dtype=bf16)] * 2,
        compiler_params=params(8),
        cost_estimate=cost(2 * ROWS * D * 2 * LEFT, 16e6),
        name="feat_partial",
    )(low, w, *deps)


def local(
    layer_input,
    input_gain,
    proj_inner,
    proj_step,
    proj_state,
    proj_output,
    conv_inner,
    conv_inner_bias,
    conv_state,
    conv_state_bias,
    inner_gain,
    decay_log,
    step_bias,
    skip_gain,
    out_cotangent,
):
    zl = lax.axis_index("zl")
    step_cols = jnp.where(
        zl == 0, jnp.pad(proj_step, ((0, 0), (0, 122))), jnp.pad(proj_step, ((0, 0), (6, 116)))
    )
    state_cols = jnp.where(zl == 0, proj_state[:, :N], proj_state[:, N:])
    shard = jnp.concatenate(
        [proj_inner[:, 0], proj_inner[:, 1], state_cols, step_cols, proj_output.T], axis=1
    )
    near = spread(shard, "first")

    coef = jnp.pad(jnp.stack([decay_log, step_bias, skip_gain]), ((0, 0), (0, 122))).reshape(1, HALF)
    small = jnp.concatenate(
        [touch(conv_inner, (near[0],)), conv_inner_bias[None], inner_gain[None], coef, jnp.zeros((1, HALF), f32)], axis=0
    )
    prm, heads = pl.pallas_call(
        param_kernel,
        in_specs=[VM, VM],
        out_specs=[VM, VM],
        out_shape=[shape(8, CH), shape(8, 128)],
        compiler_params=params(1),
        cost_estimate=cost(1, 1),
        name="parameters",
    )(small, send(small, "zl", 1))
    prs = jnp.concatenate([conv_state, conv_state_bias[None], jnp.zeros((3, 2 * N), f32)], axis=0)

    rows = (layer_input, send(layer_input, "x", 1), send(layer_input, "x", 3))
    rows = rows + (send(rows[1][:, :CH], "x", 1), send(rows[2][:, CH:], "x", 3))
    line = line_up((shard,) + near, (rows[1], rows[2], prm, heads, prs))
    under, over = send(line, "second", 1), send(line, "second", 3)
    one, two = send(under[:192], "second", 1), send(over[192:], "second", 3)
    feat, feat_t = normalize(rows, input_gain[None])
    mine = (line, under, over, touch(one, (feat,)), two)
    weights = mine + tuple(send(a, "c", 1) for a in mine)
    w_in, w_o, pre = project(feat, weights)
    below, above = send(out_cotangent, "x", 1), send(out_cotangent, "x", 3)
    cot_rows = (out_cotangent, below, above, send(below[:, :CH], "x", 1), send(above[:, CH:], "x", 3))

    act, hs0, msg = forward(0, pre, None, None, None, prm, prs, heads)
    msg = send(msg, "zl", 1)
    act, hs1 = forward(1, pre, act, hs0, None, prm, prs, heads)
    act, hs2 = forward(2, pre, act, hs1, msg, prm, prs, heads)
    cot, gm, gb, sums = cotangent(cot_rows, w_o, pre, act, prm)
    all_sums = (sums,) + spread(sums, "x")
    parts = out_partial(gb, w_o)
    out_terms, (out_up,) = ring(parts, "x", row_middle)
    dssd, lowz, mixed, ggain = gate_back(all_sums, gm, act, pre, prm, (parts[0],))

    own, far, gains = early_grads(feat_t, cot, lowz, mixed, w_in)
    far = send(far, "c", 1)
    scan = (prm, prs, heads)
    low, *carried, back = backward(2, pre, msg, act, hs2, dssd, lowz, *scan, None, None, None, (own,))
    back = send(back, "zl", 1)
    parts = core_sum(own, far, (), (low,), "early_core_sum")
    early_terms, (early_up,) = ring(parts, "second", functools.partial(tile_middle, False))
    low, *carried = backward(1, pre, None, act, hs1, dssd, lowz, *scan, carried, None, low, (parts[0], out_up))
    deps = (early_up,)
    low, _, _, acc, accs = backward(0, pre, None, act, hs0, dssd, lowz, *scan, carried, back, low, deps)

    own, far, small = late_grads(feat_t, low, w_in, gains, acc, accs, ggain, out_terms[1:] + early_terms[1:])
    far = send(far, "c", 1)
    feat_parts = feat_partial(low, w_in, (own,))
    parts = core_sum(own, far, (small,), (feat_parts[0],), "late_core_sum")
    late_terms, (late_up, near) = ring(parts, "second", functools.partial(tile_middle, True))
    feat_terms, (feat_up,) = ring(feat_parts, "x", row_middle, (late_up,))
    parts = tile_sums(
        axis_sum_kernel,
        early_terms + late_terms + (near,),
        [shape(224, CH, dtype=bf16)] * 4,
        (),
        "axis_sum",
    )
    early, late, small, to_x = tile_sums(
        last_sum_kernel,
        deal(parts, "first"),
        [shape(96, CH), shape(96, CH), shape(16, CH), shape(48, CH, dtype=bf16)],
        (),
        "last_sum",
    )
    g_state, g_input_gain, g_conv_state, g_conv_state_bias = tile_sums(
        x_sum_kernel,
        (to_x,) + spread(to_x, "x") + (input_gain[None],),
        [shape(96, 2 * N), shape(1, D), shape(4, 2 * N), shape(1, 2 * N)],
        feat_terms[1:],
        "x_sum",
    )

    own = lambda a: jnp.where(zl == 0, a[..., :HALF], a[..., HALF:])
    six = lambda a: jnp.where(zl == 0, a[:6], a[6:12])
    conv = own(small[:7])
    g_skip = six(small[5].reshape(12, 64).sum(axis=1))
    g_decay, g_bias = six(small[7, :128]), six(small[7, 256:384])
    g_step = jnp.where(zl == 0, late[:, 512:518], late[:, 518:524])

    values = layer_input.astype(f32)
    squares = all_sums[0][0] + all_sums[1][0] + all_sums[2][0] + all_sums[3][0]
    at = lax.rem(192 * lax.axis_index("x") + 256 + 256 * zl, ROWS)
    squares = lax.dynamic_slice_in_dim(jnp.concatenate([squares, squares]), at, 192)
    scale = lax.rsqrt(squares / DI + EPS)[:, None]
    layer_output = (values + add3(out_terms) * scale).astype(bf16)
    inv = lax.rsqrt(jnp.mean(values * values, axis=1, keepdims=True) + EPS)
    weighted = add3(feat_terms) * input_gain
    input_grad = (
        out_cotangent.astype(f32)
        + weighted * inv
        - values * (inv * inv * inv) * jnp.mean(weighted * values, axis=1, keepdims=True)
    )
    return (
        layer_output,
        input_grad,
        g_input_gain[0],
        jnp.stack([early[:, :HALF], late[:, :HALF]], axis=1),
        g_step,
        g_state,
        early[:, HALF:].T,
        conv[:4],
        conv[4],
        g_conv_state,
        g_conv_state_bias[0],
        conv[6],
        g_decay,
        g_bias,
        g_skip,
    )


def solution(mesh):
    split = Mesh(mesh.devices.reshape(SIZES), AX)
    everything = FSDP + TP
    return jax.shard_map(
        local,
        mesh=split,
        in_specs=(
            P(everything, None),
            P(),
            P(FSDP, None, TP),
            P(FSDP, TP),
            P(FSDP, None),
            P(TP, FSDP),
            P(None, TP),
            P(TP),
            P(),
            P(),
            P(TP),
            P(TP),
            P(TP),
            P(TP),
            P(everything, None),
        ),
        out_specs=(
            P(everything, None),
            P(everything, None),
            P(),
            P(FSDP, None, TP),
            P(FSDP, TP),
            P(FSDP, None),
            P(TP, FSDP),
            P(None, TP),
            P(TP),
            P(),
            P(),
            P(TP),
            P(TP),
            P(TP),
            P(TP),
        ),
        check_vma=False,
    )
```
